32 devices in a mesh: dp: 2 (over y), row: 4 (over z), col: 4 (over x, core).
Axes of the slice: x: 2, y: 2, z: 4, core: 2. Of those that a mesh axis runs over, the one named last changes fastest.
Arguments:
- inputs: bfloat16 [8192, 2048], P(('dp', 'col')), may hold values from -6 to 6
- prefix_len: int32 [8], P(('dp', 'col')), may hold values from 102 to 512
- norm1_gain: float32 [2048], replicated, may hold values from 0.25 to 1.75
- norm1_shift: float32 [2048], replicated, may hold values from -1.5 to 1.5
- w_qkv: float32 [3, 2048, 2048], P(None, ('dp', 'col'), 'row'), may hold values from -0.1875 to 0.1875
- b_qv: float32 [2, 2048], P(None, 'row'), may hold values from -2.5 to 2.5
- w_out: float32 [2048, 2048], P('row', ('dp', 'col')), may hold values from -0.5 to 0.5
- b_out: float32 [2048], replicated, may hold values from -2.5 to 2.5
- norm2_gain: float32 [2048], replicated, may hold values from 0.25 to 1.75
- norm2_shift: float32 [2048], replicated, may hold values from -1.5 to 1.5
- w_in: float32 [2048, 8192], P(('dp', 'col'), 'row'), may hold values from -0.125 to 0.125
- b_in: float32 [8192], P('row'), may hold values from -2.5 to 2.5
- w_down: float32 [8192, 2048], P('row', ('dp', 'col')), may hold values from -0.09375 to 0.09375
- b_down: float32 [2048], replicated, may hold values from -2.5 to 2.5
- d_output: bfloat16 [8192, 2048], P(('dp', 'col')), may hold values from -6 to 6
Outputs:
- output: bfloat16 [8192, 2048], P(('dp', 'col'))
- d_inputs: float32 [8192, 2048], P(('dp', 'col'))
- d_norm1_gain: float32 [2048], replicated
- d_norm1_shift: float32 [2048], replicated
- d_w_qkv: float32 [3, 2048, 2048], P(None, ('dp', 'col'), 'row')
- d_b_qv: float32 [2, 2048], P(None, 'row')
- d_w_out: float32 [2048, 2048], P('row', ('dp', 'col'))
- d_b_out: float32 [2048], replicated
- d_norm2_gain: float32 [2048], replicated
- d_norm2_shift: float32 [2048], replicated
- d_w_in: float32 [2048, 8192], P(('dp', 'col'), 'row')
- d_b_in: float32 [8192], P('row')
- d_w_down: float32 [8192, 2048], P('row', ('dp', 'col'))
- d_b_down: float32 [2048], replicated
The draws below stay inside these ranges and needn't reach their ends.
All inputs are finite; a program needn't handle non-finite values.
Results may differ from the reference program's by a relative error of at most 0.012.
The reference program's roundings to bfloat16 on the way count: a program that leaves them out, or rounds other values in their place, can miss the bound.
Values may be sent and summed in bfloat16 or wider, within the bound.
A program may use at most 256 MiB of HBM per device.

```python
import jax
import jax.numpy as jnp
from jax import lax

D = 2048
HEADS = 16
HEAD_DIM = 128
FF = 8192
LEN = 1024
SEQS = 8
TOKENS = 8192


def plant(array, rng, smallest, top_value):
    longest = array.shape.index(max(array.shape))
    spots = []
    for shift in (0, 1):
        where = [jax.random.randint(jax.random.fold_in(rng, axis), (), 0, length) for axis, length in enumerate(array.shape)]
        where[longest] = (where[longest] + shift) % array.shape[longest]
        spots.append(tuple(where))
    return array.at[spots[0]].set(smallest).at[spots[1]].set(top_value)


def block_levels(own_key, extent, cuts, smallest, top_value):
    factor_of, own = 1.0, jax.random.fold_in(own_key, 6)
    for dim, blocks in cuts:
        draws = jnp.exp(jax.random.uniform(jax.random.fold_in(own, dim), (blocks,), jnp.float32, smallest / len(cuts), top_value / len(cuts)))
        factor_of = factor_of * jnp.repeat(draws, extent[dim] // blocks).reshape([-1 if axis == dim else 1 for axis in range(len(extent))])
    return factor_of


def noise(own_key, shape, scale, bound, pieces=(), kind=jnp.bfloat16):
    result = scale * jax.random.normal(own_key, shape, jnp.float32)
    if pieces:
        result = result * block_levels(own_key, shape, pieces, -0.22, 0.18)
    return jnp.clip(result, -bound, bound).astype(kind)


def setup_inputs(seed: int = 0) -> dict:
    key_of = jax.random.split(jax.random.key(seed), 16)
    return {
        "inputs": noise(key_of[0], (TOKENS, D), 1.0, 6.0, ((0, 8),)),
        "prefix_len": plant(jax.random.randint(key_of[1], (SEQS,), LEN // 10, LEN // 2 + 1), jax.random.fold_in(key_of[1], 1), LEN // 10, (LEN // 2 + 1) - 1).astype(jnp.int32),
        "norm1_gain": jnp.clip(1.0 + 0.15 * jax.random.normal(key_of[2], (D,), jnp.float32), 0.25, 1.75),
        "norm1_shift": noise(key_of[3], (D,), 0.3, 1.5, (), jnp.float32),
        "w_qkv": noise(key_of[4], (3, D, D), (D // 2) ** -0.5, 0.1875, ((1, 8), (2, 4)), jnp.float32),
        "b_qv": noise(key_of[5], (2, D), 0.5, 2.5, ((1, 4),), jnp.float32),
        "w_out": noise(key_of[6], (D, D), (D // 16) ** -0.5, 0.5, ((0, 4), (1, 8)), jnp.float32),
        "b_out": noise(key_of[7], (D,), 0.5, 2.5, (), jnp.float32),
        "norm2_gain": jnp.clip(1.0 + 0.15 * jax.random.normal(key_of[8], (D,), jnp.float32), 0.25, 1.75),
        "norm2_shift": noise(key_of[9], (D,), 0.3, 1.5, (), jnp.float32),
        "w_in": noise(key_of[10], (D, FF), D ** -0.5, 0.125, ((0, 8), (1, 4)), jnp.float32),
        "b_in": noise(key_of[11], (FF,), 0.5, 2.5, ((0, 4),), jnp.float32),
        "w_down": noise(key_of[12], (FF, D), (FF // 2) ** -0.5, 0.09375, ((0, 4), (1, 8)), jnp.float32),
        "b_down": noise(key_of[13], (D,), 0.5, 2.5, (), jnp.float32),
        "d_output": noise(key_of[14], (TOKENS, D), 1.0, 6.0, ((0, 8),)),
    }


@jax.custom_vjp
def low(v):
    return lax.optimization_barrier(v.astype(jnp.bfloat16)).astype(jnp.float32)

@jax.custom_vjp
def low_back(v):
    return v

def low_keep(v):
    return (low(v), None)

def low_pass(kept, grad):
    return (grad,)

def back_keep(v):
    return (v, None)

def back_low(kept, grad):
    return (low(grad),)
low.defvjp(low_keep, low_pass)
low_back.defvjp(back_keep, back_low)
eps_norm = 1e-05
highest = lax.Precision.HIGHEST

def matmul(left, right):
    return jnp.dot(left, right, precision=highest, preferred_element_type=jnp.float32)

def layer_norm(values, norm_gain, norm_shift):
    average = lax.optimization_barrier(jnp.mean(values, axis=-1, keepdims=True))
    centered = values - average
    variance = lax.optimization_barrier(jnp.mean(centered * centered, axis=-1, keepdims=True))
    return centered * lax.rsqrt(variance + eps_norm) * norm_gain + norm_shift

def attention(queries, keys_low, values_low, prefix):
    length = queries.shape[0]
    head_q = queries.reshape(length, HEADS, HEAD_DIM)
    head_k = keys_low.reshape(length, HEADS, HEAD_DIM)
    head_v = values_low.reshape(length, HEADS, HEAD_DIM)
    raw_scores = jnp.einsum('qhd,khd->hqk', head_q, head_k, precision=highest) * HEAD_DIM ** (-0.5)
    scores = low_back(raw_scores)
    positions = jnp.arange(length, dtype=jnp.int32)
    allowed = (positions[None, :] <= positions[:, None]) | (positions[None, :] < prefix)
    scores = jnp.where(allowed[None], scores, -1000000000.0)
    row_max = lax.optimization_barrier(jnp.max(scores, axis=-1, keepdims=True))
    expo = jnp.exp(scores - row_max)
    probs = expo / lax.optimization_barrier(jnp.sum(expo, axis=-1, keepdims=True))
    context = jnp.einsum('hqk,khd->qhd', low(probs), head_v, precision=highest)
    return context.reshape(length, HEADS * HEAD_DIM)

def one_sequence(sequence, prefix, params):
    norm1_gain, norm1_shift, w_qkv, b_qv, w_out, b_out, norm2_gain, norm2_shift, w_in, b_in, w_down, b_down = params
    normed = low(layer_norm(sequence, norm1_gain, norm1_shift))
    queries = low(low_back(matmul(normed, w_qkv[0]) + b_qv[0]))
    keys_low = low(low_back(matmul(normed, w_qkv[1])))
    values_low = low(low_back(matmul(normed, w_qkv[2]) + b_qv[1]))
    context = low(low_back(attention(queries, keys_low, values_low, prefix)))
    branch = low_back(matmul(context, w_out) + b_out)
    hidden = sequence + branch
    normed_two = low(layer_norm(hidden, norm2_gain, norm2_shift))
    pre_act = low_back(matmul(normed_two, w_in) + b_in)
    activated = low(jax.nn.gelu(pre_act, approximate=False))
    return hidden + matmul(activated, w_down) + b_down

def forward(source, prefix_len, params):
    norm1_gain, norm1_shift, w_qkv, b_qv, w_out, b_out, norm2_gain, norm2_shift, w_in, b_in, w_down, b_down = params
    lowered = (norm1_gain, norm1_shift, low(w_qkv), b_qv, low(w_out), b_out, norm2_gain, norm2_shift, low(w_in), b_in, low(w_down), b_down)

    def per_sequence(totals, entries):
        sequence, prefix = entries
        return (totals, jax.checkpoint(one_sequence)(sequence, prefix, lowered))
    _, outputs = lax.scan(per_sequence, None, (source.reshape(SEQS, LEN, D), prefix_len))
    return outputs.reshape(TOKENS, D)

def reference(inputs, prefix_len, norm1_gain, norm1_shift, w_qkv, b_qv, w_out, b_out, norm2_gain, norm2_shift, w_in, b_in, w_down, b_down, d_output):
    params = (norm1_gain, norm1_shift, w_qkv, b_qv, w_out, b_out, norm2_gain, norm2_shift, w_in, b_in, w_down, b_down)
    source = inputs.astype(jnp.float32)
    output, pull = jax.vjp(lambda src, prm: forward(src, prefix_len, prm), source, params)
    d_source, grads = pull(d_output.astype(jnp.float32))
    return (output.astype(jnp.bfloat16), d_source, grads[0], grads[1], grads[2], grads[3], grads[4], grads[5], grads[6], grads[7], grads[8], grads[9], grads[10], grads[11])
```

```python
from functools import partial

import jax
import jax.numpy as jnp
from jax import lax
from jax.sharding import PartitionSpec as P

HEAD_DIM = 128


eps_norm = 1e-05


def norm_forward(values, norm_gain, norm_shift):
    average = jnp.mean(values, axis=-1, keepdims=True)
    centered = values - average
    variance = jnp.mean(centered * centered, axis=-1, keepdims=True)
    inverse = lax.rsqrt(variance + eps_norm)
    scaled = centered * inverse
    return (scaled * norm_gain + norm_shift, scaled, inverse)


def norm_backward(grad, scaled, inverse, norm_gain):
    grad_scaled = grad * norm_gain
    return inverse * (
        grad_scaled
        - jnp.mean(grad_scaled, axis=-1, keepdims=True)
        - scaled * jnp.mean(grad_scaled * scaled, axis=-1, keepdims=True)
    )


def block_scores(queries, keys_low, block_start, block_rows, prefix):
    length, width = keys_low.shape
    heads = width // HEAD_DIM
    score_scale = HEAD_DIM ** (-0.5)
    query_block = lax.dynamic_slice_in_dim(queries, block_start, block_rows, 0).reshape(
        block_rows, heads, HEAD_DIM
    )
    key_heads = keys_low.reshape(length, heads, HEAD_DIM)
    scores = (
        jnp.einsum("qhd,khd->hqk", query_block, key_heads, preferred_element_type=jnp.float32)
        * score_scale
    )
    rows_here = block_start + lax.iota(jnp.int32, block_rows)
    columns = lax.iota(jnp.int32, length)
    allowed = (columns[None, :] <= rows_here[:, None]) | (columns[None, :] < prefix)
    return (jnp.where(allowed[None], scores, -1000000000.0), query_block, key_heads)


def attend_forward(queries, keys_low, values_low, prefix, block_rows):
    length, width = queries.shape
    heads = width // HEAD_DIM
    value_heads = values_low.reshape(length, heads, HEAD_DIM)

    def one_block(block_index):
        block_start = block_index * block_rows
        scores, _, _ = block_scores(queries, keys_low, block_start, block_rows, prefix)
        row_max = jnp.max(scores, axis=-1)
        expo = jnp.exp(scores - row_max[..., None])
        row_total = jnp.sum(expo, axis=-1)
        probs_low = (expo / row_total[..., None]).astype(jnp.bfloat16)
        context = jnp.einsum(
            "hqk,khd->qhd", probs_low, value_heads, preferred_element_type=jnp.float32
        )
        return (context.reshape(block_rows, width), row_max, row_total)

    contexts, maxima, totals = lax.map(one_block, jnp.arange(length // block_rows, dtype=jnp.int32))
    return (contexts.reshape(length, width), maxima, totals)


def attend_backward(queries, keys_low, values_low, prefix, block_rows, maxima, totals, d_context):
    length, width = queries.shape
    heads = width // HEAD_DIM
    score_scale = HEAD_DIM ** (-0.5)
    value_heads = values_low.reshape(length, heads, HEAD_DIM)

    def one_block(sums, entries):
        block_index, row_max, row_total = entries
        block_start = block_index * block_rows
        scores, query_block, key_heads = block_scores(
            queries, keys_low, block_start, block_rows, prefix
        )
        probs = jnp.exp(scores - row_max[..., None]) / row_total[..., None]
        probs_low = probs.astype(jnp.bfloat16)
        grad_block = lax.dynamic_slice_in_dim(d_context, block_start, block_rows, 0).reshape(
            block_rows, heads, HEAD_DIM
        )
        d_probs = jnp.einsum(
            "qhd,khd->hqk", grad_block, value_heads, preferred_element_type=jnp.float32
        )
        inner = jnp.sum(d_probs * probs, axis=-1, keepdims=True)
        d_scores = (probs * (d_probs - inner)).astype(jnp.bfloat16)
        d_query = (
            jnp.einsum("hqk,khd->qhd", d_scores, key_heads, preferred_element_type=jnp.float32)
            * score_scale
        )
        d_keys = (
            sums[0]
            + jnp.einsum("hqk,qhd->khd", d_scores, query_block, preferred_element_type=jnp.float32)
            * score_scale
        )
        d_values = sums[1] + jnp.einsum(
            "hqk,qhd->khd", probs_low, grad_block, preferred_element_type=jnp.float32
        )
        return ((d_keys, d_values), d_query.reshape(block_rows, width).astype(jnp.bfloat16))

    zeros = jnp.zeros((length, heads, HEAD_DIM), jnp.float32)
    count = length // block_rows
    (d_keys, d_values), d_queries = lax.scan(
        one_block, (zeros, zeros), (jnp.arange(count, dtype=jnp.int32), maxima, totals)
    )
    return (
        d_queries.reshape(length, width),
        d_keys.reshape(length, width).astype(jnp.bfloat16),
        d_values.reshape(length, width).astype(jnp.bfloat16),
    )


def scatter_low(grad, dim):
    low = grad.astype(jnp.bfloat16)
    summed = lax.psum_scatter(low, ("dp", "col"), scatter_dimension=dim, tiled=True)
    return summed.astype(jnp.float32)


def local(
    inputs,
    prefix_len,
    norm1_gain,
    norm1_shift,
    w_qkv,
    b_qv,
    w_out,
    b_out,
    norm2_gain,
    norm2_shift,
    w_in,
    b_in,
    w_down,
    b_down,
    d_output,
):
    low_mats = (
        w_qkv.astype(jnp.bfloat16),
        w_out.astype(jnp.bfloat16),
        w_in.astype(jnp.bfloat16),
        w_down.astype(jnp.bfloat16),
    )
    full_qkv, full_out, full_in, full_down = (
        lax.all_gather(low_mats[0], ("dp", "col"), axis=1, tiled=True),
        lax.all_gather(low_mats[1], ("dp", "col"), axis=1, tiled=True),
        lax.all_gather(low_mats[2], ("dp", "col"), axis=0, tiled=True),
        lax.all_gather(low_mats[3], ("dp", "col"), axis=1, tiled=True),
    )
    length = inputs.shape[0]
    block_rows = 512
    prefix = prefix_len[0]
    source = inputs.astype(jnp.float32)
    normed1, scaled1, inverse1 = norm_forward(source, norm1_gain, norm1_shift)
    normed1_low = normed1.astype(jnp.bfloat16)
    projected = jnp.einsum("td,cdn->ctn", normed1_low, full_qkv, preferred_element_type=jnp.float32)
    bias_rows = jnp.stack([b_qv[0], jnp.zeros_like(b_qv[0]), b_qv[1]])
    projected = (projected + bias_rows[:, None, :]).astype(jnp.bfloat16)
    queries, keys_low, values_low = (projected[0], projected[1], projected[2])
    context, maxima, totals = attend_forward(queries, keys_low, values_low, prefix, block_rows)
    context_low = context.astype(jnp.bfloat16)
    attn_partial = jnp.dot(context_low, full_out, preferred_element_type=jnp.float32)
    hidden = source + lax.psum(attn_partial.astype(jnp.bfloat16), "row").astype(jnp.float32) + b_out
    normed2, scaled2, inverse2 = norm_forward(hidden, norm2_gain, norm2_shift)
    normed2_low = normed2.astype(jnp.bfloat16)
    pre_act = jnp.dot(normed2_low, full_in, preferred_element_type=jnp.float32) + b_in
    activated, gelu_pull = jax.vjp(partial(jax.nn.gelu, approximate=False), pre_act)
    activated_low = activated.astype(jnp.bfloat16)
    mlp_partial = jnp.dot(activated_low, full_down, preferred_element_type=jnp.float32)
    result = hidden + lax.psum(mlp_partial.astype(jnp.bfloat16), "row").astype(jnp.float32) + b_down
    output = result.astype(jnp.bfloat16)
    grad_top = d_output.astype(jnp.float32)
    grad_bdown = jnp.sum(grad_top, axis=0)
    grad_wdown = jnp.einsum(
        "tf,td->fd", activated_low, d_output, preferred_element_type=jnp.float32
    )
    grad_act = jnp.einsum("td,fd->tf", d_output, full_down, preferred_element_type=jnp.float32)
    grad_pre = gelu_pull(grad_act)[0].astype(jnp.bfloat16)
    grad_bin = jnp.sum(grad_pre.astype(jnp.float32), axis=0)
    grad_win = jnp.einsum("td,tf->df", normed2_low, grad_pre, preferred_element_type=jnp.float32)
    norm2_partial = jnp.einsum("tf,df->td", grad_pre, full_in, preferred_element_type=jnp.float32)
    grad_normed2 = lax.psum(norm2_partial.astype(jnp.bfloat16), "row").astype(jnp.float32)
    grad_gain2 = jnp.sum(grad_normed2 * scaled2, axis=0)
    grad_shift2 = jnp.sum(grad_normed2, axis=0)
    grad_hidden = grad_top + norm_backward(grad_normed2, scaled2, inverse2, norm2_gain)
    grad_branch = grad_hidden.astype(jnp.bfloat16)
    grad_bout = jnp.sum(grad_branch.astype(jnp.float32), axis=0)
    grad_wout = jnp.einsum(
        "tr,td->rd", context_low, grad_branch, preferred_element_type=jnp.float32
    )
    grad_context = jnp.einsum(
        "td,rd->tr", grad_branch, full_out, preferred_element_type=jnp.float32
    ).astype(jnp.bfloat16)
    grad_queries, grad_keys, grad_values = attend_backward(
        queries, keys_low, values_low, prefix, block_rows, maxima, totals, grad_context
    )
    grad_projected = jnp.stack([grad_queries, grad_keys, grad_values])
    grad_bqv = jnp.stack(
        [
            jnp.sum(grad_queries.astype(jnp.float32), axis=0),
            jnp.sum(grad_values.astype(jnp.float32), axis=0),
        ]
    )
    grad_wqkv = jnp.einsum(
        "td,ctn->cdn", normed1_low, grad_projected, preferred_element_type=jnp.float32
    )
    norm1_partial = jnp.einsum(
        "ctn,cdn->td", grad_projected, full_qkv, preferred_element_type=jnp.float32
    )
    grad_normed1 = lax.psum(norm1_partial.astype(jnp.bfloat16), "row").astype(jnp.float32)
    grad_gain1 = jnp.sum(grad_normed1 * scaled1, axis=0)
    grad_shift1 = jnp.sum(grad_normed1, axis=0)
    d_inputs = grad_hidden + norm_backward(grad_normed1, scaled1, inverse1, norm1_gain)
    sent_wqkv, sent_wout, sent_win, sent_wdown = (
        scatter_low(grad_wqkv, 1),
        scatter_low(grad_wout, 1),
        scatter_low(grad_win, 0),
        scatter_low(grad_wdown, 1),
    )
    small = lax.psum(
        (
            grad_gain1,
            grad_shift1,
            grad_bqv,
            grad_bout,
            grad_gain2,
            grad_shift2,
            grad_bin,
            grad_bdown,
        ),
        ("dp", "col"),
    )
    return (
        output,
        d_inputs,
        small[0],
        small[1],
        sent_wqkv,
        small[2],
        sent_wout,
        small[3],
        small[4],
        small[5],
        sent_win,
        small[6],
        sent_wdown,
        small[7],
    )


def solution(mesh):
    return jax.shard_map(
        local,
        mesh=mesh,
        in_specs=(
            P(("dp", "col"), None),
            P(("dp", "col")),
            P(),
            P(),
            P(None, ("dp", "col"), "row"),
            P(None, "row"),
            P("row", ("dp", "col")),
            P(),
            P(),
            P(),
            P(("dp", "col"), "row"),
            P("row"),
            P("row", ("dp", "col")),
            P(),
            P(("dp", "col"), None),
        ),
        out_specs=(
            P(("dp", "col"), None),
            P(("dp", "col"), None),
            P(),
            P(),
            P(None, ("dp", "col"), "row"),
            P(None, "row"),
            P("row", ("dp", "col")),
            P(),
            P(),
            P(),
            P(("dp", "col"), "row"),
            P("row"),
            P("row", ("dp", "col")),
            P(),
        ),
        check_vma=False,
    )
```

```python
from functools import partial

import jax
import jax.numpy as jnp
from jax import lax
from jax.experimental import pallas as pl
from jax.experimental.pallas import tpu as pltpu
from jax.sharding import PartitionSpec as P

HEAD_DIM = 128
MESH_IDS = pl.DeviceIdType.MESH
CHUNK = 32
LAG = 2


eps_norm = 1e-05


def norm_forward(values, norm_gain, norm_shift):
    average = jnp.mean(values, axis=-1, keepdims=True)
    centered = values - average
    variance = jnp.mean(centered * centered, axis=-1, keepdims=True)
    inverse = lax.rsqrt(variance + eps_norm)
    scaled = centered * inverse
    return (scaled * norm_gain + norm_shift, scaled, inverse)


def norm_backward(grad, scaled, inverse, norm_gain):
    grad_scaled = grad * norm_gain
    return inverse * (
        grad_scaled
        - jnp.mean(grad_scaled, axis=-1, keepdims=True)
        - scaled * jnp.mean(grad_scaled * scaled, axis=-1, keepdims=True)
    )


def block_scores(queries, keys_low, block_start, block_rows, prefix):
    length, width = keys_low.shape
    heads = width // HEAD_DIM
    score_scale = HEAD_DIM ** (-0.5)
    query_block = lax.dynamic_slice_in_dim(queries, block_start, block_rows, 0).reshape(
        block_rows, heads, HEAD_DIM
    )
    key_heads = keys_low.reshape(length, heads, HEAD_DIM)
    scores = (
        jnp.einsum("qhd,khd->hqk", query_block, key_heads, preferred_element_type=jnp.float32)
        * score_scale
    )
    rows_here = block_start + lax.iota(jnp.int32, block_rows)
    columns = lax.iota(jnp.int32, length)
    allowed = (columns[None, :] <= rows_here[:, None]) | (columns[None, :] < prefix)
    return (jnp.where(allowed[None], scores, -1000000000.0), query_block, key_heads)


def attend_forward(queries, keys_low, values_low, prefix, block_rows):
    length, width = queries.shape
    heads = width // HEAD_DIM
    value_heads = values_low.reshape(length, heads, HEAD_DIM)

    def one_block(block_index):
        block_start = block_index * block_rows
        scores, _, _ = block_scores(queries, keys_low, block_start, block_rows, prefix)
        row_max = jnp.max(scores, axis=-1)
        expo = jnp.exp(scores - row_max[..., None])
        row_total = jnp.sum(expo, axis=-1)
        probs_low = (expo / row_total[..., None]).astype(jnp.bfloat16)
        context = jnp.einsum(
            "hqk,khd->qhd", probs_low, value_heads, preferred_element_type=jnp.float32
        )
        return (context.reshape(block_rows, width), row_max, row_total)

    contexts, maxima, totals = lax.map(one_block, jnp.arange(length // block_rows, dtype=jnp.int32))
    return (contexts.reshape(length, width), maxima, totals)


def attend_backward(queries, keys_low, values_low, prefix, block_rows, maxima, totals, d_context):
    length, width = queries.shape
    heads = width // HEAD_DIM
    score_scale = HEAD_DIM ** (-0.5)
    value_heads = values_low.reshape(length, heads, HEAD_DIM)

    def one_block(sums, entries):
        block_index, row_max, row_total = entries
        block_start = block_index * block_rows
        scores, query_block, key_heads = block_scores(
            queries, keys_low, block_start, block_rows, prefix
        )
        probs = jnp.exp(scores - row_max[..., None]) / row_total[..., None]
        probs_low = probs.astype(jnp.bfloat16)
        grad_block = lax.dynamic_slice_in_dim(d_context, block_start, block_rows, 0).reshape(
            block_rows, heads, HEAD_DIM
        )
        d_probs = jnp.einsum(
            "qhd,khd->hqk", grad_block, value_heads, preferred_element_type=jnp.float32
        )
        inner = jnp.sum(d_probs * probs, axis=-1, keepdims=True)
        d_scores = (probs * (d_probs - inner)).astype(jnp.bfloat16)
        d_query = (
            jnp.einsum("hqk,khd->qhd", d_scores, key_heads, preferred_element_type=jnp.float32)
            * score_scale
        )
        d_keys = (
            sums[0]
            + jnp.einsum("hqk,qhd->khd", d_scores, query_block, preferred_element_type=jnp.float32)
            * score_scale
        )
        d_values = sums[1] + jnp.einsum(
            "hqk,qhd->khd", probs_low, grad_block, preferred_element_type=jnp.float32
        )
        return ((d_keys, d_values), d_query.reshape(block_rows, width).astype(jnp.bfloat16))

    zeros = jnp.zeros((length, heads, HEAD_DIM), jnp.float32)
    count = length // block_rows
    (d_keys, d_values), d_queries = lax.scan(
        one_block, (zeros, zeros), (jnp.arange(count, dtype=jnp.int32), maxima, totals)
    )
    return (
        d_queries.reshape(length, width),
        d_keys.reshape(length, width).astype(jnp.bfloat16),
        d_values.reshape(length, width).astype(jnp.bfloat16),
    )


def sum_row_kernel(n, p_ref, o_ref, held, rs_s, rs_r, ag_s, ag_r, loc):
    half = p_ref.shape[0] // 2
    chunks = half // CHUNK
    r = lax.axis_index("row")
    last = n - 1
    bar = pltpu.get_barrier_semaphore()
    for cond, dev in ((r > 0, r - 1), (r < last, r + 1)):

        @pl.when(cond)
        def _():
            pl.semaphore_signal(bar, inc=1, device_id={"row": dev}, device_id_type=MESH_IDS)

    inside = (r > 0) & (r < last)

    @pl.when(inside)
    def _():
        pl.semaphore_wait(bar, 2)

    @pl.when(jnp.logical_not(inside))
    def _():
        pl.semaphore_wait(bar, 1)

    place = (r, last - r)
    after = (jnp.minimum(r + 1, last), jnp.maximum(r - 1, 0))
    before = (jnp.maximum(r - 1, 0), jnp.minimum(r + 1, last))

    def rows(d, c):
        return pl.ds(pl.multiple_of((half if d == 0 else 0) + c * CHUNK, CHUNK), CHUNK)

    def onward(d, c, src):
        return pltpu.make_async_remote_copy(
            src_ref=src.at[rows(d, c)],
            dst_ref=held.at[rows(d, c)],
            send_sem=rs_s.at[d, c],
            recv_sem=rs_r.at[d, c],
            device_id={"row": after[d]},
            device_id_type=MESH_IDS,
        )

    def back(d, c, src):
        return pltpu.make_async_remote_copy(
            src_ref=src.at[rows(d, c)],
            dst_ref=o_ref.at[rows(d, c)],
            send_sem=ag_s.at[d, c],
            recv_sem=ag_r.at[d, c],
            device_id={"row": before[d]},
            device_id_type=MESH_IDS,
        )

    def keep(d, c):
        return pltpu.make_async_copy(held.at[rows(d, c)], o_ref.at[rows(d, c)], loc.at[c])

    def step(t, carry):
        for d in (0, 1):

            @pl.when((place[d] == 0) & (t < chunks))
            def _():
                onward(d, t, p_ref).start()

            c = t - LAG * place[d]

            @pl.when((place[d] > 0) & (c >= 0) & (c < chunks))
            def _():
                onward(d, c, p_ref).wait_recv()
                here = rows(d, c)
                held[here] = (
                    held[here].astype(jnp.float32) + p_ref[here].astype(jnp.float32)
                ).astype(jnp.bfloat16)

                @pl.when(place[d] < last)
                def _():
                    onward(d, c, held).start()

                @pl.when(place[d] == last)
                def _():
                    back(d, c, held).start()
                    keep(d, c).start()

        for d in (0, 1):
            c = t - LAG * (2 * last - place[d])

            @pl.when((place[d] < last) & (c >= 0) & (c < chunks))
            def _():
                back(d, c, o_ref).wait_recv()

                @pl.when(place[d] > 0)
                def _():
                    back(d, c, o_ref).start()

        return carry

    lax.fori_loop(0, chunks + LAG * 2 * last, step, 0)

    def drain(c, carry):
        for d in (0, 1):

            @pl.when(place[d] < last)
            def _():
                onward(d, c, p_ref).wait_send()

            @pl.when(place[d] > 0)
            def _():
                back(d, c, o_ref).wait_send()

            @pl.when(place[d] == last)
            def _():
                keep(d, c).wait()

        return carry

    lax.fori_loop(0, chunks, drain, 0)


def sum_row(partial_low, collective_id):
    n = lax.axis_size("row")
    chunks = partial_low.shape[0] // 2 // CHUNK
    dma = pltpu.SemaphoreType.DMA
    return pl.pallas_call(
        partial(sum_row_kernel, n),
        out_shape=jax.ShapeDtypeStruct(partial_low.shape, partial_low.dtype),
        in_specs=[pl.BlockSpec(memory_space=pltpu.VMEM)],
        out_specs=pl.BlockSpec(memory_space=pl.ANY),
        scratch_shapes=[
            pltpu.VMEM(partial_low.shape, partial_low.dtype),
            dma((2, chunks)),
            dma((2, chunks)),
            dma((2, chunks)),
            dma((2, chunks)),
            dma((chunks,)),
        ],
        compiler_params=pltpu.CompilerParams(
            collective_id=collective_id, has_side_effects=True, vmem_limit_bytes=16 * 2**20
        ),
    )(partial_low)


def scatter_low(grad, dim):
    low = grad.astype(jnp.bfloat16)
    summed = lax.psum_scatter(low, ("dp", "col"), scatter_dimension=dim, tiled=True)
    return summed.astype(jnp.float32)


def local(
    inputs,
    prefix_len,
    norm1_gain,
    norm1_shift,
    w_qkv,
    b_qv,
    w_out,
    b_out,
    norm2_gain,
    norm2_shift,
    w_in,
    b_in,
    w_down,
    b_down,
    d_output,
):
    low_mats = (
        w_qkv.astype(jnp.bfloat16),
        w_out.astype(jnp.bfloat16),
        w_in.astype(jnp.bfloat16),
        w_down.astype(jnp.bfloat16),
    )
    full_qkv, full_out, full_in, full_down = (
        lax.all_gather(low_mats[0], ("dp", "col"), axis=1, tiled=True),
        lax.all_gather(low_mats[1], ("dp", "col"), axis=1, tiled=True),
        lax.all_gather(low_mats[2], ("dp", "col"), axis=0, tiled=True),
        lax.all_gather(low_mats[3], ("dp", "col"), axis=1, tiled=True),
    )
    length = inputs.shape[0]
    block_rows = 512
    prefix = prefix_len[0]
    source = inputs.astype(jnp.float32)
    normed1, scaled1, inverse1 = norm_forward(source, norm1_gain, norm1_shift)
    normed1_low = normed1.astype(jnp.bfloat16)
    projected = jnp.einsum("td,cdn->ctn", normed1_low, full_qkv, preferred_element_type=jnp.float32)
    bias_rows = jnp.stack([b_qv[0], jnp.zeros_like(b_qv[0]), b_qv[1]])
    projected = (projected + bias_rows[:, None, :]).astype(jnp.bfloat16)
    queries, keys_low, values_low = (projected[0], projected[1], projected[2])
    context, maxima, totals = attend_forward(queries, keys_low, values_low, prefix, block_rows)
    context_low = context.astype(jnp.bfloat16)
    attn_partial = jnp.dot(context_low, full_out, preferred_element_type=jnp.float32)
    hidden = source + sum_row(attn_partial.astype(jnp.bfloat16), 0).astype(jnp.float32) + b_out
    normed2, scaled2, inverse2 = norm_forward(hidden, norm2_gain, norm2_shift)
    normed2_low = normed2.astype(jnp.bfloat16)
    pre_act = jnp.dot(normed2_low, full_in, preferred_element_type=jnp.float32) + b_in
    activated, gelu_pull = jax.vjp(partial(jax.nn.gelu, approximate=False), pre_act)
    activated_low = activated.astype(jnp.bfloat16)
    mlp_partial = jnp.dot(activated_low, full_down, preferred_element_type=jnp.float32)
    result = hidden + sum_row(mlp_partial.astype(jnp.bfloat16), 1).astype(jnp.float32) + b_down
    output = result.astype(jnp.bfloat16)
    grad_top = d_output.astype(jnp.float32)
    grad_bdown = jnp.sum(grad_top, axis=0)
    grad_wdown = jnp.einsum(
        "tf,td->fd", activated_low, d_output, preferred_element_type=jnp.float32
    )
    grad_act = jnp.einsum("td,fd->tf", d_output, full_down, preferred_element_type=jnp.float32)
    grad_pre = gelu_pull(grad_act)[0].astype(jnp.bfloat16)
    grad_bin = jnp.sum(grad_pre.astype(jnp.float32), axis=0)
    grad_win = jnp.einsum("td,tf->df", normed2_low, grad_pre, preferred_element_type=jnp.float32)
    norm2_partial = jnp.einsum("tf,df->td", grad_pre, full_in, preferred_element_type=jnp.float32)
    grad_normed2 = sum_row(norm2_partial.astype(jnp.bfloat16), 2).astype(jnp.float32)
    grad_gain2 = jnp.sum(grad_normed2 * scaled2, axis=0)
    grad_shift2 = jnp.sum(grad_normed2, axis=0)
    grad_hidden = grad_top + norm_backward(grad_normed2, scaled2, inverse2, norm2_gain)
    grad_branch = grad_hidden.astype(jnp.bfloat16)
    grad_bout = jnp.sum(grad_branch.astype(jnp.float32), axis=0)
    grad_wout = jnp.einsum(
        "tr,td->rd", context_low, grad_branch, preferred_element_type=jnp.float32
    )
    grad_context = jnp.einsum(
        "td,rd->tr", grad_branch, full_out, preferred_element_type=jnp.float32
    ).astype(jnp.bfloat16)
    grad_queries, grad_keys, grad_values = attend_backward(
        queries, keys_low, values_low, prefix, block_rows, maxima, totals, grad_context
    )
    grad_projected = jnp.stack([grad_queries, grad_keys, grad_values])
    grad_bqv = jnp.stack(
        [
            jnp.sum(grad_queries.astype(jnp.float32), axis=0),
            jnp.sum(grad_values.astype(jnp.float32), axis=0),
        ]
    )
    grad_wqkv = jnp.einsum(
        "td,ctn->cdn", normed1_low, grad_projected, preferred_element_type=jnp.float32
    )
    norm1_partial = jnp.einsum(
        "ctn,cdn->td", grad_projected, full_qkv, preferred_element_type=jnp.float32
    )
    grad_normed1 = sum_row(norm1_partial.astype(jnp.bfloat16), 3).astype(jnp.float32)
    grad_gain1 = jnp.sum(grad_normed1 * scaled1, axis=0)
    grad_shift1 = jnp.sum(grad_normed1, axis=0)
    d_inputs = grad_hidden + norm_backward(grad_normed1, scaled1, inverse1, norm1_gain)
    sent_wqkv, sent_wout, sent_win, sent_wdown = (
        scatter_low(grad_wqkv, 1),
        scatter_low(grad_wout, 1),
        scatter_low(grad_win, 0),
        scatter_low(grad_wdown, 1),
    )
    small = lax.psum(
        (
            grad_gain1,
            grad_shift1,
            grad_bqv,
            grad_bout,
            grad_gain2,
            grad_shift2,
            grad_bin,
            grad_bdown,
        ),
        ("dp", "col"),
    )
    return (
        output,
        d_inputs,
        small[0],
        small[1],
        sent_wqkv,
        small[2],
        sent_wout,
        small[3],
        small[4],
        small[5],
        sent_win,
        small[6],
        sent_wdown,
        small[7],
    )


def solution(mesh):
    return jax.shard_map(
        local,
        mesh=mesh,
        in_specs=(
            P(("dp", "col"), None),
            P(("dp", "col")),
            P(),
            P(),
            P(None, ("dp", "col"), "row"),
            P(None, "row"),
            P("row", ("dp", "col")),
            P(),
            P(),
            P(),
            P(("dp", "col"), "row"),
            P("row"),
            P("row", ("dp", "col")),
            P(),
            P(("dp", "col"), None),
        ),
        out_specs=(
            P(("dp", "col"), None),
            P(("dp", "col"), None),
            P(),
            P(),
            P(None, ("dp", "col"), "row"),
            P(None, "row"),
            P("row", ("dp", "col")),
            P(),
            P(),
            P(),
            P(("dp", "col"), "row"),
            P("row"),
            P("row", ("dp", "col")),
            P(),
        ),
        check_vma=False,
    )
```

```python
from functools import partial

import jax
import jax.numpy as jnp
from jax import lax
from jax.experimental import pallas as pl
from jax.experimental.pallas import tpu as pltpu
from jax.sharding import PartitionSpec as P

HEAD_DIM = 128
MESH_IDS = pl.DeviceIdType.MESH
CHUNK = 32
LAG = 2


eps_norm = 1e-05


def norm_forward(values, norm_gain, norm_shift):
    average = jnp.mean(values, axis=-1, keepdims=True)
    centered = values - average
    variance = jnp.mean(centered * centered, axis=-1, keepdims=True)
    inverse = lax.rsqrt(variance + eps_norm)
    scaled = centered * inverse
    return (scaled * norm_gain + norm_shift, scaled, inverse)


def norm_backward(grad, scaled, inverse, norm_gain):
    grad_scaled = grad * norm_gain
    return inverse * (
        grad_scaled
        - jnp.mean(grad_scaled, axis=-1, keepdims=True)
        - scaled * jnp.mean(grad_scaled * scaled, axis=-1, keepdims=True)
    )


def block_scores(queries, keys_low, block_start, block_rows, prefix):
    length, width = keys_low.shape
    heads = width // HEAD_DIM
    score_scale = HEAD_DIM ** (-0.5)
    query_block = lax.dynamic_slice_in_dim(queries, block_start, block_rows, 0).reshape(
        block_rows, heads, HEAD_DIM
    )
    key_heads = keys_low.reshape(length, heads, HEAD_DIM)
    scores = (
        jnp.einsum("qhd,khd->hqk", query_block, key_heads, preferred_element_type=jnp.float32)
        * score_scale
    )
    rows_here = block_start + lax.iota(jnp.int32, block_rows)
    columns = lax.iota(jnp.int32, length)
    allowed = (columns[None, :] <= rows_here[:, None]) | (columns[None, :] < prefix)
    return (jnp.where(allowed[None], scores, -1000000000.0), query_block, key_heads)


def attend_forward(queries, keys_low, values_low, prefix, block_rows):
    length, width = queries.shape
    heads = width // HEAD_DIM
    value_heads = values_low.reshape(length, heads, HEAD_DIM)

    def one_block(block_index):
        block_start = block_index * block_rows
        scores, _, _ = block_scores(queries, keys_low, block_start, block_rows, prefix)
        row_max = jnp.max(scores, axis=-1)
        expo = jnp.exp(scores - row_max[..., None])
        row_total = jnp.sum(expo, axis=-1)
        probs_low = (expo / row_total[..., None]).astype(jnp.bfloat16)
        context = jnp.einsum(
            "hqk,khd->qhd", probs_low, value_heads, preferred_element_type=jnp.float32
        )
        return (context.reshape(block_rows, width), row_max, row_total)

    contexts, maxima, totals = lax.map(one_block, jnp.arange(length // block_rows, dtype=jnp.int32))
    return (contexts.reshape(length, width), maxima, totals)


def dot(left, right, left_dim, right_dim):
    return lax.dot_general(
        left, right, (((left_dim,), (right_dim,)), ((), ())), preferred_element_type=jnp.float32
    )


def line_sum(n, p_ref, o_ref, held, rs_s, rs_r, ag_s, ag_r, loc):
    half = p_ref.shape[0] // 2
    chunks = half // CHUNK
    r = lax.axis_index("row")
    last = n - 1
    bar = pltpu.get_barrier_semaphore()
    for cond, dev in ((r > 0, r - 1), (r < last, r + 1)):

        @pl.when(cond)
        def _():
            pl.semaphore_signal(bar, inc=1, device_id={"row": dev}, device_id_type=MESH_IDS)

    inside = (r > 0) & (r < last)

    @pl.when(inside)
    def _():
        pl.semaphore_wait(bar, 2)

    @pl.when(jnp.logical_not(inside))
    def _():
        pl.semaphore_wait(bar, 1)

    place = (r, last - r)
    after = (jnp.minimum(r + 1, last), jnp.maximum(r - 1, 0))
    before = (jnp.maximum(r - 1, 0), jnp.minimum(r + 1, last))

    def rows(d, c):
        return pl.ds(pl.multiple_of((half if d == 0 else 0) + c * CHUNK, CHUNK), CHUNK)

    def onward(d, c, src):
        return pltpu.make_async_remote_copy(
            src_ref=src.at[rows(d, c)],
            dst_ref=held.at[rows(d, c)],
            send_sem=rs_s.at[d, c],
            recv_sem=rs_r.at[d, c],
            device_id={"row": after[d]},
            device_id_type=MESH_IDS,
        )

    def back(d, c, src):
        return pltpu.make_async_remote_copy(
            src_ref=src.at[rows(d, c)],
            dst_ref=o_ref.at[rows(d, c)],
            send_sem=ag_s.at[d, c],
            recv_sem=ag_r.at[d, c],
            device_id={"row": before[d]},
            device_id_type=MESH_IDS,
        )

    def keep(d, c):
        return pltpu.make_async_copy(held.at[rows(d, c)], o_ref.at[rows(d, c)], loc.at[c])

    def step(t):
        for d in (0, 1):

            @pl.when((place[d] == 0) & (t < chunks))
            def _():
                onward(d, t, p_ref).start()

            c = t - LAG * place[d]

            @pl.when((place[d] > 0) & (c >= 0) & (c < chunks))
            def _():
                onward(d, c, p_ref).wait_recv()
                here = rows(d, c)
                held[here] = (
                    held[here].astype(jnp.float32) + p_ref[here].astype(jnp.float32)
                ).astype(jnp.bfloat16)

                @pl.when(place[d] < last)
                def _():
                    onward(d, c, held).start()

                @pl.when(place[d] == last)
                def _():
                    back(d, c, held).start()
                    keep(d, c).start()

        for d in (0, 1):
            c = t - LAG * (2 * last - place[d])

            @pl.when((place[d] < last) & (c >= 0) & (c < chunks))
            def _():
                back(d, c, o_ref).wait_recv()

                @pl.when(place[d] > 0)
                def _():
                    back(d, c, o_ref).start()

    def drain():
        def one(c, carry):
            for d in (0, 1):

                @pl.when(place[d] < last)
                def _():
                    onward(d, c, p_ref).wait_send()

                @pl.when(place[d] > 0)
                def _():
                    back(d, c, o_ref).wait_send()

                @pl.when(place[d] == last)
                def _():
                    keep(d, c).wait()

            return carry

        lax.fori_loop(0, chunks, one, 0)

    return step, drain


def line_steps(n, total_rows):
    return total_rows // 2 // CHUNK + LAG * 2 * (n - 1)


def line_scratch(shape):
    chunks = shape[0] // 2 // CHUNK
    dma = pltpu.SemaphoreType.DMA
    return [
        pltpu.VMEM(shape, jnp.bfloat16),
        dma((2, chunks)),
        dma((2, chunks)),
        dma((2, chunks)),
        dma((2, chunks)),
        dma((chunks,)),
    ]


def loop(start, stop, body):
    def one(t, carry):
        body(t)
        return carry

    lax.fori_loop(start, stop, one, 0)


IN_VMEM = pl.BlockSpec(memory_space=pltpu.VMEM)
IN_HBM = pl.BlockSpec(memory_space=pl.ANY)


def low_shape(*shape):
    return jax.ShapeDtypeStruct(shape, jnp.bfloat16)


def kernel_params(collective_id, mib):
    return pltpu.CompilerParams(
        collective_id=collective_id, has_side_effects=True, vmem_limit_bytes=mib * 2**20
    )


COST = pl.CostEstimate(flops=1000, bytes_accessed=1000, transcendentals=0)


def sum_row_kernel(n, p_ref, o_ref, *line):
    step, drain = line_sum(n, p_ref, o_ref, *line)
    loop(0, line_steps(n, p_ref.shape[0]), step)
    drain()


def sum_row(partial_low):
    return pl.pallas_call(
        partial(sum_row_kernel, lax.axis_size("row")),
        out_shape=low_shape(*partial_low.shape),
        in_specs=[IN_VMEM],
        out_specs=IN_HBM,
        scratch_shapes=line_scratch(partial_low.shape),
        compiler_params=kernel_params(0, 16),
        cost_estimate=COST,
    )(partial_low)


TILE_M = 512
TILE_N = 1024


def products_sum_kernel(n, p_ref, *refs):
    pairs = 2
    sources = refs[: 2 * pairs]
    o_ref = refs[2 * pairs]
    outs = refs[2 * pairs + 1 : 3 * pairs + 1]
    held = refs[3 * pairs + 1 : 5 * pairs + 1]
    stage, load_sem, store_sem = refs[5 * pairs + 1 : 5 * pairs + 4]
    line = refs[5 * pairs + 4 :]
    loads = [
        pltpu.make_async_copy(src, dst, load_sem.at[i])
        for i, (src, dst) in enumerate(zip(sources, held))
    ]
    for load in loads:
        load.start()
    step, drain = line_sum(n, p_ref, o_ref, *line)
    steps = line_steps(n, p_ref.shape[0])
    across = outs[0].shape[1] // TILE_N
    tiles = (outs[0].shape[0] // TILE_M) * across
    begin = 3

    def store(k, tile):
        m = pl.ds(pl.multiple_of((tile // across) * TILE_M, TILE_M), TILE_M)
        c = pl.ds(pl.multiple_of(lax.rem(tile, across) * TILE_N, TILE_N), TILE_N)
        slot = lax.rem(tile, 2)
        return m, c, slot, pltpu.make_async_copy(
            stage.at[slot], outs[k].at[m, c], store_sem.at[slot]
        )

    loop(0, begin, step)
    for k in range(pairs):
        loads[2 * k].wait()
        loads[2 * k + 1].wait()

        def body(t):
            step(t)
            tile = t - begin - k * tiles
            m, c, slot, copy = store(k, tile)

            if k == 0:

                @pl.when(tile >= 2)
                def _():
                    store(k, tile - 2)[3].wait()
            else:
                copy.wait()

            stage[slot] = dot(held[2 * k][:, m], held[2 * k + 1][:, c], 0, 0).astype(jnp.bfloat16)
            copy.start()

        loop(begin + k * tiles, begin + (k + 1) * tiles, body)
    loop(begin + pairs * tiles, steps, step)
    for slot in range(2):
        store(pairs - 1, slot)[3].wait()
    drain()


def products_sum(partial_low, pairs):
    sources = [array for pair in pairs for array in pair]
    out = [low_shape(left.shape[1], right.shape[1]) for left, right in pairs]
    dma = pltpu.SemaphoreType.DMA
    return pl.pallas_call(
        partial(products_sum_kernel, lax.axis_size("row")),
        out_shape=[low_shape(*partial_low.shape)] + out,
        in_specs=[IN_VMEM] + [IN_HBM] * len(sources),
        out_specs=[IN_HBM] * (1 + len(out)),
        scratch_shapes=[pltpu.VMEM(array.shape, jnp.bfloat16) for array in sources]
        + [pltpu.VMEM((2, TILE_M, TILE_N), jnp.bfloat16), dma((len(sources),)), dma((2,))]
        + line_scratch(partial_low.shape),
        compiler_params=kernel_params(1, 48),
        cost_estimate=COST,
    )(partial_low, *sources)


QUERY_ROWS = 256


def attend_piece(i, prefix, cols, q, k, v, k_t, d_context, d_proj, d_key, d_value, first):
    start = i * QUERY_ROWS
    width = max(start + QUERY_ROWS, q.shape[0] // 2)
    here = slice(start, start + QUERY_ROWS)
    score_scale = HEAD_DIM ** (-0.5)
    q_block, g_block = q[here, cols], d_context[here, cols]
    scores = dot(k[:width, cols], q_block, 1, 1) * score_scale
    key = lax.broadcasted_iota(jnp.int32, scores.shape, 0)
    query = lax.broadcasted_iota(jnp.int32, scores.shape, 1) + start
    scores = jnp.where((key <= query) | (key < prefix), scores, -1000000000.0)
    expo = jnp.exp(scores - jnp.max(scores, axis=0, keepdims=True))
    probs = expo * (1.0 / jnp.sum(expo, axis=0, keepdims=True))
    d_probs = dot(v[:width, cols], g_block, 1, 1)
    inner = jnp.sum(d_probs * probs, axis=0, keepdims=True)
    d_scores = (probs * (d_probs - inner)).astype(jnp.bfloat16)
    d_query = dot(k_t[cols, :width], d_scores, 1, 0) * score_scale
    d_proj[0, here, cols] = d_query.T.astype(jnp.bfloat16)
    for total, term in (
        (d_key, dot(d_scores, q_block, 1, 0)),
        (d_value, dot(probs.astype(jnp.bfloat16), g_block, 1, 0)),
    ):
        if first:
            total[...] = term
        else:
            total[:width] += term


def attend_sum_kernel(
    n, prefix_ref, p_ref, q, k, v, k_t, d_context, n1_hbm, ctx_hbm, branch_hbm,
    o_ref, d_proj, d_bias, d_wqkv, d_wout,
    n1, ctx, branch, d_key, d_value, load_sem, *line,
):
    loads = [
        pltpu.make_async_copy(src, dst, load_sem.at[i])
        for i, (src, dst) in enumerate(((n1_hbm, n1), (ctx_hbm, ctx), (branch_hbm, branch)))
    ]
    for load in loads:
        load.start()
    step, drain = line_sum(n, p_ref, o_ref, *line)
    steps = line_steps(n, p_ref.shape[0])
    prefix = prefix_ref[0]
    blocks = q.shape[0] // QUERY_ROWS
    heads = q.shape[1] // HEAD_DIM

    def head(h):
        cols = pl.ds(pl.multiple_of(h * HEAD_DIM, HEAD_DIM), HEAD_DIM)
        for j in range(blocks):
            step(h * blocks + j)
            attend_piece(
                blocks - 1 - j, prefix, cols, q, k, v, k_t, d_context, d_proj, d_key, d_value,
                j == 0,
            )
        d_proj[1, :, cols] = (d_key[...] * HEAD_DIM ** (-0.5)).astype(jnp.bfloat16)
        d_proj[2, :, cols] = d_value[...].astype(jnp.bfloat16)
        for b, c in ((0, 0), (1, 2)):
            d_bias[b : b + 1, cols] = jnp.sum(
                d_proj[c, :, cols].astype(jnp.float32), axis=0, keepdims=True
            )

    loop(0, heads, head)
    for load in loads:
        load.wait()
    begin = heads * blocks
    tiles = n1.shape[1] // TILE_M

    for c in range(3):

        def body(t):
            step(t)
            m = pl.ds(pl.multiple_of((t - begin - c * tiles) * TILE_M, TILE_M), TILE_M)
            d_wqkv[c, m] = dot(n1[:, m], d_proj[c], 0, 0).astype(jnp.bfloat16)
            if c == 0:
                d_wout[:, m] = dot(ctx[...], branch[:, m], 0, 0).astype(jnp.bfloat16)

        loop(begin + c * tiles, begin + (c + 1) * tiles, body)
    loop(begin + 3 * tiles, steps, step)
    drain()


def attend_sum(prefix_len, partial_low, q, k, v, d_context, normed1, context, d_branch):
    tokens, width = q.shape
    depth = normed1.shape[1]
    dma = pltpu.SemaphoreType.DMA
    return pl.pallas_call(
        partial(attend_sum_kernel, lax.axis_size("row")),
        out_shape=[
            low_shape(*partial_low.shape),
            low_shape(3, tokens, width),
            jax.ShapeDtypeStruct((2, width), jnp.float32),
            low_shape(3, depth, width),
            low_shape(width, depth),
        ],
        in_specs=[pl.BlockSpec(memory_space=pltpu.SMEM)] + [IN_VMEM] * 6 + [IN_HBM] * 3,
        out_specs=[IN_HBM] + [IN_VMEM] * 4,
        scratch_shapes=[
            pltpu.VMEM((tokens, depth), jnp.bfloat16),
            pltpu.VMEM((tokens, width), jnp.bfloat16),
            pltpu.VMEM((tokens, depth), jnp.bfloat16),
            pltpu.VMEM((tokens, HEAD_DIM), jnp.float32),
            pltpu.VMEM((tokens, HEAD_DIM), jnp.float32),
            dma((3,)),
        ]
        + line_scratch(partial_low.shape),
        compiler_params=kernel_params(2, 56),
        cost_estimate=COST,
    )(prefix_len, partial_low, q, k, v, k.T, d_context, normed1, context, d_branch)


def scatter_low(grad, dim):
    summed = lax.psum_scatter(grad, ("dp", "col"), scatter_dimension=dim, tiled=True)
    return summed.astype(jnp.float32)


def local(
    inputs,
    prefix_len,
    norm1_gain,
    norm1_shift,
    w_qkv,
    b_qv,
    w_out,
    b_out,
    norm2_gain,
    norm2_shift,
    w_in,
    b_in,
    w_down,
    b_down,
    d_output,
):
    low_mats = (
        w_qkv.astype(jnp.bfloat16),
        w_out.astype(jnp.bfloat16),
        w_in.astype(jnp.bfloat16),
        w_down.astype(jnp.bfloat16),
    )
    full_qkv, full_out, full_in, full_down = (
        lax.all_gather(low_mats[0], ("dp", "col"), axis=1, tiled=True),
        lax.all_gather(low_mats[1], ("dp", "col"), axis=1, tiled=True),
        lax.all_gather(low_mats[2], ("dp", "col"), axis=0, tiled=True),
        lax.all_gather(low_mats[3], ("dp", "col"), axis=1, tiled=True),
    )
    length = inputs.shape[0]
    block_rows = 512
    prefix = prefix_len[0]
    source = inputs.astype(jnp.float32)
    normed1, scaled1, inverse1 = norm_forward(source, norm1_gain, norm1_shift)
    normed1_low = normed1.astype(jnp.bfloat16)
    projected = jnp.einsum("td,cdn->ctn", normed1_low, full_qkv, preferred_element_type=jnp.float32)
    bias_rows = jnp.stack([b_qv[0], jnp.zeros_like(b_qv[0]), b_qv[1]])
    projected = (projected + bias_rows[:, None, :]).astype(jnp.bfloat16)
    queries, keys_low, values_low = (projected[0], projected[1], projected[2])
    context, maxima, totals = attend_forward(queries, keys_low, values_low, prefix, block_rows)
    context_low = context.astype(jnp.bfloat16)
    attn_partial = jnp.dot(context_low, full_out, preferred_element_type=jnp.float32)
    hidden = source + sum_row(attn_partial.astype(jnp.bfloat16)).astype(jnp.float32) + b_out
    normed2, scaled2, inverse2 = norm_forward(hidden, norm2_gain, norm2_shift)
    normed2_low = normed2.astype(jnp.bfloat16)
    pre_act = jnp.dot(normed2_low, full_in, preferred_element_type=jnp.float32) + b_in
    activated, gelu_pull = jax.vjp(partial(jax.nn.gelu, approximate=False), pre_act)
    activated_low = activated.astype(jnp.bfloat16)
    mlp_partial = jnp.dot(activated_low, full_down, preferred_element_type=jnp.float32)
    grad_top = d_output.astype(jnp.float32)
    grad_bdown = jnp.sum(grad_top, axis=0)
    grad_act = jnp.einsum("td,fd->tf", d_output, full_down, preferred_element_type=jnp.float32)
    grad_pre = gelu_pull(grad_act)[0].astype(jnp.bfloat16)
    grad_bin = jnp.sum(grad_pre.astype(jnp.float32), axis=0)
    norm2_partial = jnp.einsum("tf,df->td", grad_pre, full_in, preferred_element_type=jnp.float32)
    summed2, grad_wdown, grad_win = products_sum(
        norm2_partial.astype(jnp.bfloat16), ((activated_low, d_output), (normed2_low, grad_pre))
    )
    grad_normed2 = summed2.astype(jnp.float32)
    grad_gain2 = jnp.sum(grad_normed2 * scaled2, axis=0)
    grad_shift2 = jnp.sum(grad_normed2, axis=0)
    grad_hidden = grad_top + norm_backward(grad_normed2, scaled2, inverse2, norm2_gain)
    grad_branch = grad_hidden.astype(jnp.bfloat16)
    grad_bout = jnp.sum(grad_branch.astype(jnp.float32), axis=0)
    grad_context = jnp.einsum(
        "td,rd->tr", grad_branch, full_out, preferred_element_type=jnp.float32
    ).astype(jnp.bfloat16)
    mlp_sum, grad_projected, grad_bqv, grad_wqkv, grad_wout = attend_sum(
        prefix_len, mlp_partial.astype(jnp.bfloat16), queries, keys_low, values_low,
        grad_context, normed1_low, context_low, grad_branch,
    )
    output = (hidden + mlp_sum.astype(jnp.float32) + b_down).astype(jnp.bfloat16)
    norm1_partial = jnp.einsum(
        "ctn,cdn->td", grad_projected, full_qkv, preferred_element_type=jnp.float32
    )
    sent_win = scatter_low(grad_win, 0)
    sent_wdown = scatter_low(grad_wdown, 1)
    norm1_low = norm1_partial.astype(jnp.bfloat16)
    grad_wqkv, grad_wout, sent_win, sent_wdown = lax.optimization_barrier(
        (grad_wqkv, grad_wout, sent_win, sent_wdown)
    )
    sent_wout, sent_wqkv = scatter_low(grad_wout, 1), scatter_low(grad_wqkv, 1)
    grad_normed1 = sum_row(norm1_low).astype(jnp.float32)
    grad_gain1 = jnp.sum(grad_normed1 * scaled1, axis=0)
    grad_shift1 = jnp.sum(grad_normed1, axis=0)
    d_inputs = grad_hidden + norm_backward(grad_normed1, scaled1, inverse1, norm1_gain)
    small = lax.psum(
        (
            grad_gain1,
            grad_shift1,
            grad_bqv,
            grad_bout,
            grad_gain2,
            grad_shift2,
            grad_bin,
            grad_bdown,
        ),
        ("dp", "col"),
    )
    return (
        output,
        d_inputs,
        small[0],
        small[1],
        sent_wqkv,
        small[2],
        sent_wout,
        small[3],
        small[4],
        small[5],
        sent_win,
        small[6],
        sent_wdown,
        small[7],
    )


def solution(mesh):
    return jax.shard_map(
        local,
        mesh=mesh,
        in_specs=(
            P(("dp", "col"), None),
            P(("dp", "col")),
            P(),
            P(),
            P(None, ("dp", "col"), "row"),
            P(None, "row"),
            P("row", ("dp", "col")),
            P(),
            P(),
            P(),
            P(("dp", "col"), "row"),
            P("row"),
            P("row", ("dp", "col")),
            P(),
            P(("dp", "col"), None),
        ),
        out_specs=(
            P(("dp", "col"), None),
            P(("dp", "col"), None),
            P(),
            P(),
            P(None, ("dp", "col"), "row"),
            P(None, "row"),
            P("row", ("dp", "col")),
            P(),
            P(),
            P(),
            P(("dp", "col"), "row"),
            P("row"),
            P("row", ("dp", "col")),
            P(),
        ),
        check_vma=False,
    )
```

```python
from functools import partial

import jax
import jax.numpy as jnp
from jax import lax
from jax.experimental import pallas as pl
from jax.experimental.pallas import tpu as pltpu
from jax.sharding import PartitionSpec as P

HEAD_DIM = 128
MESH_IDS = pl.DeviceIdType.MESH
CHUNK = 32
LAG = 2


eps_norm = 1e-05


def norm_forward(values, norm_gain, norm_shift):
    average = jnp.mean(values, axis=-1, keepdims=True)
    centered = values - average
    variance = jnp.mean(centered * centered, axis=-1, keepdims=True)
    inverse = lax.rsqrt(variance + eps_norm)
    scaled = centered * inverse
    return (scaled * norm_gain + norm_shift, scaled, inverse)


def norm_backward(grad, scaled, inverse, norm_gain):
    grad_scaled = grad * norm_gain
    return inverse * (
        grad_scaled
        - jnp.mean(grad_scaled, axis=-1, keepdims=True)
        - scaled * jnp.mean(grad_scaled * scaled, axis=-1, keepdims=True)
    )


def dot(left, right, left_dim, right_dim):
    return lax.dot_general(
        left, right, (((left_dim,), (right_dim,)), ((), ())), preferred_element_type=jnp.float32
    )


def greet_row(n, others=()):
    r = lax.axis_index("row")
    last = n - 1
    bar = pltpu.get_barrier_semaphore()
    for cond, dev in ((r > 0, r - 1), (r < last, r + 1)):

        @pl.when(cond)
        def _():
            pl.semaphore_signal(bar, inc=1, device_id={"row": dev}, device_id_type=MESH_IDS)

    for other in others:
        pl.semaphore_signal(bar, inc=1, device_id=other, device_id_type=MESH_IDS)
    inside = (r > 0) & (r < last)

    @pl.when(inside)
    def _():
        pl.semaphore_wait(bar, 2 + len(others))

    @pl.when(jnp.logical_not(inside))
    def _():
        pl.semaphore_wait(bar, 1 + len(others))


def plane_partners():
    y, x = lax.axis_index("dp"), lax.axis_index("col")
    far_x, near = lax.rem(x + 2, 4), x + 1 - 2 * lax.rem(x, 2)
    far_near = lax.rem(near + 2, 4)
    ids = {"x": {"col": far_x}, "y": {"dp": 1 - y}, "near": {"col": near}}
    mine = {"own": y * 4 + x, "x": y * 4 + far_x, "y": (1 - y) * 4 + x, "xy": (1 - y) * 4 + far_x}
    theirs = {
        "own": y * 4 + near,
        "x": y * 4 + far_near,
        "y": (1 - y) * 4 + near,
        "xy": (1 - y) * 4 + far_near,
    }
    return ids, mine, theirs


KINDS = ("own", "x", "y", "xy")


def plane_gather(pieces, send_sem, recv_sem, near_send, near_recv, local_sem):
    ids, mine, theirs = plane_partners()
    count = len(pieces)

    def remote(kind, k, to, src, dst):
        row = KINDS.index(kind)
        near = to == "near"
        return pltpu.make_async_remote_copy(
            src_ref=src,
            dst_ref=dst,
            send_sem=(near_send if near else send_sem).at[row, k],
            recv_sem=(near_recv if near else recv_sem).at[row, k],
            device_id=ids[to],
            device_id_type=MESH_IDS,
        )

    def outgoing(k):
        own, place = pieces[k](mine["own"])
        return [remote("x", k, "x", own, place), remote("y", k, "y", own, place)]

    def local(k):
        own, place = pieces[k](mine["own"])
        return pltpu.make_async_copy(own, place, local_sem.at[k])

    def onward(k):
        kind, to = ("x", "y") if k % 2 == 0 else ("y", "x")
        place = pieces[k](mine[kind])[1]
        return remote("xy", k, to, place, place)

    def share(kind, k):
        own, place = pieces[k](mine[kind])
        return remote(kind, k, "near", own if kind == "own" else place, place)

    def start():
        for k in range(count):
            for copy in outgoing(k):
                copy.start()
        for k in range(count):
            share("own", k).start()
            local(k).start()

    def arrive(k):
        for copy in outgoing(k):
            copy.wait_recv()
        onward(k).start()
        share("x", k).start()
        share("y", k).start()

    def arrive_far(k):
        onward(k).wait_recv()
        share("xy", k).start()

    def finish():
        for k in range(count):
            local(k).wait()
            for copy in outgoing(k):
                copy.wait_send()
            onward(k).wait_send()
            for kind in KINDS:
                place = pieces[k](theirs[kind])[1]
                share(kind, k).wait_send()
                remote(kind, k, "near", place, place).wait_recv()

    return list(ids.values()), start, arrive, arrive_far, finish


def line_sum(n, p_ref, o_ref, held, rs_s, rs_r, ag_s, ag_r, loc):
    half = p_ref.shape[0] // 2
    chunks = half // CHUNK
    r = lax.axis_index("row")
    last = n - 1
    place = (r, last - r)
    after = (jnp.minimum(r + 1, last), jnp.maximum(r - 1, 0))
    before = (jnp.maximum(r - 1, 0), jnp.minimum(r + 1, last))

    def rows(d, c):
        return pl.ds(pl.multiple_of((half if d == 0 else 0) + c * CHUNK, CHUNK), CHUNK)

    def onward(d, c, src):
        return pltpu.make_async_remote_copy(
            src_ref=src.at[rows(d, c)],
            dst_ref=held.at[rows(d, c)],
            send_sem=rs_s.at[d, c],
            recv_sem=rs_r.at[d, c],
            device_id={"row": after[d]},
            device_id_type=MESH_IDS,
        )

    def back(d, c, src):
        return pltpu.make_async_remote_copy(
            src_ref=src.at[rows(d, c)],
            dst_ref=o_ref.at[rows(d, c)],
            send_sem=ag_s.at[d, c],
            recv_sem=ag_r.at[d, c],
            device_id={"row": before[d]},
            device_id_type=MESH_IDS,
        )

    def keep(d, c):
        return pltpu.make_async_copy(held.at[rows(d, c)], o_ref.at[rows(d, c)], loc.at[c])

    def step(t):
        for d in (0, 1):

            @pl.when((place[d] == 0) & (t >= 0) & (t < chunks))
            def _():
                onward(d, t, p_ref).start()

            c = t - LAG * place[d]

            @pl.when((place[d] > 0) & (c >= 0) & (c < chunks))
            def _():
                onward(d, c, p_ref).wait_recv()
                here = rows(d, c)
                held[here] = (
                    held[here].astype(jnp.float32) + p_ref[here].astype(jnp.float32)
                ).astype(jnp.bfloat16)

                @pl.when(place[d] < last)
                def _():
                    onward(d, c, held).start()

                @pl.when(place[d] == last)
                def _():
                    back(d, c, held).start()
                    keep(d, c).start()

        for d in (0, 1):
            c = t - LAG * (2 * last - place[d])

            @pl.when((place[d] < last) & (c >= 0) & (c < chunks))
            def _():
                back(d, c, o_ref).wait_recv()

                @pl.when(place[d] > 0)
                def _():
                    back(d, c, o_ref).start()

    def settle(c):
        for d in (0, 1):

            @pl.when(place[d] < last)
            def _():
                onward(d, c, p_ref).wait_send()

            @pl.when(place[d] == last)
            def _():
                keep(d, c).wait()

    def finish(c):
        for d in (0, 1):

            @pl.when(place[d] > 0)
            def _():
                back(d, c, o_ref).wait_send()

    def drain():
        def both(c):
            settle(c)
            finish(c)

        loop(0, chunks, both)

    return step, drain, settle, lambda: loop(0, chunks, finish)


def line_steps(n, total_rows):
    return total_rows // 2 // CHUNK + LAG * 2 * (n - 1)


def line_scratch(shape):
    chunks = shape[0] // 2 // CHUNK
    dma = pltpu.SemaphoreType.DMA
    return [
        pltpu.VMEM(shape, jnp.bfloat16),
        dma((2, chunks)),
        dma((2, chunks)),
        dma((2, chunks)),
        dma((2, chunks)),
        dma((chunks,)),
    ]


def loop(start, stop, body):
    def one(t, carry):
        body(t)
        return carry

    lax.fori_loop(start, stop, one, 0)


COST = pl.CostEstimate(flops=1000, bytes_accessed=1000, transcendentals=0)
IN_VMEM = pl.BlockSpec(memory_space=pltpu.VMEM)
IN_HBM = pl.BlockSpec(memory_space=pl.ANY)


def low_shape(*shape):
    return jax.ShapeDtypeStruct(shape, jnp.bfloat16)


def kernel_params(collective_id, mib):
    return pltpu.CompilerParams(
        collective_id=collective_id, has_side_effects=True, vmem_limit_bytes=mib * 2**20
    )


def sum_row_kernel(n, p_ref, o_ref, *line):
    greet_row(n)
    step, drain = line_sum(n, p_ref, o_ref, *line)[:2]
    loop(0, line_steps(n, p_ref.shape[0]), step)
    drain()


def sum_row(partial_low):
    return pl.pallas_call(
        partial(sum_row_kernel, lax.axis_size("row")),
        out_shape=low_shape(*partial_low.shape),
        in_specs=[IN_VMEM],
        out_specs=IN_HBM,
        scratch_shapes=line_scratch(partial_low.shape),
        compiler_params=kernel_params(0, 16),
        cost_estimate=COST,
    )(partial_low)


TILE = 512
BLOCK = 256


def mlp_sums_kernel(
    n, spread, ctx, w_out, b_out, gain, shift, b_in, src_hbm, w_in_hbm, w_down_hbm, g_hbm,
    branch, d_normed, mlp, d_wdown, d_win, d_bin,
    p, w_in, w_down, g, normed, act, d_pre, mlp_acc, d_acc, rows_a, rows_b, stage, w_stage,
    load_sem, block_sem, mlp_sem, store_sem, *more,
):
    tokens, depth = p.shape
    units = act.shape[1]
    half = tokens // 2
    part = BLOCK // 2
    blocks = tokens // BLOCK
    per_block = part // CHUNK
    quarters = units // TILE

    def sides(j):
        low_rows = pl.ds(pl.multiple_of(j * part, part), part)
        high_rows = pl.ds(pl.multiple_of(half + j * part, part), part)
        return low_rows, high_rows

    def own(j, side=None):
        if side is None:
            return pl.ds(pl.multiple_of(j * BLOCK, BLOCK), BLOCK)
        return pl.ds(pl.multiple_of(j * BLOCK + side * part, part), part)

    lines, gather_sems = more[:12], more[12:]
    loads = []
    others = []
    if spread:
        deep, wide = w_in_hbm.shape[0], w_down_hbm.shape[1]

        def in_piece(k, place):
            size = deep // 2
            there = pl.ds(pl.multiple_of(place * deep + k * size, size), size)
            return w_in_hbm.at[pl.ds(k * size, size)], w_in.at[there]

        def down_piece(k, place):
            some = pl.ds(k * (units // 2), units // 2)
            cols = pl.ds(pl.multiple_of(place * wide, wide), wide)
            return w_down_hbm.at[some], w_down.at[some, cols]

        pieces = [partial(f, k) for f in (in_piece, down_piece) for k in range(2)]
        others, start_gather, arrive, arrive_far, finish_gather = plane_gather(
            pieces, *gather_sems
        )
    else:
        loads = [
            pltpu.make_async_copy(w_in_hbm, w_in, load_sem.at[0]),
            pltpu.make_async_copy(w_down_hbm, w_down, load_sem.at[1]),
        ]
    for j in range(blocks):
        for side, here in enumerate((j * part, half + j * part)):
            loads.append(
                pltpu.make_async_copy(
                    g_hbm.at[pl.ds(here, part)],
                    g.at[pl.ds(j * BLOCK + side * part, part)],
                    load_sem.at[2 + 2 * j + side],
                )
            )
    for load in loads:
        load.start()
    d_bin[...] = jnp.zeros_like(d_bin)
    greet_row(n, others)
    if spread:
        start_gather()
    step1, _, settle1, finish1 = line_sum(n, p, branch, *lines[:6])
    step2, drain2, _, _ = line_sum(n, p, d_normed, *lines[6:])

    def project(j):
        low_rows, high_rows = sides(j)
        both = jnp.concatenate([ctx[low_rows], ctx[high_rows]], axis=0)
        for c in range(0, depth, TILE):
            cols = slice(c, c + TILE)
            term = dot(both, w_out[:, cols], 1, 0).astype(jnp.bfloat16)
            p[low_rows, cols] = term[:part]
            p[high_rows, cols] = term[part:]
        loop(j * per_block, (j + 1) * per_block, step1)

    for j in range(blocks):
        project(j)
        if spread and j == blocks - 2:
            for k in range(len(pieces)):
                arrive(k)
    if spread:
        for k in range(len(pieces)):
            arrive_far(k)
        finish_gather()
    for load in loads:
        load.wait()

    def norm_block(j):
        loop(j * per_block, (j + 1) * per_block, settle1)
        copies = []
        for i, (src, dst) in enumerate(((branch, rows_a), (src_hbm, rows_b))):
            for side, here in enumerate(sides(j)):
                copies.append(
                    pltpu.make_async_copy(
                        src.at[here], dst.at[pl.ds(side * part, part)], block_sem.at[i, side]
                    )
                )
        for copy in copies:
            copy.start()
        for copy in copies:
            copy.wait()

        def few(k):
            here = pl.ds(pl.multiple_of(k * 64, 64), 64)
            there = pl.ds(pl.multiple_of(j * BLOCK + k * 64, 64), 64)
            source = rows_b[here].astype(jnp.float32)
            hidden = source + rows_a[here].astype(jnp.float32) + b_out[...]
            normed[there] = norm_forward(hidden, gain[...], shift[...])[0].astype(jnp.bfloat16)

        loop(0, BLOCK // 64, few)

    def mlp_out(j):
        return [
            pltpu.make_async_copy(
                stage.at[pl.ds(side * part, part)], mlp.at[here], mlp_sem.at[side]
            )
            for side, here in enumerate(sides(j))
        ]

    first = tokens // 2 // CHUNK

    def block(j):
        for q in range(quarters):
            t = first + j * per_block + q
            step1(t)
            step2(t - first - per_block)
            if q == 0:
                norm_block(j)
            units_q = slice(q * TILE, (q + 1) * TILE)
            here = own(j)
            pre = dot(normed[here], w_in[:, units_q], 1, 0) + b_in[:, units_q]
            d_act = dot(g[here], w_down[units_q], 1, 1)
            lower = 0.5 * (1.0 + lax.erf(pre * 0.5**0.5))
            act[here, units_q] = (pre * lower).astype(jnp.bfloat16)
            slope = lower + pre * (jnp.exp(-0.5 * pre * pre) * (0.5 / jnp.pi) ** 0.5)
            low_pre = (d_act * slope).astype(jnp.bfloat16)
            d_pre[here, units_q] = low_pre
            d_bin[:, units_q] += jnp.sum(low_pre.astype(jnp.float32), axis=0, keepdims=True)
            for c in range(0, depth, TILE):
                cols = slice(c, c + TILE)
                m_term = dot(act[here, units_q], w_down[units_q, cols], 1, 0)
                d_term = dot(d_pre[here, units_q], w_in[cols, units_q], 1, 1)
                if q == 0:
                    mlp_acc[:, cols] = m_term
                    d_acc[:, cols] = d_term
                elif q < quarters - 1:
                    mlp_acc[:, cols] += m_term
                    d_acc[:, cols] += d_term
                else:
                    if c == 0:

                        @pl.when(j > 0)
                        def _():
                            for copy in mlp_out(j - 1):
                                copy.wait()

                    stage[:, cols] = (mlp_acc[:, cols] + m_term).astype(jnp.bfloat16)
                    d_low = (d_acc[:, cols] + d_term).astype(jnp.bfloat16)
                    for side, rows in enumerate(sides(j)):
                        p[rows, cols] = d_low[side * part : (side + 1) * part]
        for copy in mlp_out(j):
            copy.start()

    loop(0, blocks, block)
    begin = first
    steps = line_steps(n, tokens)
    tick = tokens // 2 // CHUNK - per_block
    jobs = ((act, g, d_wdown), (normed, d_pre, d_win))
    for k, (left, right, out) in enumerate(jobs):
        across = out.shape[1] // TILE
        tiles = (out.shape[0] // TILE) * across

        def store(tile, slot):
            m = pl.ds(pl.multiple_of((tile // across) * TILE, TILE), TILE)
            c = pl.ds(pl.multiple_of(lax.rem(tile, across) * TILE, TILE), TILE)
            copy = pltpu.make_async_copy(w_stage.at[slot], out.at[m, c], store_sem.at[slot])
            return m, c, copy

        def body(u):
            step2(tick + k * (tiles // 2) + u)
            for slot in range(2):
                m, c, copy = store(2 * u + slot, slot)
                if k == 0:

                    @pl.when(u > 0)
                    def _():
                        copy.wait()
                else:
                    copy.wait()
                w_stage[slot] = dot(left[:, m], right[:, c], 0, 0).astype(jnp.bfloat16)
                copy.start()

        loop(0, tiles // 2, body)
        tick_end = tick + (k + 1) * (tiles // 2)
    if tick_end < steps:
        loop(tick_end, steps, step2)
    for slot in range(2):
        store(slot, slot)[2].wait()
    for copy in mlp_out(blocks - 1):
        copy.wait()
    finish1()
    drain2()


def mlp_sums(context, w_out, b_out, gain, shift, b_in, inputs, w_in, w_down, d_output):
    tokens, depth = inputs.shape
    units = w_in.shape[1]
    spread = w_in.shape[0] < depth
    dma = pltpu.SemaphoreType.DMA
    low_buffer = lambda *shape: pltpu.VMEM(shape, jnp.bfloat16)
    return pl.pallas_call(
        partial(mlp_sums_kernel, lax.axis_size("row"), spread),
        out_shape=[
            low_shape(tokens, depth),
            low_shape(tokens, depth),
            low_shape(tokens, depth),
            low_shape(units, depth),
            low_shape(depth, units),
            jax.ShapeDtypeStruct((1, units), jnp.float32),
        ],
        in_specs=[IN_VMEM] * 6 + [IN_HBM] * 4,
        out_specs=[IN_HBM] * 5 + [IN_VMEM],
        scratch_shapes=[
            low_buffer(tokens, depth),
            low_buffer(depth, units),
            low_buffer(units, depth),
            low_buffer(tokens, depth),
            low_buffer(tokens, depth),
            low_buffer(tokens, units),
            low_buffer(tokens, units),
            pltpu.VMEM((BLOCK, depth), jnp.float32),
            pltpu.VMEM((BLOCK, depth), jnp.float32),
            low_buffer(BLOCK, depth),
            low_buffer(BLOCK, depth),
            low_buffer(BLOCK, depth),
            low_buffer(2, TILE, TILE),
            dma((2 + 2 * (tokens // BLOCK),)),
            dma((2, 2)),
            dma((2,)),
            dma((2,)),
        ]
        + line_scratch((tokens, depth))
        + line_scratch((tokens, depth))
        + ([dma((4, 4))] * 4 + [dma((4,))] if spread else []),
        compiler_params=kernel_params(1, 61),
        cost_estimate=COST,
    )(
        context, w_out, b_out[None], gain[None], shift[None], b_in[None],
        inputs, w_in, w_down, d_output,
    )


QUERY_ROWS = 256


def block_probs(i, prefix, cols, q, k):
    start = i * QUERY_ROWS
    width = max(start + QUERY_ROWS, q.shape[0] // 2)
    here = slice(start, start + QUERY_ROWS)
    scores = dot(k[:width, cols], q[here, cols], 1, 1) * HEAD_DIM ** (-0.5)
    key = lax.broadcasted_iota(jnp.int32, scores.shape, 0)
    query = lax.broadcasted_iota(jnp.int32, scores.shape, 1) + start
    scores = jnp.where((key <= query) | (key < prefix), scores, -1000000000.0)
    expo = jnp.exp(scores - jnp.max(scores, axis=0, keepdims=True))
    return here, width, expo * (1.0 / jnp.sum(expo, axis=0, keepdims=True))


def attend_kernel(prefix_ref, projected, context):
    q, k, v = (projected.at[c] for c in range(3))
    prefix = prefix_ref[0]

    def head(h):
        cols = pl.ds(pl.multiple_of(h * HEAD_DIM, HEAD_DIM), HEAD_DIM)
        v_t = v[:, cols].T
        for i in range(q.shape[0] // QUERY_ROWS):
            here, width, probs = block_probs(i, prefix, cols, q, k)
            out = dot(v_t[:, :width], probs.astype(jnp.bfloat16), 1, 0)
            context[here, cols] = out.T.astype(jnp.bfloat16)

    loop(0, q.shape[1] // HEAD_DIM, head)


def attend(prefix_len, projected):
    return pl.pallas_call(
        attend_kernel,
        out_shape=low_shape(*projected.shape[1:]),
        in_specs=[pl.BlockSpec(memory_space=pltpu.SMEM), IN_VMEM],
        out_specs=IN_VMEM,
        compiler_params=pltpu.CompilerParams(vmem_limit_bytes=32 * 2**20),
        cost_estimate=COST,
    )(prefix_len, projected)


def attend_piece(i, prefix, cols, q, k, v, k_t, d_context, d_proj, d_key, d_value, first):
    score_scale = HEAD_DIM ** (-0.5)
    here, width, probs = block_probs(i, prefix, cols, q, k)
    q_block, g_block = q[here, cols], d_context[here, cols]
    d_probs = dot(v[:width, cols], g_block, 1, 1)
    inner = jnp.sum(d_probs * probs, axis=0, keepdims=True)
    d_scores = (probs * (d_probs - inner)).astype(jnp.bfloat16)
    d_query = dot(k_t[:, :width], d_scores, 1, 0) * score_scale
    d_proj[0, here, cols] = d_query.T.astype(jnp.bfloat16)
    for total, term in (
        (d_key, dot(d_scores, q_block, 1, 0)),
        (d_value, dot(probs.astype(jnp.bfloat16), g_block, 1, 0)),
    ):
        if first:
            total[...] = term
        else:
            total[:width] += term


def attend_sum_kernel(
    n, prefix_ref, p_ref, projected, d_context, n1_hbm, ctx_hbm, branch_hbm,
    o_ref, d_proj, d_bias, d_wqkv, d_wout,
    n1, ctx, branch, d_key, d_value, load_sem, *line,
):
    loads = [
        pltpu.make_async_copy(src, dst, load_sem.at[i])
        for i, (src, dst) in enumerate(((n1_hbm, n1), (ctx_hbm, ctx), (branch_hbm, branch)))
    ]
    for load in loads:
        load.start()
    greet_row(n)
    step, drain = line_sum(n, p_ref, o_ref, *line)[:2]
    steps = line_steps(n, p_ref.shape[0])
    prefix = prefix_ref[0]
    q, k, v = (projected.at[c] for c in range(3))
    blocks = q.shape[0] // QUERY_ROWS
    heads = q.shape[1] // HEAD_DIM

    def head(h):
        cols = pl.ds(pl.multiple_of(h * HEAD_DIM, HEAD_DIM), HEAD_DIM)
        k_t = k[:, cols].T
        for j in range(blocks):
            step(h * blocks + j)
            attend_piece(
                blocks - 1 - j, prefix, cols, q, k, v, k_t, d_context, d_proj, d_key, d_value,
                j == 0,
            )
        d_proj[1, :, cols] = (d_key[...] * HEAD_DIM ** (-0.5)).astype(jnp.bfloat16)
        d_proj[2, :, cols] = d_value[...].astype(jnp.bfloat16)
        for b, c in ((0, 0), (1, 2)):
            d_bias[b : b + 1, cols] = jnp.sum(
                d_proj[c, :, cols].astype(jnp.float32), axis=0, keepdims=True
            )

    loop(0, heads, head)
    for load in loads:
        load.wait()
    begin = heads * blocks
    tiles = n1.shape[1] // TILE

    for c in range(3):

        def body(t):
            step(t)
            m = pl.ds(pl.multiple_of((t - begin - c * tiles) * TILE, TILE), TILE)
            d_wqkv[c, m] = dot(n1[:, m], d_proj[c], 0, 0).astype(jnp.bfloat16)
            if c == 0:
                d_wout[:, m] = dot(ctx[...], branch[:, m], 0, 0).astype(jnp.bfloat16)

        loop(begin + c * tiles, begin + (c + 1) * tiles, body)
    loop(begin + 3 * tiles, steps, step)
    drain()


def attend_sum(prefix_len, partial_low, projected, d_context, normed1, context, d_branch):
    _, tokens, width = projected.shape
    depth = normed1.shape[1]
    dma = pltpu.SemaphoreType.DMA
    return pl.pallas_call(
        partial(attend_sum_kernel, lax.axis_size("row")),
        out_shape=[
            low_shape(*partial_low.shape),
            low_shape(3, tokens, width),
            jax.ShapeDtypeStruct((2, width), jnp.float32),
            low_shape(3, depth, width),
            low_shape(width, depth),
        ],
        in_specs=[pl.BlockSpec(memory_space=pltpu.SMEM)] + [IN_VMEM] * 3 + [IN_HBM] * 3,
        out_specs=[IN_HBM] + [IN_VMEM] * 4,
        scratch_shapes=[
            pltpu.VMEM((tokens, depth), jnp.bfloat16),
            pltpu.VMEM((tokens, width), jnp.bfloat16),
            pltpu.VMEM((tokens, depth), jnp.bfloat16),
            pltpu.VMEM((tokens, HEAD_DIM), jnp.float32),
            pltpu.VMEM((tokens, HEAD_DIM), jnp.float32),
            dma((3,)),
        ]
        + line_scratch(partial_low.shape),
        compiler_params=kernel_params(2, 56),
        cost_estimate=COST,
    )(prefix_len, partial_low, projected, d_context, normed1, context, d_branch)


def scatter_low(grad, dim):
    summed = lax.psum_scatter(grad, ("dp", "col"), scatter_dimension=dim, tiled=True)
    return summed.astype(jnp.float32)


def local(
    inputs,
    prefix_len,
    norm1_gain,
    norm1_shift,
    w_qkv,
    b_qv,
    w_out,
    b_out,
    norm2_gain,
    norm2_shift,
    w_in,
    b_in,
    w_down,
    b_down,
    d_output,
):
    low_mats = (
        w_qkv.astype(jnp.bfloat16),
        w_out.astype(jnp.bfloat16),
        w_in.astype(jnp.bfloat16),
        w_down.astype(jnp.bfloat16),
    )
    full_qkv, full_out, full_in, full_down = (
        lax.all_gather(low_mats[0], ("dp", "col"), axis=1, tiled=True),
        lax.all_gather(low_mats[1], ("dp", "col"), axis=1, tiled=True),
        low_mats[2],
        low_mats[3],
    )
    if (lax.axis_size("dp"), lax.axis_size("col")) != (2, 4):
        full_in = lax.all_gather(full_in, ("dp", "col"), axis=0, tiled=True)
        full_down = lax.all_gather(full_down, ("dp", "col"), axis=1, tiled=True)
    source = inputs.astype(jnp.float32)
    normed1, scaled1, inverse1 = norm_forward(source, norm1_gain, norm1_shift)
    normed1_low = normed1.astype(jnp.bfloat16)
    projected = jnp.einsum("td,cdn->ctn", normed1_low, full_qkv, preferred_element_type=jnp.float32)
    bias_rows = jnp.stack([b_qv[0], jnp.zeros_like(b_qv[0]), b_qv[1]])
    projected = (projected + bias_rows[:, None, :]).astype(jnp.bfloat16)
    context_low = attend(prefix_len, projected)
    attn_sum, summed2, mlp_partial, grad_wdown, grad_win, grad_bin = mlp_sums(
        context_low, full_out, b_out, norm2_gain, norm2_shift, b_in,
        inputs, full_in, full_down, d_output,
    )
    grad_bin = grad_bin[0]
    hidden = source + attn_sum.astype(jnp.float32) + b_out
    _, scaled2, inverse2 = norm_forward(hidden, norm2_gain, norm2_shift)
    grad_top = d_output.astype(jnp.float32)
    grad_bdown = jnp.sum(grad_top, axis=0)
    grad_normed2 = summed2.astype(jnp.float32)
    grad_gain2 = jnp.sum(grad_normed2 * scaled2, axis=0)
    grad_shift2 = jnp.sum(grad_normed2, axis=0)
    grad_hidden = grad_top + norm_backward(grad_normed2, scaled2, inverse2, norm2_gain)
    grad_branch = grad_hidden.astype(jnp.bfloat16)
    grad_bout = jnp.sum(grad_branch.astype(jnp.float32), axis=0)
    grad_context = jnp.einsum(
        "td,rd->tr", grad_branch, full_out, preferred_element_type=jnp.float32
    ).astype(jnp.bfloat16)
    mlp_sum, grad_projected, grad_bqv, grad_wqkv, grad_wout = attend_sum(
        prefix_len, mlp_partial, projected, grad_context, normed1_low, context_low, grad_branch
    )
    output = (hidden + mlp_sum.astype(jnp.float32) + b_down).astype(jnp.bfloat16)
    norm1_partial = jnp.einsum(
        "ctn,cdn->td", grad_projected, full_qkv, preferred_element_type=jnp.float32
    )
    sent_win = scatter_low(grad_win, 0)
    sent_wdown = scatter_low(grad_wdown, 1)
    norm1_low = norm1_partial.astype(jnp.bfloat16)
    grad_wqkv, grad_wout, sent_win, sent_wdown = lax.optimization_barrier(
        (grad_wqkv, grad_wout, sent_win, sent_wdown)
    )
    sent_wout, sent_wqkv = scatter_low(grad_wout, 1), scatter_low(grad_wqkv, 1)
    grad_normed1 = sum_row(norm1_low).astype(jnp.float32)
    grad_gain1 = jnp.sum(grad_normed1 * scaled1, axis=0)
    grad_shift1 = jnp.sum(grad_normed1, axis=0)
    d_inputs = grad_hidden + norm_backward(grad_normed1, scaled1, inverse1, norm1_gain)
    small = lax.psum(
        (
            grad_gain1,
            grad_shift1,
            grad_bqv,
            grad_bout,
            grad_gain2,
            grad_shift2,
            grad_bin,
            grad_bdown,
        ),
        ("dp", "col"),
    )
    return (
        output,
        d_inputs,
        small[0],
        small[1],
        sent_wqkv,
        small[2],
        sent_wout,
        small[3],
        small[4],
        small[5],
        sent_win,
        small[6],
        sent_wdown,
        small[7],
    )


def solution(mesh):
    return jax.shard_map(
        local,
        mesh=mesh,
        in_specs=(
            P(("dp", "col"), None),
            P(("dp", "col")),
            P(),
            P(),
            P(None, ("dp", "col"), "row"),
            P(None, "row"),
            P("row", ("dp", "col")),
            P(),
            P(),
            P(),
            P(("dp", "col"), "row"),
            P("row"),
            P("row", ("dp", "col")),
            P(),
            P(("dp", "col"), None),
        ),
        out_specs=(
            P(("dp", "col"), None),
            P(("dp", "col"), None),
            P(),
            P(),
            P(None, ("dp", "col"), "row"),
            P(None, "row"),
            P("row", ("dp", "col")),
            P(),
            P(),
            P(),
            P(("dp", "col"), "row"),
            P("row"),
            P("row", ("dp", "col")),
            P(),
        ),
        check_vma=False,
    )
```

```python
from functools import partial

import jax
import jax.numpy as jnp
from jax import lax
from jax.experimental import pallas as pl
from jax.experimental.pallas import tpu as pltpu
from jax.sharding import PartitionSpec as P

HEAD_DIM = 128
MESH_IDS = pl.DeviceIdType.MESH
CHUNK = 32
LAG = 2


eps_norm = 1e-05


def norm_forward(values, norm_gain, norm_shift):
    average = jnp.mean(values, axis=-1, keepdims=True)
    centered = values - average
    variance = jnp.mean(centered * centered, axis=-1, keepdims=True)
    inverse = lax.rsqrt(variance + eps_norm)
    scaled = centered * inverse
    return (scaled * norm_gain + norm_shift, scaled, inverse)


def norm_backward(grad, scaled, inverse, norm_gain):
    grad_scaled = grad * norm_gain
    return inverse * (
        grad_scaled
        - jnp.mean(grad_scaled, axis=-1, keepdims=True)
        - scaled * jnp.mean(grad_scaled * scaled, axis=-1, keepdims=True)
    )


def dot(left, right, left_dim, right_dim):
    return lax.dot_general(
        left, right, (((left_dim,), (right_dim,)), ((), ())), preferred_element_type=jnp.float32
    )


def greet_row(n, others=()):
    r = lax.axis_index("row")
    last = n - 1
    bar = pltpu.get_barrier_semaphore()
    for cond, dev in ((r > 0, r - 1), (r < last, r + 1)):

        @pl.when(cond)
        def _():
            pl.semaphore_signal(bar, inc=1, device_id={"row": dev}, device_id_type=MESH_IDS)

    for other in others:
        pl.semaphore_signal(bar, inc=1, device_id=other, device_id_type=MESH_IDS)
    inside = (r > 0) & (r < last)

    @pl.when(inside)
    def _():
        pl.semaphore_wait(bar, 2 + len(others))

    @pl.when(jnp.logical_not(inside))
    def _():
        pl.semaphore_wait(bar, 1 + len(others))


def plane_partners():
    y, x = lax.axis_index("dp"), lax.axis_index("col")
    far_x, near = lax.rem(x + 2, 4), x + 1 - 2 * lax.rem(x, 2)
    far_near = lax.rem(near + 2, 4)
    ids = {"x": {"col": far_x}, "y": {"dp": 1 - y}, "near": {"col": near}}
    mine = {"own": y * 4 + x, "x": y * 4 + far_x, "y": (1 - y) * 4 + x, "xy": (1 - y) * 4 + far_x}
    theirs = {
        "own": y * 4 + near,
        "x": y * 4 + far_near,
        "y": (1 - y) * 4 + near,
        "xy": (1 - y) * 4 + far_near,
    }
    return ids, mine, theirs


KINDS = ("own", "x", "y", "xy")


def plane_gather(pieces, send_sem, recv_sem, near_send, near_recv, local_sem):
    ids, mine, theirs = plane_partners()
    count = len(pieces)

    def remote(kind, k, to, src, dst):
        row = KINDS.index(kind)
        near = to == "near"
        return pltpu.make_async_remote_copy(
            src_ref=src,
            dst_ref=dst,
            send_sem=(near_send if near else send_sem).at[row, k],
            recv_sem=(near_recv if near else recv_sem).at[row, k],
            device_id=ids[to],
            device_id_type=MESH_IDS,
        )

    def outgoing(k):
        own, place = pieces[k](mine["own"])
        return [remote("x", k, "x", own, place), remote("y", k, "y", own, place)]

    def local(k):
        own, place = pieces[k](mine["own"])
        return pltpu.make_async_copy(own, place, local_sem.at[k])

    def onward(k):
        kind, to = ("x", "y") if k % 2 == 0 else ("y", "x")
        place = pieces[k](mine[kind])[1]
        return remote("xy", k, to, place, place)

    def share(kind, k):
        own, place = pieces[k](mine[kind])
        return remote(kind, k, "near", own if kind == "own" else place, place)

    def start():
        for k in range(count):
            for copy in outgoing(k):
                copy.start()
        for k in range(count):
            share("own", k).start()
            local(k).start()

    def arrive(k):
        for copy in outgoing(k):
            copy.wait_recv()
        onward(k).start()
        share("x", k).start()
        share("y", k).start()

    def arrive_far(k):
        onward(k).wait_recv()
        share("xy", k).start()

    def finish():
        for k in range(count):
            local(k).wait()
            for copy in outgoing(k):
                copy.wait_send()
            onward(k).wait_send()
            for kind in KINDS:
                place = pieces[k](theirs[kind])[1]
                share(kind, k).wait_send()
                remote(kind, k, "near", place, place).wait_recv()

    return list(ids.values()), start, arrive, arrive_far, finish


def line_sum(n, p_ref, o_ref, held, rs_s, rs_r, ag_s, ag_r, loc):
    half = o_ref.shape[0] // 2
    chunks = held.shape[0] // 2 // CHUNK
    r = lax.axis_index("row")
    last = n - 1
    place = (r, last - r)
    after = (jnp.minimum(r + 1, last), jnp.maximum(r - 1, 0))
    before = (jnp.maximum(r - 1, 0), jnp.minimum(r + 1, last))

    def rows(d, c):
        return pl.ds(pl.multiple_of((half if d == 0 else 0) + c * CHUNK, CHUNK), CHUNK)

    def slot(d, c):
        return pl.ds(pl.multiple_of((1 - d) * chunks * CHUNK + c * CHUNK, CHUNK), CHUNK)


    def onward(d, c, src):
        return pltpu.make_async_remote_copy(
            src_ref=src.at[rows(d, c) if src is p_ref else slot(d, c)],
            dst_ref=held.at[slot(d, c)],
            send_sem=rs_s.at[d, c],
            recv_sem=rs_r.at[d, c],
            device_id={"row": after[d]},
            device_id_type=MESH_IDS,
        )

    def back(d, c, src):
        return pltpu.make_async_remote_copy(
            src_ref=src.at[slot(d, c) if src is held else rows(d, c)],
            dst_ref=o_ref.at[rows(d, c)],
            send_sem=ag_s.at[d, c],
            recv_sem=ag_r.at[d, c],
            device_id={"row": before[d]},
            device_id_type=MESH_IDS,
        )

    def keep(d, c):
        return pltpu.make_async_copy(held.at[slot(d, c)], o_ref.at[rows(d, c)], loc.at[c])

    def step(t):
        for d in (0, 1):

            @pl.when((place[d] == 0) & (t >= 0) & (t < chunks))
            def _():
                onward(d, t, p_ref).start()

            c = t - LAG * place[d]

            @pl.when((place[d] > 0) & (c >= 0) & (c < chunks))
            def _():
                onward(d, c, p_ref).wait_recv()
                here = slot(d, c)
                held[here] = (
                    held[here].astype(jnp.float32) + p_ref[rows(d, c)].astype(jnp.float32)
                ).astype(jnp.bfloat16)

                @pl.when(place[d] < last)
                def _():
                    onward(d, c, held).start()

                @pl.when(place[d] == last)
                def _():
                    back(d, c, held).start()
                    keep(d, c).start()

        for d in (0, 1):
            c = t - LAG * (2 * last - place[d])

            @pl.when((place[d] < last) & (c >= 0) & (c < chunks))
            def _():
                back(d, c, o_ref).wait_recv()

                @pl.when(place[d] > 0)
                def _():
                    back(d, c, o_ref).start()

    def settle(c):
        for d in (0, 1):

            @pl.when(place[d] < last)
            def _():
                onward(d, c, p_ref).wait_send()

            @pl.when(place[d] == last)
            def _():
                keep(d, c).wait()

    def finish(c):
        for d in (0, 1):

            @pl.when(place[d] > 0)
            def _():
                back(d, c, o_ref).wait_send()

    def drain():
        def both(c):
            settle(c)
            finish(c)

        loop(0, chunks, both)

    return step, drain, settle, lambda: loop(0, chunks, finish)


def line_steps(n, total_rows):
    return total_rows // 2 // CHUNK + LAG * 2 * (n - 1)


def line_scratch(shape):
    chunks = shape[0] // 2 // CHUNK
    dma = pltpu.SemaphoreType.DMA
    return [
        pltpu.VMEM(shape, jnp.bfloat16),
        dma((2, chunks)),
        dma((2, chunks)),
        dma((2, chunks)),
        dma((2, chunks)),
        dma((chunks,)),
    ]


def loop(start, stop, body):
    def one(t, carry):
        body(t)
        return carry

    lax.fori_loop(start, stop, one, 0)


COST = pl.CostEstimate(flops=1000, bytes_accessed=1000, transcendentals=0)
IN_VMEM = pl.BlockSpec(memory_space=pltpu.VMEM)
IN_HBM = pl.BlockSpec(memory_space=pl.ANY)


def low_shape(*shape):
    return jax.ShapeDtypeStruct(shape, jnp.bfloat16)


def kernel_params(collective_id, mib):
    return pltpu.CompilerParams(
        collective_id=collective_id, has_side_effects=True, vmem_limit_bytes=mib * 2**20
    )


TILE = 512
BLOCK = 256


def mlp_sums_kernel(
    n, spread, ctx, w_out, b_out, gain, shift, b_in, src_hbm, w_in_hbm, w_down_hbm, g_hbm,
    branch, d_normed, mlp, d_wdown, d_win, d_bin,
    p, w_in, w_down, g, normed, act, d_pre, mlp_acc, d_acc, rows_a, rows_b, stage, w_stage,
    load_sem, block_sem, mlp_sem, store_sem, *more,
):
    tokens, depth = p.shape
    units = act.shape[1]
    half = tokens // 2
    part = BLOCK // 2
    blocks = tokens // BLOCK
    per_block = part // CHUNK
    quarters = units // TILE

    def sides(j):
        low_rows = pl.ds(pl.multiple_of(j * part, part), part)
        high_rows = pl.ds(pl.multiple_of(half + j * part, part), part)
        return low_rows, high_rows

    def own(j, side=None):
        if side is None:
            return pl.ds(pl.multiple_of(j * BLOCK, BLOCK), BLOCK)
        return pl.ds(pl.multiple_of(j * BLOCK + side * part, part), part)

    lines, gather_sems = more[:12], more[12:]
    loads = []
    others = []
    if spread:
        deep, wide = w_in_hbm.shape[0], w_down_hbm.shape[1]

        def in_piece(k, place):
            size = deep // 2
            there = pl.ds(pl.multiple_of(place * deep + k * size, size), size)
            return w_in_hbm.at[pl.ds(k * size, size)], w_in.at[there]

        def down_piece(k, place):
            some = pl.ds(k * (units // 2), units // 2)
            cols = pl.ds(pl.multiple_of(place * wide, wide), wide)
            return w_down_hbm.at[some], w_down.at[some, cols]

        pieces = [partial(f, k) for f in (in_piece, down_piece) for k in range(2)]
        others, start_gather, arrive, arrive_far, finish_gather = plane_gather(
            pieces, *gather_sems
        )
    else:
        loads = [
            pltpu.make_async_copy(w_in_hbm, w_in, load_sem.at[0]),
            pltpu.make_async_copy(w_down_hbm, w_down, load_sem.at[1]),
        ]
    for j in range(blocks):
        for side, here in enumerate((j * part, half + j * part)):
            loads.append(
                pltpu.make_async_copy(
                    g_hbm.at[pl.ds(here, part)],
                    g.at[pl.ds(j * BLOCK + side * part, part)],
                    load_sem.at[2 + 2 * j + side],
                )
            )
    for load in loads:
        load.start()
    d_bin[...] = jnp.zeros_like(d_bin)
    greet_row(n, others)
    if spread:
        start_gather()
    step1, _, settle1, finish1 = line_sum(n, p, branch, *lines[:6])
    step2, drain2, _, _ = line_sum(n, p, d_normed, *lines[6:])

    def project(j):
        low_rows, high_rows = sides(j)
        both = jnp.concatenate([ctx[low_rows], ctx[high_rows]], axis=0)
        for c in range(0, depth, TILE):
            cols = slice(c, c + TILE)
            term = dot(both, w_out[:, cols], 1, 0).astype(jnp.bfloat16)
            p[low_rows, cols] = term[:part]
            p[high_rows, cols] = term[part:]
        loop(j * per_block, (j + 1) * per_block, step1)

    for j in range(blocks):
        project(j)
        if spread and j == blocks - 2:
            for k in range(len(pieces)):
                arrive(k)
    if spread:
        for k in range(len(pieces)):
            arrive_far(k)
        finish_gather()
    for load in loads:
        load.wait()

    def norm_block(j):
        loop(j * per_block, (j + 1) * per_block, settle1)
        copies = []
        for i, (src, dst) in enumerate(((branch, rows_a), (src_hbm, rows_b))):
            for side, here in enumerate(sides(j)):
                copies.append(
                    pltpu.make_async_copy(
                        src.at[here], dst.at[pl.ds(side * part, part)], block_sem.at[i, side]
                    )
                )
        for copy in copies:
            copy.start()
        for copy in copies:
            copy.wait()

        def few(k):
            here = pl.ds(pl.multiple_of(k * 64, 64), 64)
            there = pl.ds(pl.multiple_of(j * BLOCK + k * 64, 64), 64)
            source = rows_b[here].astype(jnp.float32)
            hidden = source + rows_a[here].astype(jnp.float32) + b_out[...]
            normed[there] = norm_forward(hidden, gain[...], shift[...])[0].astype(jnp.bfloat16)

        loop(0, BLOCK // 64, few)

    def mlp_out(j):
        return [
            pltpu.make_async_copy(
                stage.at[pl.ds(side * part, part)], mlp.at[here], mlp_sem.at[side]
            )
            for side, here in enumerate(sides(j))
        ]

    first = tokens // 2 // CHUNK

    def block(j):
        for q in range(quarters):
            t = first + j * per_block + q
            step1(t)
            step2(t - first - per_block)
            if q == 0:
                norm_block(j)
            units_q = slice(q * TILE, (q + 1) * TILE)
            here = own(j)
            pre = dot(normed[here], w_in[:, units_q], 1, 0) + b_in[:, units_q]
            d_act = dot(g[here], w_down[units_q], 1, 1)
            lower = 0.5 * (1.0 + lax.erf(pre * 0.5**0.5))
            act[here, units_q] = (pre * lower).astype(jnp.bfloat16)
            slope = lower + pre * (jnp.exp(-0.5 * pre * pre) * (0.5 / jnp.pi) ** 0.5)
            low_pre = (d_act * slope).astype(jnp.bfloat16)
            d_pre[here, units_q] = low_pre
            d_bin[:, units_q] += jnp.sum(low_pre.astype(jnp.float32), axis=0, keepdims=True)
            for c in range(0, depth, TILE):
                cols = slice(c, c + TILE)
                m_term = dot(act[here, units_q], w_down[units_q, cols], 1, 0)
                d_term = dot(d_pre[here, units_q], w_in[cols, units_q], 1, 1)
                if q == 0:
                    mlp_acc[:, cols] = m_term
                    d_acc[:, cols] = d_term
                elif q < quarters - 1:
                    mlp_acc[:, cols] += m_term
                    d_acc[:, cols] += d_term
                else:
                    if c == 0:

                        @pl.when(j > 0)
                        def _():
                            for copy in mlp_out(j - 1):
                                copy.wait()

                    stage[:, cols] = (mlp_acc[:, cols] + m_term).astype(jnp.bfloat16)
                    d_low = (d_acc[:, cols] + d_term).astype(jnp.bfloat16)
                    for side, rows in enumerate(sides(j)):
                        p[rows, cols] = d_low[side * part : (side + 1) * part]
        for copy in mlp_out(j):
            copy.start()

    loop(0, blocks, block)
    begin = first
    steps = line_steps(n, tokens)
    tick = tokens // 2 // CHUNK - per_block
    jobs = ((act, g, d_wdown), (normed, d_pre, d_win))
    for k, (left, right, out) in enumerate(jobs):
        across = out.shape[1] // TILE
        tiles = (out.shape[0] // TILE) * across

        def store(tile, slot):
            m = pl.ds(pl.multiple_of((tile // across) * TILE, TILE), TILE)
            c = pl.ds(pl.multiple_of(lax.rem(tile, across) * TILE, TILE), TILE)
            copy = pltpu.make_async_copy(w_stage.at[slot], out.at[m, c], store_sem.at[slot])
            return m, c, copy

        def body(u):
            step2(tick + k * (tiles // 2) + u)
            for slot in range(2):
                m, c, copy = store(2 * u + slot, slot)
                if k == 0:

                    @pl.when(u > 0)
                    def _():
                        copy.wait()
                else:
                    copy.wait()
                w_stage[slot] = dot(left[:, m], right[:, c], 0, 0).astype(jnp.bfloat16)
                copy.start()

        loop(0, tiles // 2, body)
        tick_end = tick + (k + 1) * (tiles // 2)
    if tick_end < steps:
        loop(tick_end, steps, step2)
    for slot in range(2):
        store(slot, slot)[2].wait()
    for copy in mlp_out(blocks - 1):
        copy.wait()
    finish1()
    drain2()


def mlp_sums(context, w_out, b_out, gain, shift, b_in, inputs, w_in, w_down, d_output):
    tokens, depth = inputs.shape
    units = w_in.shape[1]
    spread = w_in.shape[0] < depth
    dma = pltpu.SemaphoreType.DMA
    low_buffer = lambda *shape: pltpu.VMEM(shape, jnp.bfloat16)
    return pl.pallas_call(
        partial(mlp_sums_kernel, lax.axis_size("row"), spread),
        out_shape=[
            low_shape(tokens, depth),
            low_shape(tokens, depth),
            low_shape(tokens, depth),
            low_shape(units, depth),
            low_shape(depth, units),
            jax.ShapeDtypeStruct((1, units), jnp.float32),
        ],
        in_specs=[IN_VMEM] * 6 + [IN_HBM] * 4,
        out_specs=[IN_HBM] * 5 + [IN_VMEM],
        scratch_shapes=[
            low_buffer(tokens, depth),
            low_buffer(depth, units),
            low_buffer(units, depth),
            low_buffer(tokens, depth),
            low_buffer(tokens, depth),
            low_buffer(tokens, units),
            low_buffer(tokens, units),
            pltpu.VMEM((BLOCK, depth), jnp.float32),
            pltpu.VMEM((BLOCK, depth), jnp.float32),
            low_buffer(BLOCK, depth),
            low_buffer(BLOCK, depth),
            low_buffer(BLOCK, depth),
            low_buffer(2, TILE, TILE),
            dma((2 + 2 * (tokens // BLOCK),)),
            dma((2, 2)),
            dma((2,)),
            dma((2,)),
        ]
        + line_scratch((tokens, depth))
        + line_scratch((tokens, depth))
        + ([dma((4, 4))] * 4 + [dma((4,))] if spread else []),
        compiler_params=kernel_params(1, 61),
        cost_estimate=COST,
    )(
        context, w_out, b_out[None], gain[None], shift[None], b_in[None],
        inputs, w_in, w_down, d_output,
    )


QUERY_ROWS = 256


def block_probs(i, prefix, cols, q, k):
    start = i * QUERY_ROWS
    width = max(start + QUERY_ROWS, q.shape[0] // 2)
    here = slice(start, start + QUERY_ROWS)
    scores = dot(k[:width, cols], q[here, cols], 1, 1) * HEAD_DIM ** (-0.5)
    key = lax.broadcasted_iota(jnp.int32, scores.shape, 0)
    query = lax.broadcasted_iota(jnp.int32, scores.shape, 1) + start
    scores = jnp.where((key <= query) | (key < prefix), scores, -1000000000.0)
    expo = jnp.exp(scores - jnp.max(scores, axis=0, keepdims=True))
    return here, width, expo * (1.0 / jnp.sum(expo, axis=0, keepdims=True))


def attend_kernel(prefix_ref, projected, context):
    q, k, v = (projected.at[c] for c in range(3))
    prefix = prefix_ref[0]

    def head(h):
        cols = pl.ds(pl.multiple_of(h * HEAD_DIM, HEAD_DIM), HEAD_DIM)
        v_t = v[:, cols].T
        for i in range(q.shape[0] // QUERY_ROWS):
            here, width, probs = block_probs(i, prefix, cols, q, k)
            out = dot(v_t[:, :width], probs.astype(jnp.bfloat16), 1, 0)
            context[here, cols] = out.T.astype(jnp.bfloat16)

    loop(0, q.shape[1] // HEAD_DIM, head)


def attend(prefix_len, projected):
    return pl.pallas_call(
        attend_kernel,
        out_shape=low_shape(*projected.shape[1:]),
        in_specs=[pl.BlockSpec(memory_space=pltpu.SMEM), IN_VMEM],
        out_specs=IN_VMEM,
        compiler_params=pltpu.CompilerParams(vmem_limit_bytes=32 * 2**20),
        cost_estimate=COST,
    )(prefix_len, projected)


def attend_piece(i, prefix, cols, q, k, v, k_t, d_context, d_proj, d_key, d_value, first):
    score_scale = HEAD_DIM ** (-0.5)
    here, width, probs = block_probs(i, prefix, cols, q, k)
    q_block, g_block = q[here, cols], d_context[here, cols]
    d_probs = dot(v[:width, cols], g_block, 1, 1)
    inner = jnp.sum(d_probs * probs, axis=0, keepdims=True)
    d_scores = (probs * (d_probs - inner)).astype(jnp.bfloat16)
    d_query = dot(k_t[:, :width], d_scores, 1, 0) * score_scale
    d_proj[0, here, cols] = d_query.T.astype(jnp.bfloat16)
    for total, term in (
        (d_key, dot(d_scores, q_block, 1, 0)),
        (d_value, dot(probs.astype(jnp.bfloat16), g_block, 1, 0)),
    ):
        if first:
            total[...] = term
        else:
            total[:width] += term


def plane_scatter(pieces, sems):
    ids, mine, theirs = plane_partners()
    near_send, near_recv, far_send, far_recv, last_send, last_recv, load_sem = sems
    count = len(pieces)

    def remote(src, dst, send, recv, to):
        return pltpu.make_async_remote_copy(
            src_ref=src,
            dst_ref=dst,
            send_sem=send,
            recv_sem=recv,
            device_id=ids[to],
            device_id_type=MESH_IDS,
        )

    def near(i, k):
        block, to, _, _, _ = pieces[k]
        place = theirs[KINDS[i]]
        return remote(block(place), to(i), near_send.at[i, k], near_recv.at[i, k], "near")

    def load(i, k):
        block, _, own, _, _ = pieces[k]
        return pltpu.make_async_copy(block(mine[KINDS[i]]), own(i), load_sem.at[i, k])

    def far(k):
        _, _, own, to, _ = pieces[k]
        return remote(own(3), to(), far_send.at[k], far_recv.at[k], "x" if k % 2 == 0 else "y")

    def last(i, k):
        _, _, own, _, to = pieces[k]
        return remote(
            own(i), to(i - 1), last_send.at[i - 1, k], last_recv.at[i - 1, k], KINDS[i]
        )

    def add(target, term):
        flat = target.shape[0]

        def some(r):
            here = pl.ds(pl.multiple_of(r * 128, 128), 128)
            target[here] = (
                target[here].astype(jnp.float32) + term[here].astype(jnp.float32)
            ).astype(jnp.bfloat16)

        loop(0, flat // 128, some)

    def start():
        for i in (3, 1, 2, 0):
            for k in range(count):
                near(i, k).start()
                load(i, k).start()

    def pair():
        for i in (3, 1, 2, 0):
            for k in range(count):
                near(i, k).wait_recv()
                load(i, k).wait()
                add(pieces[k][2](i), pieces[k][1](i))
                if i == 3:
                    far(k).start()
                elif i == 1 + k % 2:
                    last(i, k).start()

    def cross():
        for k in range(count):
            far(k).wait_recv()
            i = 2 - k % 2
            add(pieces[k][2](i), pieces[k][3]())
            last(i, k).start()

    def collect(k):
        for i in (1, 2):
            last(i, k).wait_recv()
        return pieces[k][2](0), pieces[k][4](0), pieces[k][4](1)

    def finish():
        for k in range(count):
            for i in range(4):
                near(i, k).wait_send()
            far(k).wait_send()
            for i in (1, 2):
                last(i, k).wait_send()

    return start, pair, cross, collect, finish


def sums_out(kind, vectors, slots, send_sem, recv_sem):
    ids = plane_partners()[0]

    def copy(i):
        return pltpu.make_async_remote_copy(
            src_ref=vectors,
            dst_ref=slots.at[i],
            send_sem=send_sem.at[kind, i],
            recv_sem=recv_sem.at[kind, i],
            device_id=ids[("near", "x", "y")[i]],
            device_id_type=MESH_IDS,
        )

    def begin(i):
        copy(i).start()

    def end(i):
        copy(i).wait()
        vectors[...] += slots[i]

    return begin, end


SLICE = 64
RING = 4


def backward_kernel(
    n, spread, prefix_ref, projected, d_bin, b_out, gain1, gain2,
    mlp_hbm, n1_hbm, ctx_hbm, w_qkv_hbm, w_out_hbm, src_hbm, attn_hbm, g_hbm, dn2_hbm,
    mlp_sum, d_inputs, d_hidden, d_wqkv, d_wout, sum_wqkv, sum_wout, early, late,
    p, d_context, n1, ctx, branch, d_key, d_value, d_proj, w_stage, total, weights, ring,
    p_sem, slice_sem, load_sem, store_sem, ring_in, ring_out, *more,
):
    lines, more = more[:12], more[12:]
    tokens, depth = p.shape
    width = projected.shape[2]
    half = tokens // 2
    chunks = half // CHUNK
    blocks = tokens // BLOCK
    part = BLOCK // 2
    per_block = part // CHUNK
    travel = LAG * 2 * (n - 1)
    prefix = prefix_ref[0]

    def sides(j, size):
        return (
            pl.ds(pl.multiple_of(j * size, size), size),
            pl.ds(pl.multiple_of(half + j * size, size), size),
        )

    p_loads = [
        [
            pltpu.make_async_copy(mlp_hbm.at[rows], p.at[rows], p_sem.at[side, j])
            for side, rows in enumerate((pl.ds(j * part, part), pl.ds(half + j * part, part)))
        ]
        for j in range(blocks)
    ]
    for loads in p_loads:
        for load in loads:
            load.start()
    w_out_load = pltpu.make_async_copy(w_out_hbm, total.at[pl.ds(0, width)], load_sem.at[0])
    w_out_load.start()
    loads = [
        pltpu.make_async_copy(src, dst, load_sem.at[1 + i])
        for i, (src, dst) in enumerate(
            ((n1_hbm, n1), (ctx_hbm, ctx), (w_qkv_hbm, weights), (src_hbm, n1))
        )
    ]
    early[...] = jnp.zeros_like(early)
    late[...] = jnp.zeros_like(late)
    early[4:5] = d_bin[...]
    others = []
    if spread:
        slots_e, slots_l, small_s, small_r = more[:4]
        qkv_near, qkv_own, qkv_far, qkv_last, out_near, out_own, out_far, out_last = more[4:12]
        qkv_sum, out_sum, sum_sem = more[12:15]
        others = list(plane_partners()[0].values())
        early_begin, early_end = sums_out(0, early, slots_e, small_s, small_r)
        late_begin, late_end = sums_out(1, late, slots_l, small_s, small_r)
        places = 8
        deep, wide = depth // places, depth // places
        size = deep // 2
        tall = width // 2

        def qkv_piece(c, k):
            def block(place):
                there = pl.ds(pl.multiple_of(place * deep + k * size, size), size)
                return d_wqkv.at[c, there]

            some = pl.ds(k * size, size)
            return (
                block,
                lambda i: qkv_near.at[i, c, some],
                lambda i: qkv_own.at[i, c, some],
                lambda: qkv_far.at[c, some],
                lambda i: qkv_last.at[i, c, some],
            )

        def out_piece(k):
            some = pl.ds(k * tall, tall)

            def block(place):
                cols = pl.ds(pl.multiple_of(place * wide, wide), wide)
                return d_wout.at[some, cols]

            return (
                block,
                lambda i: out_near.at[i, some],
                lambda i: out_own.at[i, some],
                lambda: out_far.at[some],
                lambda i: out_last.at[i, some],
            )

        pieces = [qkv_piece(c, k) for c in range(3) for k in range(2)]
        pieces += [out_piece(k) for k in range(2)]
        start_scatter, pair, cross, collect, finish_scatter = plane_scatter(pieces, more[15:])
        stores = [
            pltpu.make_async_copy(qkv_sum, sum_wqkv, sum_sem.at[0]),
            pltpu.make_async_copy(out_sum, sum_wout, sum_sem.at[1]),
        ]

        def total_of(k):
            own, one, two = collect(k)
            if k < 6:
                target = qkv_sum.at[k // 2, pl.ds((k % 2) * size, size)]
            else:
                target = out_sum.at[pl.ds((k % 2) * tall, tall)]

            def some(r):
                here = pl.ds(pl.multiple_of(r * 128, 128), 128)
                target[here] = (
                    own[here].astype(jnp.float32)
                    + one[here].astype(jnp.float32)
                    + two[here].astype(jnp.float32)
                )

            loop(0, target.shape[0] // 128, some)

    greet_row(n, others)
    step1, _, settle1, finish1 = line_sum(n, p, mlp_sum, *lines[:6])
    step2, _, settle2, finish2 = line_sum(n, p, total, *lines[6:])

    def both_steps(t):
        step1(t)
        step2(t - chunks)

    slices = tokens // SLICE

    def slice_rows(k):
        return pl.ds(pl.multiple_of(k * SLICE, SLICE), SLICE)

    def slice_slot(k, i):
        return pl.ds(pl.multiple_of(half + (lax.rem(k, 2) * 4 + i) * SLICE, SLICE), SLICE)

    def slice_loads(k):
        return [
            pltpu.make_async_copy(
                src.at[slice_rows(k)], total.at[slice_slot(k, i)], slice_sem.at[lax.rem(k, 2), i]
            )
            for i, src in enumerate((dn2_hbm, attn_hbm, src_hbm, g_hbm))
        ]

    def hidden_store(k):
        return pltpu.make_async_copy(
            ring.at[lax.rem(k, RING)], d_hidden.at[slice_rows(k)], ring_out.at[lax.rem(k, RING), 0]
        )

    def norm_slice(k):
        @pl.when(k + 1 < slices)
        def _():
            for load in slice_loads(k + 1):
                load.start()

        for load in slice_loads(k):
            load.wait()

        @pl.when(k >= RING)
        def _():
            hidden_store(k - RING).wait()

        dn, attn, source, g = (total[slice_slot(k, i)].astype(jnp.float32) for i in range(4))
        _, scaled, inverse = norm_forward(source + attn + b_out[...], 1.0, 0.0)
        grad = g + norm_backward(dn, scaled, inverse, gain2[...])
        low = grad.astype(jnp.bfloat16)
        branch[slice_rows(k)] = low
        for i, term in enumerate((low.astype(jnp.float32), dn * scaled, dn, g)):
            early[i : i + 1] += jnp.sum(term, axis=0, keepdims=True)
        ring[lax.rem(k, RING)] = grad
        hidden_store(k).start()

    for load in slice_loads(0):
        load.start()
    norm_ticks = 4
    for load in p_loads[0]:
        load.wait()

    def norm_tick(t):
        step1(t)
        loop(t * (slices // norm_ticks), (t + 1) * (slices // norm_ticks), norm_slice)

    loop(0, norm_ticks, norm_tick)
    for k in range(slices - RING, slices):
        hidden_store(k).wait()
    for some in p_loads[1:]:
        for load in some:
            load.wait()
    for load in loads[:3]:
        load.start()
    w_out_load.wait()

    def context_rows(i):
        rows = pl.ds(pl.multiple_of(i * BLOCK, BLOCK), BLOCK)
        d_context[rows] = dot(branch[rows], total[:width], 1, 1).astype(jnp.bfloat16)

    loop(0, tokens // BLOCK, context_rows)

    q, k, v = (projected.at[c] for c in range(3))
    q_blocks = tokens // QUERY_ROWS
    heads = width // HEAD_DIM
    head_ticks = q_blocks // 2

    def head(h):
        cols = pl.ds(pl.multiple_of(h * HEAD_DIM, HEAD_DIM), HEAD_DIM)
        k_t = k[:, cols].T
        for j in range(q_blocks):
            if j % 2 == 0:
                step1(norm_ticks + h * head_ticks + j // 2)
            attend_piece(
                q_blocks - 1 - j, prefix, cols, q, k, v, k_t, d_context, d_proj, d_key, d_value,
                j == 0,
            )
        d_proj[1, :, cols] = (d_key[...] * HEAD_DIM ** (-0.5)).astype(jnp.bfloat16)
        d_proj[2, :, cols] = d_value[...].astype(jnp.bfloat16)

    loop(0, heads, head)
    for b, c in ((0, 0), (1, 2)):
        early[5:6, b * width : (b + 1) * width] = jnp.sum(
            d_proj[c].astype(jnp.float32), axis=0, keepdims=True
        )
    for load in loads[:3]:
        load.wait()
    tick = norm_ticks + heads * head_ticks
    tiles = depth // TILE

    def tile_store(c, m):
        some = pl.ds(m * TILE, TILE)
        out = d_wqkv.at[c, some] if c < 3 else d_wout.at[:, some]
        return pltpu.make_async_copy(w_stage.at[m % 2], out, store_sem.at[m % 2])

    for c in range(4):
        step1(tick + c)
        for m in range(tiles):
            some = slice(m * TILE, (m + 1) * TILE)
            if c or m > 1:
                before = (c, m - 2) if m > 1 else (c - 1, tiles + m - 2)
                tile_store(*before).wait()
            if c < 3:
                term = dot(n1[:, some], d_proj[c], 0, 0)
            else:
                term = dot(ctx[...], branch[:, some], 0, 0)
            w_stage[m % 2] = term.astype(jnp.bfloat16)
            tile_store(c, m).start()
    for m in (tiles - 2, tiles - 1):
        tile_store(3, m).wait()
    loads[3].start()
    if tick + 4 < chunks:
        loop(tick + 4, chunks, step1)
    if spread:
        start_scatter()

    def gradient(j):
        loop(j * per_block, (j + 1) * per_block, settle1)
        low_rows, high_rows = sides(j, part)
        rows = [
            jnp.concatenate([d_proj[c, low_rows], d_proj[c, high_rows]], axis=0) for c in range(3)
        ]
        for i in range(0, depth, TILE):
            cols = slice(i, i + TILE)
            term = dot(rows[0], weights[0, cols], 1, 1)
            for c in (1, 2):
                term += dot(rows[c], weights[c, cols], 1, 1)
            term = term.astype(jnp.bfloat16)
            p[low_rows, cols] = term[:part]
            p[high_rows, cols] = term[part:]

    def hidden_loads(c):
        return [
            pltpu.make_async_copy(
                d_hidden.at[rows],
                ring.at[lax.rem(c, RING), pl.ds(side * CHUNK, CHUNK)],
                ring_in.at[lax.rem(c, RING), side],
            )
            for side, rows in enumerate(sides(c, CHUNK))
        ]

    def input_stores(c):
        return [
            pltpu.make_async_copy(
                ring.at[lax.rem(c, RING), pl.ds(side * CHUNK, CHUNK)],
                d_inputs.at[rows],
                ring_out.at[lax.rem(c, RING), side],
            )
            for side, rows in enumerate(sides(c, CHUNK))
        ]

    def norm_rows(c):
        settle2(c)
        for load in hidden_loads(c):
            load.wait()
        for side, rows in enumerate(sides(c, CHUNK)):
            _, scaled, inverse = norm_forward(n1[rows].astype(jnp.float32), 1.0, 0.0)
            grad = total[rows].astype(jnp.float32)
            late[0:1] += jnp.sum(grad * scaled, axis=0, keepdims=True)
            late[1:2] += jnp.sum(grad, axis=0, keepdims=True)
            here = pl.ds(side * CHUNK, CHUNK)
            ring[lax.rem(c, RING), here] += norm_backward(grad, scaled, inverse, gain1[...])
        for store in input_stores(c):
            store.start()

        @pl.when(c >= 2)
        def _():
            for store in input_stores(c - 2):
                store.wait()

        @pl.when(c + 2 < chunks)
        def _():
            for load in hidden_loads(c + 2):
                load.start()

    arrival = chunks + travel

    def tick_of(t):
        both_steps(t)

        @pl.when(t >= arrival)
        def _():
            norm_rows(t - arrival)

    for j in range(blocks):
        gradient(j)
        if j == blocks - 1:
            for c in range(2):
                for load in hidden_loads(c):
                    load.start()
            loads[3].wait()
        begin = chunks + j * per_block
        loop(begin, begin + per_block, tick_of if j == blocks - 1 else both_steps)
        if spread and j == 0:
            pair()
        if spread and j == 2:
            cross()
            for i in range(3):
                early_begin(i)
                early_end(i)
    begin = chunks + blocks * per_block
    middle = begin + per_block
    loop(begin, middle, tick_of)
    if spread:
        for k in range(len(pieces)):
            total_of(k)
        for store in stores:
            store.start()
    loop(middle, arrival + chunks, tick_of)
    if spread:
        for i in range(3):
            late_begin(i)
            late_end(i)
    for c in (chunks - 2, chunks - 1):
        for store in input_stores(c):
            store.wait()
    if spread:
        finish_scatter()
        for store in stores:
            store.wait()
    finish1()
    finish2()


def backward(
    prefix_len, projected, d_bin, b_out, gain1, gain2, mlp_partial, normed1, context, w_qkv, w_out,
    inputs, attn_sum, d_output, summed2,
):
    tokens, depth = inputs.shape
    width = w_out.shape[0]
    spread = (lax.axis_size("dp"), lax.axis_size("col")) == (2, 4)
    dma = pltpu.SemaphoreType.DMA
    buffer = lambda *shape: pltpu.VMEM(shape, jnp.bfloat16)
    wide_buffer = lambda *shape: pltpu.VMEM(shape, jnp.float32)
    single = lambda *shape: jax.ShapeDtypeStruct(shape, jnp.float32)
    sums, scatter_scratch = [single(8, 128), single(8, 128)], []
    if spread:
        block, side = (3, depth // 8, width), (width, depth // 8)
        sums = [single(*block), single(*side)]
        scatter_scratch = [wide_buffer(3, 8, depth), wide_buffer(3, 8, depth)]
        scatter_scratch += [dma((2, 3)), dma((2, 3))]
        for shape in (block, side):
            scatter_scratch += [
                buffer(4, *shape), buffer(4, *shape), buffer(*shape), buffer(2, *shape)
            ]
        scatter_scratch += [wide_buffer(*block), wide_buffer(*side)]
        scatter_scratch += [dma((2,)), dma((4, 8)), dma((4, 8)), dma((8,)), dma((8,))]
        scatter_scratch += [dma((2, 8)), dma((2, 8)), dma((4, 8))]
    out = pl.pallas_call(
        partial(backward_kernel, lax.axis_size("row"), spread),
        out_shape=[
            low_shape(tokens, depth),
            single(tokens, depth),
            single(tokens, depth),
            low_shape(3, depth, width),
            low_shape(width, depth),
            *sums,
            single(8, depth),
            single(8, depth),
        ],
        in_specs=[pl.BlockSpec(memory_space=pltpu.SMEM)] + [IN_VMEM] * 5 + [IN_HBM] * 9,
        out_specs=[IN_HBM] * 7 + [IN_VMEM] * 2,
        scratch_shapes=[
            buffer(tokens, depth),
            buffer(tokens, width),
            buffer(tokens, depth),
            buffer(tokens, width),
            buffer(tokens, depth),
            wide_buffer(tokens, HEAD_DIM),
            wide_buffer(tokens, HEAD_DIM),
            buffer(3, tokens, width),
            buffer(2, TILE, TILE),
            buffer(tokens, depth),
            buffer(*w_qkv.shape),
            wide_buffer(RING, SLICE, depth),
            dma((2, tokens // BLOCK)),
            dma((2, 4)),
            dma((5,)),
            dma((2,)),
            dma((RING, 2)),
            dma((RING, 2)),
        ]
        + line_scratch((tokens, depth))
        + line_scratch((tokens, depth))
        + scatter_scratch,
        compiler_params=kernel_params(2, 63),
        cost_estimate=COST,
    )(
        prefix_len, projected, d_bin, b_out[None], gain1[None], gain2[None], mlp_partial, normed1,
        context, w_qkv, w_out, inputs, attn_sum, d_output, summed2,
    )
    mlp_sum, d_inputs, _, d_wqkv, d_wout, sum_wqkv, sum_wout, early, late = out
    if not spread:
        early, late = lax.psum((early, late), ("dp", "col"))
        sum_wqkv, sum_wout = scatter_low(d_wqkv, 1), scatter_low(d_wout, 1)
    return mlp_sum, d_inputs, sum_wqkv, sum_wout, early, late


def scatter_low(grad, dim):
    summed = lax.psum_scatter(grad, ("dp", "col"), scatter_dimension=dim, tiled=True)
    return summed.astype(jnp.float32)


def local(
    inputs,
    prefix_len,
    norm1_gain,
    norm1_shift,
    w_qkv,
    b_qv,
    w_out,
    b_out,
    norm2_gain,
    norm2_shift,
    w_in,
    b_in,
    w_down,
    b_down,
    d_output,
):
    low_mats = (
        w_qkv.astype(jnp.bfloat16),
        w_out.astype(jnp.bfloat16),
        w_in.astype(jnp.bfloat16),
        w_down.astype(jnp.bfloat16),
    )
    full_qkv, full_out, full_in, full_down = (
        lax.all_gather(low_mats[0], ("dp", "col"), axis=1, tiled=True),
        lax.all_gather(low_mats[1], ("dp", "col"), axis=1, tiled=True),
        low_mats[2],
        low_mats[3],
    )
    if (lax.axis_size("dp"), lax.axis_size("col")) != (2, 4):
        full_in = lax.all_gather(full_in, ("dp", "col"), axis=0, tiled=True)
        full_down = lax.all_gather(full_down, ("dp", "col"), axis=1, tiled=True)
    source = inputs.astype(jnp.float32)
    normed1, _, _ = norm_forward(source, norm1_gain, norm1_shift)
    normed1_low = normed1.astype(jnp.bfloat16)
    projected = jnp.einsum("td,cdn->ctn", normed1_low, full_qkv, preferred_element_type=jnp.float32)
    bias_rows = jnp.stack([b_qv[0], jnp.zeros_like(b_qv[0]), b_qv[1]])
    projected = (projected + bias_rows[:, None, :]).astype(jnp.bfloat16)
    context_low = attend(prefix_len, projected)
    attn_sum, summed2, mlp_partial, grad_wdown, grad_win, grad_bin = mlp_sums(
        context_low, full_out, b_out, norm2_gain, norm2_shift, b_in,
        inputs, full_in, full_down, d_output,
    )
    sent_win = scatter_low(grad_win, 0)
    sent_wdown = scatter_low(grad_wdown, 1)
    mlp_sum, d_inputs, sent_wqkv, sent_wout, early, late = backward(
        prefix_len, projected, grad_bin, b_out, norm1_gain, norm2_gain, mlp_partial, normed1_low,
        context_low, full_qkv, full_out, inputs, attn_sum, d_output, summed2,
    )
    hidden = source + attn_sum.astype(jnp.float32) + b_out
    output = (hidden + mlp_sum.astype(jnp.float32) + b_down).astype(jnp.bfloat16)
    width = b_qv.shape[1]
    return (
        output,
        d_inputs,
        late[0],
        late[1],
        sent_wqkv,
        early[5, : 2 * width].reshape(2, width),
        sent_wout,
        early[0],
        early[1],
        early[2],
        sent_win,
        early[4],
        sent_wdown,
        early[3],
    )


def solution(mesh):
    return jax.shard_map(
        local,
        mesh=mesh,
        in_specs=(
            P(("dp", "col"), None),
            P(("dp", "col")),
            P(),
            P(),
            P(None, ("dp", "col"), "row"),
            P(None, "row"),
            P("row", ("dp", "col")),
            P(),
            P(),
            P(),
            P(("dp", "col"), "row"),
            P("row"),
            P("row", ("dp", "col")),
            P(),
            P(("dp", "col"), None),
        ),
        out_specs=(
            P(("dp", "col"), None),
            P(("dp", "col"), None),
            P(),
            P(),
            P(None, ("dp", "col"), "row"),
            P(None, "row"),
            P("row", ("dp", "col")),
            P(),
            P(),
            P(),
            P(("dp", "col"), "row"),
            P("row"),
            P("row", ("dp", "col")),
            P(),
        ),
        check_vma=False,
    )
```

```python
from functools import partial

import jax
import jax.numpy as jnp
from jax import lax
from jax.experimental import pallas as pl
from jax.experimental.pallas import tpu as pltpu
from jax.sharding import PartitionSpec as P

HEAD_DIM = 128
MESH_IDS = pl.DeviceIdType.MESH
CHUNK = 32
LAG = 2


eps_norm = 1e-05


def norm_forward(values, norm_gain, norm_shift):
    average = jnp.mean(values, axis=-1, keepdims=True)
    centered = values - average
    variance = jnp.mean(centered * centered, axis=-1, keepdims=True)
    inverse = lax.rsqrt(variance + eps_norm)
    scaled = centered * inverse
    return (scaled * norm_gain + norm_shift, scaled, inverse)


def norm_backward(grad, scaled, inverse, norm_gain):
    grad_scaled = grad * norm_gain
    return inverse * (
        grad_scaled
        - jnp.mean(grad_scaled, axis=-1, keepdims=True)
        - scaled * jnp.mean(grad_scaled * scaled, axis=-1, keepdims=True)
    )


def dot(left, right, left_dim, right_dim):
    return lax.dot_general(
        left, right, (((left_dim,), (right_dim,)), ((), ())), preferred_element_type=jnp.float32
    )


def greet_row(n, others=()):
    r = lax.axis_index("row")
    last = n - 1
    bar = pltpu.get_barrier_semaphore()
    for cond, dev in ((r > 0, r - 1), (r < last, r + 1)):

        @pl.when(cond)
        def _():
            pl.semaphore_signal(bar, inc=1, device_id={"row": dev}, device_id_type=MESH_IDS)

    for other in others:
        pl.semaphore_signal(bar, inc=1, device_id=other, device_id_type=MESH_IDS)
    inside = (r > 0) & (r < last)

    @pl.when(inside)
    def _():
        pl.semaphore_wait(bar, 2 + len(others))

    @pl.when(jnp.logical_not(inside))
    def _():
        pl.semaphore_wait(bar, 1 + len(others))


def plane_partners():
    y, x = lax.axis_index("dp"), lax.axis_index("col")
    far_x, near = lax.rem(x + 2, 4), x + 1 - 2 * lax.rem(x, 2)
    far_near = lax.rem(near + 2, 4)
    ids = {"x": {"col": far_x}, "y": {"dp": 1 - y}, "near": {"col": near}}
    mine = {"own": y * 4 + x, "x": y * 4 + far_x, "y": (1 - y) * 4 + x, "xy": (1 - y) * 4 + far_x}
    theirs = {
        "own": y * 4 + near,
        "x": y * 4 + far_near,
        "y": (1 - y) * 4 + near,
        "xy": (1 - y) * 4 + far_near,
    }
    return ids, mine, theirs


KINDS = ("own", "x", "y", "xy")


def plane_gather(pieces, send_sem, recv_sem, near_send, near_recv, local_sem):
    ids, mine, theirs = plane_partners()
    count = len(pieces)

    def remote(kind, k, to, src, dst):
        row = KINDS.index(kind)
        near = to == "near"
        return pltpu.make_async_remote_copy(
            src_ref=src,
            dst_ref=dst,
            send_sem=(near_send if near else send_sem).at[row, k],
            recv_sem=(near_recv if near else recv_sem).at[row, k],
            device_id=ids[to],
            device_id_type=MESH_IDS,
        )

    def outgoing(k):
        own, place = pieces[k](mine["own"])
        return [remote("x", k, "x", own, place), remote("y", k, "y", own, place)]

    def local(k):
        own, place = pieces[k](mine["own"])
        return pltpu.make_async_copy(own, place, local_sem.at[k])

    def onward(k):
        kind, to = ("x", "y") if k % 2 == 0 else ("y", "x")
        place = pieces[k](mine[kind])[1]
        return remote("xy", k, to, place, place)

    def share(kind, k):
        own, place = pieces[k](mine[kind])
        return remote(kind, k, "near", own if kind == "own" else place, place)

    def start():
        for k in range(count):
            for copy in outgoing(k):
                copy.start()
        for k in range(count):
            share("own", k).start()
            local(k).start()

    def arrive(k):
        for copy in outgoing(k):
            copy.wait_recv()
        onward(k).start()
        share("x", k).start()
        share("y", k).start()

    def arrive_far(k):
        onward(k).wait_recv()
        share("xy", k).start()

    def finish():
        for k in range(count):
            local(k).wait()
            for copy in outgoing(k):
                copy.wait_send()
            onward(k).wait_send()
            for kind in KINDS:
                place = pieces[k](theirs[kind])[1]
                share(kind, k).wait_send()
                remote(kind, k, "near", place, place).wait_recv()

    return list(ids.values()), start, arrive, arrive_far, finish


def line_sum(n, p_ref, o_ref, held, rs_s, rs_r, ag_s, ag_r, loc):
    half = o_ref.shape[0] // 2
    chunks = held.shape[0] // 2 // CHUNK
    r = lax.axis_index("row")
    last = n - 1
    place = (r, last - r)
    after = (jnp.minimum(r + 1, last), jnp.maximum(r - 1, 0))
    before = (jnp.maximum(r - 1, 0), jnp.minimum(r + 1, last))

    def rows(d, c):
        return pl.ds(pl.multiple_of((half if d == 0 else 0) + c * CHUNK, CHUNK), CHUNK)

    def slot(d, c):
        return pl.ds(pl.multiple_of((1 - d) * chunks * CHUNK + c * CHUNK, CHUNK), CHUNK)


    def onward(d, c, src):
        return pltpu.make_async_remote_copy(
            src_ref=src.at[rows(d, c) if src is p_ref else slot(d, c)],
            dst_ref=held.at[slot(d, c)],
            send_sem=rs_s.at[d, c],
            recv_sem=rs_r.at[d, c],
            device_id={"row": after[d]},
            device_id_type=MESH_IDS,
        )

    def back(d, c, src):
        return pltpu.make_async_remote_copy(
            src_ref=src.at[slot(d, c) if src is held else rows(d, c)],
            dst_ref=o_ref.at[rows(d, c)],
            send_sem=ag_s.at[d, c],
            recv_sem=ag_r.at[d, c],
            device_id={"row": before[d]},
            device_id_type=MESH_IDS,
        )

    def keep(d, c):
        return pltpu.make_async_copy(held.at[slot(d, c)], o_ref.at[rows(d, c)], loc.at[c])

    def step(t):
        for d in (0, 1):

            @pl.when((place[d] == 0) & (t >= 0) & (t < chunks))
            def _():
                onward(d, t, p_ref).start()

            c = t - LAG * place[d]

            @pl.when((place[d] > 0) & (c >= 0) & (c < chunks))
            def _():
                onward(d, c, p_ref).wait_recv()
                here = slot(d, c)
                held[here] = (
                    held[here].astype(jnp.float32) + p_ref[rows(d, c)].astype(jnp.float32)
                ).astype(jnp.bfloat16)

                @pl.when(place[d] < last)
                def _():
                    onward(d, c, held).start()

                @pl.when(place[d] == last)
                def _():
                    back(d, c, held).start()
                    keep(d, c).start()

        for d in (0, 1):
            c = t - LAG * (2 * last - place[d])

            @pl.when((place[d] < last) & (c >= 0) & (c < chunks))
            def _():
                back(d, c, o_ref).wait_recv()

                @pl.when(place[d] > 0)
                def _():
                    back(d, c, o_ref).start()

    def settle(c):
        for d in (0, 1):

            @pl.when(place[d] < last)
            def _():
                onward(d, c, p_ref).wait_send()

            @pl.when(place[d] == last)
            def _():
                keep(d, c).wait()

    def finish(c):
        for d in (0, 1):

            @pl.when(place[d] > 0)
            def _():
                back(d, c, o_ref).wait_send()

    def drain():
        def both(c):
            settle(c)
            finish(c)

        loop(0, chunks, both)

    return step, drain, settle, lambda: loop(0, chunks, finish)


def line_steps(n, total_rows):
    return total_rows // 2 // CHUNK + LAG * 2 * (n - 1)


def line_scratch(shape):
    chunks = shape[0] // 2 // CHUNK
    dma = pltpu.SemaphoreType.DMA
    return [
        pltpu.VMEM(shape, jnp.bfloat16),
        dma((2, chunks)),
        dma((2, chunks)),
        dma((2, chunks)),
        dma((2, chunks)),
        dma((chunks,)),
    ]


def loop(start, stop, body):
    def one(t, carry):
        body(t)
        return carry

    lax.fori_loop(start, stop, one, 0)


COST = pl.CostEstimate(flops=1000, bytes_accessed=1000, transcendentals=0)
IN_VMEM = pl.BlockSpec(memory_space=pltpu.VMEM)
IN_HBM = pl.BlockSpec(memory_space=pl.ANY)


def low_shape(*shape):
    return jax.ShapeDtypeStruct(shape, jnp.bfloat16)


def kernel_params(collective_id, mib):
    return pltpu.CompilerParams(
        collective_id=collective_id, has_side_effects=True, vmem_limit_bytes=mib * 2**20
    )


TILE = 512
FEW = 16
BLOCK = 256


def mlp_sums_kernel(
    n, spread, ctx, w_out, b_out, gain, shift, b_in, src_hbm, w_in_hbm, w_down_hbm, g_hbm,
    branch, d_normed, mlp, d_wdown, d_win, d_bin,
    p, w_in, w_down, g, normed, act, d_pre, mlp_acc, d_acc, rows_a, rows_b, stage, w_stage,
    load_sem, block_sem, mlp_sem, store_sem, *more,
):
    tokens, depth = p.shape
    units = act.shape[1]
    half = tokens // 2
    part = BLOCK // 2
    blocks = tokens // BLOCK
    per_block = part // CHUNK
    quarters = units // TILE

    def sides(j):
        low_rows = pl.ds(pl.multiple_of(j * part, part), part)
        high_rows = pl.ds(pl.multiple_of(half + j * part, part), part)
        return low_rows, high_rows

    def own(j, side=None):
        if side is None:
            return pl.ds(pl.multiple_of(j * BLOCK, BLOCK), BLOCK)
        return pl.ds(pl.multiple_of(j * BLOCK + side * part, part), part)

    lines, gather_sems = more[:12], more[12:]
    loads = []
    others = []
    if spread:
        deep, wide = w_in_hbm.shape[0], w_down_hbm.shape[1]

        def in_piece(k, place):
            size = deep // 2
            there = pl.ds(pl.multiple_of(place * deep + k * size, size), size)
            return w_in_hbm.at[pl.ds(k * size, size)], w_in.at[there]

        def down_piece(k, place):
            some = pl.ds(k * (units // 2), units // 2)
            cols = pl.ds(pl.multiple_of(place * wide, wide), wide)
            return w_down_hbm.at[some], w_down.at[some, cols]

        pieces = [partial(f, k) for f in (in_piece, down_piece) for k in range(2)]
        others, start_gather, arrive, arrive_far, finish_gather = plane_gather(
            pieces, *gather_sems
        )
    else:
        loads = [
            pltpu.make_async_copy(w_in_hbm, w_in, load_sem.at[0]),
            pltpu.make_async_copy(w_down_hbm, w_down, load_sem.at[1]),
        ]
    for j in range(blocks):
        for side, here in enumerate((j * part, half + j * part)):
            loads.append(
                pltpu.make_async_copy(
                    g_hbm.at[pl.ds(here, part)],
                    g.at[pl.ds(j * BLOCK + side * part, part)],
                    load_sem.at[2 + 2 * j + side],
                )
            )
    for load in loads:
        load.start()
    d_bin[...] = jnp.zeros_like(d_bin)
    greet_row(n, others)
    if spread:
        start_gather()
    step1, _, settle1, finish1 = line_sum(n, p, branch, *lines[:6])
    step2, drain2, _, _ = line_sum(n, p, d_normed, *lines[6:])

    def project(j):
        low_rows, high_rows = sides(j)
        both = jnp.concatenate([ctx[low_rows], ctx[high_rows]], axis=0)
        for c in range(0, depth, TILE):
            cols = slice(c, c + TILE)
            term = dot(both, w_out[:, cols], 1, 0).astype(jnp.bfloat16)
            p[low_rows, cols] = term[:part]
            p[high_rows, cols] = term[part:]
        loop(j * per_block, (j + 1) * per_block, step1)

    for j in range(blocks):
        project(j)
        if spread and j == blocks - 2:
            for k in range(len(pieces)):
                arrive(k)
    if spread:
        for k in range(len(pieces)):
            arrive_far(k)
        finish_gather()
    for load in loads:
        load.wait()

    def norm_block(j):
        loop(j * per_block, (j + 1) * per_block, settle1)
        copies = []
        for i, (src, dst) in enumerate(((branch, rows_a), (src_hbm, rows_b))):
            for side, here in enumerate(sides(j)):
                copies.append(
                    pltpu.make_async_copy(
                        src.at[here], dst.at[pl.ds(side * part, part)], block_sem.at[i, side]
                    )
                )
        for copy in copies:
            copy.start()
        for copy in copies:
            copy.wait()

        def few(k):
            here = pl.ds(pl.multiple_of(k * FEW, FEW), FEW)
            there = pl.ds(pl.multiple_of(j * BLOCK + k * FEW, FEW), FEW)
            source = rows_b[here].astype(jnp.float32)
            hidden = source + rows_a[here].astype(jnp.float32) + b_out[...]
            normed[there] = norm_forward(hidden, gain[...], shift[...])[0].astype(jnp.bfloat16)

        loop(0, BLOCK // FEW, few)

    def mlp_out(j):
        return [
            pltpu.make_async_copy(
                stage.at[pl.ds(side * part, part)], mlp.at[here], mlp_sem.at[side]
            )
            for side, here in enumerate(sides(j))
        ]

    first = tokens // 2 // CHUNK

    def block(j):
        for q in range(quarters):
            t = first + j * per_block + q
            step1(t)
            step2(t - first - per_block)
            if q == 0:
                norm_block(j)
            units_q = slice(q * TILE, (q + 1) * TILE)
            here = own(j)
            pre = dot(normed[here], w_in[:, units_q], 1, 0) + b_in[:, units_q]
            d_act = dot(g[here], w_down[units_q], 1, 1)
            lower = 0.5 * (1.0 + lax.erf(pre * 0.5**0.5))
            act[here, units_q] = (pre * lower).astype(jnp.bfloat16)
            slope = lower + pre * (jnp.exp(-0.5 * pre * pre) * (0.5 / jnp.pi) ** 0.5)
            low_pre = (d_act * slope).astype(jnp.bfloat16)
            d_pre[here, units_q] = low_pre
            d_bin[:, units_q] += jnp.sum(low_pre.astype(jnp.float32), axis=0, keepdims=True)
            for c in range(0, depth, TILE):
                cols = slice(c, c + TILE)
                m_term = dot(act[here, units_q], w_down[units_q, cols], 1, 0)
                d_term = dot(d_pre[here, units_q], w_in[cols, units_q], 1, 1)
                if q == 0:
                    mlp_acc[:, cols] = m_term
                    d_acc[:, cols] = d_term
                elif q < quarters - 1:
                    mlp_acc[:, cols] += m_term
                    d_acc[:, cols] += d_term
                else:
                    if c == 0:

                        @pl.when(j > 0)
                        def _():
                            for copy in mlp_out(j - 1):
                                copy.wait()

                    stage[:, cols] = (mlp_acc[:, cols] + m_term).astype(jnp.bfloat16)
                    d_low = (d_acc[:, cols] + d_term).astype(jnp.bfloat16)
                    for side, rows in enumerate(sides(j)):
                        p[rows, cols] = d_low[side * part : (side + 1) * part]
        for copy in mlp_out(j):
            copy.start()

    loop(0, blocks, block)
    begin = first
    steps = line_steps(n, tokens)
    tick = tokens // 2 // CHUNK - per_block
    jobs = ((act, g, d_wdown), (normed, d_pre, d_win))
    for k, (left, right, out) in enumerate(jobs):
        across = out.shape[1] // TILE
        tiles = (out.shape[0] // TILE) * across

        def store(tile, slot):
            m = pl.ds(pl.multiple_of((tile // across) * TILE, TILE), TILE)
            c = pl.ds(pl.multiple_of(lax.rem(tile, across) * TILE, TILE), TILE)
            copy = pltpu.make_async_copy(w_stage.at[slot], out.at[m, c], store_sem.at[slot])
            return m, c, copy

        def body(u):
            step2(tick + k * (tiles // 2) + u)
            for slot in range(2):
                m, c, copy = store(2 * u + slot, slot)
                if k == 0:

                    @pl.when(u > 0)
                    def _():
                        copy.wait()
                else:
                    copy.wait()
                w_stage[slot] = dot(left[:, m], right[:, c], 0, 0).astype(jnp.bfloat16)
                copy.start()

        loop(0, tiles // 2, body)
        tick_end = tick + (k + 1) * (tiles // 2)
    if tick_end < steps:
        loop(tick_end, steps, step2)
    for slot in range(2):
        store(slot, slot)[2].wait()
    for copy in mlp_out(blocks - 1):
        copy.wait()
    finish1()
    drain2()


def mlp_sums(context, w_out, b_out, gain, shift, b_in, inputs, w_in, w_down, d_output):
    tokens, depth = inputs.shape
    units = w_in.shape[1]
    spread = w_in.shape[0] < depth
    dma = pltpu.SemaphoreType.DMA
    low_buffer = lambda *shape: pltpu.VMEM(shape, jnp.bfloat16)
    return pl.pallas_call(
        partial(mlp_sums_kernel, lax.axis_size("row"), spread),
        out_shape=[
            low_shape(tokens, depth),
            low_shape(tokens, depth),
            low_shape(tokens, depth),
            low_shape(units, depth),
            low_shape(depth, units),
            jax.ShapeDtypeStruct((1, units), jnp.float32),
        ],
        in_specs=[IN_VMEM] * 6 + [IN_HBM] * 4,
        out_specs=[IN_HBM] * 5 + [IN_VMEM],
        scratch_shapes=[
            low_buffer(tokens, depth),
            low_buffer(depth, units),
            low_buffer(units, depth),
            low_buffer(tokens, depth),
            low_buffer(tokens, depth),
            low_buffer(tokens, units),
            low_buffer(tokens, units),
            pltpu.VMEM((BLOCK, depth), jnp.float32),
            pltpu.VMEM((BLOCK, depth), jnp.float32),
            low_buffer(BLOCK, depth),
            low_buffer(BLOCK, depth),
            low_buffer(BLOCK, depth),
            low_buffer(2, TILE, TILE),
            dma((2 + 2 * (tokens // BLOCK),)),
            dma((2, 2)),
            dma((2,)),
            dma((2,)),
        ]
        + line_scratch((tokens, depth))
        + line_scratch((tokens, depth))
        + ([dma((4, 4))] * 4 + [dma((4,))] if spread else []),
        compiler_params=kernel_params(1, 61),
        cost_estimate=COST,
    )(
        context, w_out, b_out[None], gain[None], shift[None], b_in[None],
        inputs, w_in, w_down, d_output,
    )


QUERY_ROWS = 256


def head_kernel(
    prefix_ref, src, gain, shift, b_q, b_v, w_qkv_hbm, w_out_hbm,
    normed, projected, context, full_qkv, full_out,
    weights, w_out, store_sem, *sems,
):
    tokens, depth = src.shape
    width = projected.shape[2]
    deep, wide = w_qkv_hbm.shape[1], w_out_hbm.shape[1]
    size, tall = deep // 2, width // 2

    def qkv_piece(c, k, place):
        there = pl.ds(pl.multiple_of(place * deep + k * size, size), size)
        return w_qkv_hbm.at[c, pl.ds(k * size, size)], weights.at[c, there]

    def out_piece(k, place):
        some = pl.ds(k * tall, tall)
        cols = pl.ds(pl.multiple_of(place * wide, wide), wide)
        return w_out_hbm.at[some], w_out.at[some, cols]

    qkv_pieces = [partial(qkv_piece, c, k) for c in range(3) for k in range(2)]
    out_pieces = [partial(out_piece, k) for k in range(2)]
    others, start1, arrive1, far1, finish1 = plane_gather(qkv_pieces, *sems[:5])
    _, start2, arrive2, far2, finish2 = plane_gather(out_pieces, *sems[5:])
    bar = pltpu.get_barrier_semaphore()
    for other in others:
        pl.semaphore_signal(bar, inc=1, device_id=other, device_id_type=MESH_IDS)
    pl.semaphore_wait(bar, len(others))
    start1()

    def few(r):
        here = pl.ds(pl.multiple_of(r * FEW, FEW), FEW)
        rows = norm_forward(src[here].astype(jnp.float32), gain[...], shift[...])[0]
        normed[here] = rows.astype(jnp.bfloat16)

    loop(0, tokens // FEW, few)
    for k in range(len(qkv_pieces)):
        arrive1(k)
    start2()
    for k in range(len(qkv_pieces)):
        far1(k)
    finish1()
    stores = [pltpu.make_async_copy(weights, full_qkv, store_sem.at[0])]
    stores[0].start()
    for c in range(3):

        def rows_of(i):
            here = pl.ds(pl.multiple_of(i * BLOCK, BLOCK), BLOCK)
            term = dot(normed[here], weights[c], 1, 0)
            if c != 1:
                term += (b_q if c == 0 else b_v)[...]
            projected[c, here] = term.astype(jnp.bfloat16)

        loop(0, tokens // BLOCK, rows_of)
    for k in range(len(out_pieces)):
        arrive2(k)
    attend_kernel(prefix_ref, projected, context)
    for k in range(len(out_pieces)):
        far2(k)
    finish2()
    stores.append(pltpu.make_async_copy(w_out, full_out, store_sem.at[1]))
    stores[1].start()
    for store in stores:
        store.wait()


def head(prefix_len, inputs, gain, shift, b_qv, w_qkv, w_out):
    tokens, depth = inputs.shape
    width = w_out.shape[0]
    dma = pltpu.SemaphoreType.DMA
    return pl.pallas_call(
        head_kernel,
        out_shape=[
            low_shape(tokens, depth),
            low_shape(3, tokens, width),
            low_shape(tokens, width),
            low_shape(3, depth, width),
            low_shape(width, depth),
        ],
        in_specs=[pl.BlockSpec(memory_space=pltpu.SMEM)] + [IN_VMEM] * 5 + [IN_HBM] * 2,
        out_specs=[IN_VMEM] * 3 + [IN_HBM] * 2,
        scratch_shapes=[
            pltpu.VMEM((3, depth, width), jnp.bfloat16),
            pltpu.VMEM((width, depth), jnp.bfloat16),
            dma((2,)),
        ]
        + [dma((4, 6))] * 4
        + [dma((6,))]
        + [dma((4, 2))] * 4
        + [dma((2,))],
        compiler_params=kernel_params(3, 40),
        cost_estimate=COST,
    )(prefix_len, inputs, gain[None], shift[None], b_qv[:1], b_qv[1:], w_qkv, w_out)


def block_probs(i, prefix, cols, q, k):
    start = i * QUERY_ROWS
    width = max(start + QUERY_ROWS, q.shape[0] // 2)
    here = slice(start, start + QUERY_ROWS)
    scores = dot(k[:width, cols], q[here, cols], 1, 1) * HEAD_DIM ** (-0.5)
    key = lax.broadcasted_iota(jnp.int32, scores.shape, 0)
    query = lax.broadcasted_iota(jnp.int32, scores.shape, 1) + start
    scores = jnp.where((key <= query) | (key < prefix), scores, -1000000000.0)
    expo = jnp.exp(scores - jnp.max(scores, axis=0, keepdims=True))
    return here, width, expo * (1.0 / jnp.sum(expo, axis=0, keepdims=True))


def attend_kernel(prefix_ref, projected, context):
    q, k, v = (projected.at[c] for c in range(3))
    prefix = prefix_ref[0]

    def head(h):
        cols = pl.ds(pl.multiple_of(h * HEAD_DIM, HEAD_DIM), HEAD_DIM)
        v_t = v[:, cols].T
        for i in range(q.shape[0] // QUERY_ROWS):
            here, width, probs = block_probs(i, prefix, cols, q, k)
            out = dot(v_t[:, :width], probs.astype(jnp.bfloat16), 1, 0)
            context[here, cols] = out.T.astype(jnp.bfloat16)

    loop(0, q.shape[1] // HEAD_DIM, head)


def attend(prefix_len, projected):
    return pl.pallas_call(
        attend_kernel,
        out_shape=low_shape(*projected.shape[1:]),
        in_specs=[pl.BlockSpec(memory_space=pltpu.SMEM), IN_VMEM],
        out_specs=IN_VMEM,
        compiler_params=pltpu.CompilerParams(vmem_limit_bytes=32 * 2**20),
        cost_estimate=COST,
    )(prefix_len, projected)


def attend_piece(i, prefix, cols, q, k, v, k_t, d_context, d_proj, d_key, d_value, first):
    score_scale = HEAD_DIM ** (-0.5)
    here, width, probs = block_probs(i, prefix, cols, q, k)
    q_block, g_block = q[here, cols], d_context[here, cols]
    d_probs = dot(v[:width, cols], g_block, 1, 1)
    inner = jnp.sum(d_probs * probs, axis=0, keepdims=True)
    d_scores = (probs * (d_probs - inner)).astype(jnp.bfloat16)
    d_query = dot(k_t[:, :width], d_scores, 1, 0) * score_scale
    d_proj[0, here, cols] = d_query.T.astype(jnp.bfloat16)
    for total, term in (
        (d_key, dot(d_scores, q_block, 1, 0)),
        (d_value, dot(probs.astype(jnp.bfloat16), g_block, 1, 0)),
    ):
        if first:
            total[...] = term
        else:
            total[:width] += term


def plane_scatter(pieces, sems):
    ids, mine, theirs = plane_partners()
    near_send, near_recv, far_send, far_recv, last_send, last_recv, load_sem = sems
    count = len(pieces)

    def remote(src, dst, send, recv, to):
        return pltpu.make_async_remote_copy(
            src_ref=src,
            dst_ref=dst,
            send_sem=send,
            recv_sem=recv,
            device_id=ids[to],
            device_id_type=MESH_IDS,
        )

    def near(i, k):
        block, to, _, _, _ = pieces[k]
        place = theirs[KINDS[i]]
        return remote(block(place), to(i), near_send.at[i, k], near_recv.at[i, k], "near")

    def load(i, k):
        block, _, own, _, _ = pieces[k]
        return pltpu.make_async_copy(block(mine[KINDS[i]]), own(i), load_sem.at[i, k])

    def far(k):
        _, _, own, to, _ = pieces[k]
        return remote(own(3), to(), far_send.at[k], far_recv.at[k], "x" if k % 2 == 0 else "y")

    def last(i, k):
        _, _, own, _, to = pieces[k]
        return remote(
            own(i), to(i - 1), last_send.at[i - 1, k], last_recv.at[i - 1, k], KINDS[i]
        )

    def add(target, term):
        flat = target.shape[0]

        def some(r):
            here = pl.ds(pl.multiple_of(r * 128, 128), 128)
            target[here] = (
                target[here].astype(jnp.float32) + term[here].astype(jnp.float32)
            ).astype(jnp.bfloat16)

        loop(0, flat // 128, some)

    def start():
        for i in (3, 1, 2, 0):
            for k in range(count):
                near(i, k).start()
                load(i, k).start()

    def pair():
        for i in (3, 1, 2, 0):
            for k in range(count):
                near(i, k).wait_recv()
                load(i, k).wait()
                add(pieces[k][2](i), pieces[k][1](i))
                if i == 3:
                    far(k).start()
                elif i == 1 + k % 2:
                    last(i, k).start()

    def cross():
        for k in range(count):
            far(k).wait_recv()
            i = 2 - k % 2
            add(pieces[k][2](i), pieces[k][3]())
            last(i, k).start()

    def collect(k):
        for i in (1, 2):
            last(i, k).wait_recv()
        return pieces[k][2](0), pieces[k][4](0), pieces[k][4](1)

    def finish():
        for k in range(count):
            for i in range(4):
                near(i, k).wait_send()
            far(k).wait_send()
            for i in (1, 2):
                last(i, k).wait_send()

    return start, pair, cross, collect, finish


def sums_out(kind, vectors, slots, send_sem, recv_sem):
    ids = plane_partners()[0]

    def copy(i):
        return pltpu.make_async_remote_copy(
            src_ref=vectors,
            dst_ref=slots.at[i],
            send_sem=send_sem.at[kind, i],
            recv_sem=recv_sem.at[kind, i],
            device_id=ids[("near", "x", "y")[i]],
            device_id_type=MESH_IDS,
        )

    def begin(i):
        copy(i).start()

    def end(i):
        copy(i).wait()
        vectors[...] += slots[i]

    return begin, end


SLICE = 64
RING = 4


def backward_kernel(
    n, spread, prefix_ref, projected, d_bin, b_out, gain1, gain2,
    mlp_hbm, n1_hbm, ctx_hbm, w_qkv_hbm, w_out_hbm, src_hbm, attn_hbm, g_hbm, dn2_hbm,
    mlp_sum, d_inputs, d_hidden, d_wqkv, d_wout, sum_wqkv, sum_wout, early, late,
    p, d_context, n1, ctx, branch, d_key, d_value, d_proj, w_stage, total, weights, ring, partial_sums,
    p_sem, slice_sem, load_sem, store_sem, ring_in, ring_out, *more,
):
    lines, more = more[:12], more[12:]
    tokens, depth = p.shape
    width = projected.shape[2]
    half = tokens // 2
    chunks = half // CHUNK
    blocks = tokens // BLOCK
    part = BLOCK // 2
    per_block = part // CHUNK
    travel = LAG * 2 * (n - 1)
    prefix = prefix_ref[0]

    def sides(j, size):
        return (
            pl.ds(pl.multiple_of(j * size, size), size),
            pl.ds(pl.multiple_of(half + j * size, size), size),
        )

    p_loads = [
        [
            pltpu.make_async_copy(mlp_hbm.at[rows], p.at[rows], p_sem.at[side, j])
            for side, rows in enumerate((pl.ds(j * part, part), pl.ds(half + j * part, part)))
        ]
        for j in range(blocks)
    ]
    for loads in p_loads:
        for load in loads:
            load.start()
    w_out_load = pltpu.make_async_copy(w_out_hbm, total.at[pl.ds(0, width)], load_sem.at[0])
    w_out_load.start()
    loads = [
        pltpu.make_async_copy(src, dst, load_sem.at[1 + i])
        for i, (src, dst) in enumerate(
            ((n1_hbm, n1), (ctx_hbm, ctx), (w_qkv_hbm, weights), (src_hbm, n1))
        )
    ]
    early[...] = jnp.zeros_like(early)
    late[...] = jnp.zeros_like(late)
    early[4:5] = d_bin[...]
    partial_sums[...] = jnp.zeros_like(partial_sums)
    others = []
    if spread:
        slots_e, slots_l, small_s, small_r = more[:4]
        qkv_near, qkv_own, qkv_far, qkv_last, out_near, out_own, out_far, out_last = more[4:12]
        qkv_sum, out_sum, sum_sem = more[12:15]
        others = list(plane_partners()[0].values())
        early_begin, early_end = sums_out(0, early, slots_e, small_s, small_r)
        late_begin, late_end = sums_out(1, late, slots_l, small_s, small_r)
        places = 8
        deep, wide = depth // places, depth // places
        size = deep // 2
        tall = width // 2

        def qkv_piece(c, k):
            def block(place):
                there = pl.ds(pl.multiple_of(place * deep + k * size, size), size)
                return d_wqkv.at[c, there]

            some = pl.ds(k * size, size)
            return (
                block,
                lambda i: qkv_near.at[i, c, some],
                lambda i: qkv_own.at[i, c, some],
                lambda: qkv_far.at[c, some],
                lambda i: qkv_last.at[i, c, some],
            )

        def out_piece(k):
            some = pl.ds(k * tall, tall)

            def block(place):
                cols = pl.ds(pl.multiple_of(place * wide, wide), wide)
                return d_wout.at[some, cols]

            return (
                block,
                lambda i: out_near.at[i, some],
                lambda i: out_own.at[i, some],
                lambda: out_far.at[some],
                lambda i: out_last.at[i, some],
            )

        pieces = [qkv_piece(c, k) for c in range(3) for k in range(2)]
        pieces += [out_piece(k) for k in range(2)]
        start_scatter, pair, cross, collect, finish_scatter = plane_scatter(pieces, more[15:])
        stores = [
            pltpu.make_async_copy(qkv_sum, sum_wqkv, sum_sem.at[0]),
            pltpu.make_async_copy(out_sum, sum_wout, sum_sem.at[1]),
        ]

        def total_of(k):
            own, one, two = collect(k)
            if k < 6:
                target = qkv_sum.at[k // 2, pl.ds((k % 2) * size, size)]
            else:
                target = out_sum.at[pl.ds((k % 2) * tall, tall)]

            def some(r):
                here = pl.ds(pl.multiple_of(r * 128, 128), 128)
                target[here] = (
                    own[here].astype(jnp.float32)
                    + one[here].astype(jnp.float32)
                    + two[here].astype(jnp.float32)
                )

            loop(0, target.shape[0] // 128, some)

    greet_row(n, others)
    step1, _, settle1, finish1 = line_sum(n, p, mlp_sum, *lines[:6])
    step2, _, settle2, finish2 = line_sum(n, p, total, *lines[6:])

    def both_steps(t):
        step1(t)
        step2(t - chunks)

    slices = tokens // SLICE

    def slice_rows(k):
        return pl.ds(pl.multiple_of(k * SLICE, SLICE), SLICE)

    def slice_slot(k, i):
        return pl.ds(pl.multiple_of(half + (lax.rem(k, 2) * 4 + i) * SLICE, SLICE), SLICE)

    def slice_loads(k):
        return [
            pltpu.make_async_copy(
                src.at[slice_rows(k)], total.at[slice_slot(k, i)], slice_sem.at[lax.rem(k, 2), i]
            )
            for i, src in enumerate((dn2_hbm, attn_hbm, src_hbm, g_hbm))
        ]

    def hidden_store(k):
        return pltpu.make_async_copy(
            ring.at[lax.rem(k, RING)], d_hidden.at[slice_rows(k)], ring_out.at[lax.rem(k, RING), 0]
        )

    def norm_slice(k):
        @pl.when(k + 1 < slices)
        def _():
            for load in slice_loads(k + 1):
                load.start()

        for load in slice_loads(k):
            load.wait()

        @pl.when(k >= RING)
        def _():
            hidden_store(k - RING).wait()

        def few(r):
            rows = [
                pl.ds(pl.multiple_of(half + (lax.rem(k, 2) * 4 + i) * SLICE + r * FEW, FEW), FEW)
                for i in range(4)
            ]
            dn, attn, source, g = (total[some].astype(jnp.float32) for some in rows)
            _, scaled, inverse = norm_forward(source + attn + b_out[...], 1.0, 0.0)
            grad = g + norm_backward(dn, scaled, inverse, gain2[...])
            low = grad.astype(jnp.bfloat16)
            branch[pl.ds(pl.multiple_of(k * SLICE + r * FEW, FEW), FEW)] = low
            for i, term in enumerate((low.astype(jnp.float32), dn * scaled, dn, g)):
                partial_sums[8 * i : 8 * i + 8] += term[:8] + term[8:]
            ring[lax.rem(k, RING), pl.ds(pl.multiple_of(r * FEW, FEW), FEW)] = grad

        loop(0, SLICE // FEW, few)
        hidden_store(k).start()

    for load in slice_loads(0):
        load.start()
    norm_ticks = 4
    for load in p_loads[0]:
        load.wait()

    def norm_tick(t):
        step1(t)
        loop(t * (slices // norm_ticks), (t + 1) * (slices // norm_ticks), norm_slice)

    loop(0, norm_ticks, norm_tick)
    for i in range(4):
        early[i : i + 1] = jnp.sum(partial_sums[8 * i : 8 * i + 8], axis=0, keepdims=True)
    for k in range(slices - RING, slices):
        hidden_store(k).wait()
    for some in p_loads[1:]:
        for load in some:
            load.wait()
    for load in loads[:3]:
        load.start()
    w_out_load.wait()

    def context_rows(i):
        rows = pl.ds(pl.multiple_of(i * BLOCK, BLOCK), BLOCK)
        d_context[rows] = dot(branch[rows], total[:width], 1, 1).astype(jnp.bfloat16)

    loop(0, tokens // BLOCK, context_rows)
    partial_sums[...] = jnp.zeros_like(partial_sums)

    q, k, v = (projected.at[c] for c in range(3))
    q_blocks = tokens // QUERY_ROWS
    heads = width // HEAD_DIM
    head_ticks = q_blocks // 2

    def head(h):
        cols = pl.ds(pl.multiple_of(h * HEAD_DIM, HEAD_DIM), HEAD_DIM)
        k_t = k[:, cols].T
        for j in range(q_blocks):
            if j % 2 == 0:
                step1(norm_ticks + h * head_ticks + j // 2)
            attend_piece(
                q_blocks - 1 - j, prefix, cols, q, k, v, k_t, d_context, d_proj, d_key, d_value,
                j == 0,
            )
        d_proj[1, :, cols] = (d_key[...] * HEAD_DIM ** (-0.5)).astype(jnp.bfloat16)
        d_proj[2, :, cols] = d_value[...].astype(jnp.bfloat16)

    loop(0, heads, head)
    for b, c in ((0, 0), (1, 2)):
        early[5:6, b * width : (b + 1) * width] = jnp.sum(
            d_proj[c].astype(jnp.float32), axis=0, keepdims=True
        )
    for load in loads[:3]:
        load.wait()
    tick = norm_ticks + heads * head_ticks
    tiles = depth // TILE

    def tile_store(c, m):
        some = pl.ds(m * TILE, TILE)
        out = d_wqkv.at[c, some] if c < 3 else d_wout.at[:, some]
        return pltpu.make_async_copy(w_stage.at[m % 2], out, store_sem.at[m % 2])

    for c in range(4):
        step1(tick + c)
        for m in range(tiles):
            some = slice(m * TILE, (m + 1) * TILE)
            if c or m > 1:
                before = (c, m - 2) if m > 1 else (c - 1, tiles + m - 2)
                tile_store(*before).wait()
            if c < 3:
                term = dot(n1[:, some], d_proj[c], 0, 0)
            else:
                term = dot(ctx[...], branch[:, some], 0, 0)
            w_stage[m % 2] = term.astype(jnp.bfloat16)
            tile_store(c, m).start()
    for m in (tiles - 2, tiles - 1):
        tile_store(3, m).wait()
    loads[3].start()
    if tick + 4 < chunks:
        loop(tick + 4, chunks, step1)
    if spread:
        start_scatter()

    def gradient(j):
        loop(j * per_block, (j + 1) * per_block, settle1)
        low_rows, high_rows = sides(j, part)
        rows = [
            jnp.concatenate([d_proj[c, low_rows], d_proj[c, high_rows]], axis=0) for c in range(3)
        ]
        for i in range(0, depth, TILE):
            cols = slice(i, i + TILE)
            term = dot(rows[0], weights[0, cols], 1, 1)
            for c in (1, 2):
                term += dot(rows[c], weights[c, cols], 1, 1)
            term = term.astype(jnp.bfloat16)
            p[low_rows, cols] = term[:part]
            p[high_rows, cols] = term[part:]

    def hidden_loads(c):
        return [
            pltpu.make_async_copy(
                d_hidden.at[rows],
                ring.at[lax.rem(c, RING), pl.ds(side * CHUNK, CHUNK)],
                ring_in.at[lax.rem(c, RING), side],
            )
            for side, rows in enumerate(sides(c, CHUNK))
        ]

    def input_stores(c):
        return [
            pltpu.make_async_copy(
                ring.at[lax.rem(c, RING), pl.ds(side * CHUNK, CHUNK)],
                d_inputs.at[rows],
                ring_out.at[lax.rem(c, RING), side],
            )
            for side, rows in enumerate(sides(c, CHUNK))
        ]

    def norm_rows(c):
        settle2(c)
        for load in hidden_loads(c):
            load.wait()
        for side, rows in enumerate(sides(c, CHUNK)):
            for r in range(CHUNK // FEW):
                some = pl.ds(pl.multiple_of(rows.start + r * FEW, FEW), FEW)
                _, scaled, inverse = norm_forward(n1[some].astype(jnp.float32), 1.0, 0.0)
                grad = total[some].astype(jnp.float32)
                for i, term in enumerate((grad * scaled, grad)):
                    partial_sums[8 * i : 8 * i + 8] += term[:8] + term[8:]
                here = pl.ds(side * CHUNK + r * FEW, FEW)
                ring[lax.rem(c, RING), here] += norm_backward(grad, scaled, inverse, gain1[...])
        for store in input_stores(c):
            store.start()

        @pl.when(c >= 2)
        def _():
            for store in input_stores(c - 2):
                store.wait()

        @pl.when(c + 2 < chunks)
        def _():
            for load in hidden_loads(c + 2):
                load.start()

    arrival = chunks + travel

    def tick_of(t):
        both_steps(t)

        @pl.when(t >= arrival)
        def _():
            norm_rows(t - arrival)

    for j in range(blocks):
        gradient(j)
        if j == blocks - 1:
            for c in range(2):
                for load in hidden_loads(c):
                    load.start()
            loads[3].wait()
        begin = chunks + j * per_block
        loop(begin, begin + per_block, tick_of if j == blocks - 1 else both_steps)
        if spread:
            if j == 0:
                pair()
            else:
                early_end(j - 1)
            if j < blocks - 1:
                early_begin(j)
            else:
                cross()
    begin = chunks + blocks * per_block
    middle = begin + 2 * per_block
    loop(begin, middle, tick_of)
    if spread:
        for k in range(len(pieces)):
            total_of(k)
        for store in stores:
            store.start()
    loop(middle, arrival + chunks, tick_of)
    for i in range(2):
        late[i : i + 1] = jnp.sum(partial_sums[8 * i : 8 * i + 8], axis=0, keepdims=True)
    if spread:
        for i in range(3):
            late_begin(i)
            late_end(i)
    for c in (chunks - 2, chunks - 1):
        for store in input_stores(c):
            store.wait()
    if spread:
        finish_scatter()
        for store in stores:
            store.wait()
    finish1()
    finish2()


def backward(
    prefix_len, projected, d_bin, b_out, gain1, gain2, mlp_partial, normed1, context, w_qkv, w_out,
    inputs, attn_sum, d_output, summed2,
):
    tokens, depth = inputs.shape
    width = w_out.shape[0]
    spread = (lax.axis_size("dp"), lax.axis_size("col")) == (2, 4)
    dma = pltpu.SemaphoreType.DMA
    buffer = lambda *shape: pltpu.VMEM(shape, jnp.bfloat16)
    wide_buffer = lambda *shape: pltpu.VMEM(shape, jnp.float32)
    single = lambda *shape: jax.ShapeDtypeStruct(shape, jnp.float32)
    sums, scatter_scratch = [single(8, 128), single(8, 128)], []
    if spread:
        block, side = (3, depth // 8, width), (width, depth // 8)
        sums = [single(*block), single(*side)]
        scatter_scratch = [wide_buffer(3, 8, depth), wide_buffer(3, 8, depth)]
        scatter_scratch += [dma((2, 3)), dma((2, 3))]
        for shape in (block, side):
            scatter_scratch += [
                buffer(4, *shape), buffer(4, *shape), buffer(*shape), buffer(2, *shape)
            ]
        scatter_scratch += [wide_buffer(*block), wide_buffer(*side)]
        scatter_scratch += [dma((2,)), dma((4, 8)), dma((4, 8)), dma((8,)), dma((8,))]
        scatter_scratch += [dma((2, 8)), dma((2, 8)), dma((4, 8))]
    out = pl.pallas_call(
        partial(backward_kernel, lax.axis_size("row"), spread),
        out_shape=[
            low_shape(tokens, depth),
            single(tokens, depth),
            single(tokens, depth),
            low_shape(3, depth, width),
            low_shape(width, depth),
            *sums,
            single(8, depth),
            single(8, depth),
        ],
        in_specs=[pl.BlockSpec(memory_space=pltpu.SMEM)] + [IN_VMEM] * 5 + [IN_HBM] * 9,
        out_specs=[IN_HBM] * 7 + [IN_VMEM] * 2,
        scratch_shapes=[
            buffer(tokens, depth),
            buffer(tokens, width),
            buffer(tokens, depth),
            buffer(tokens, width),
            buffer(tokens, depth),
            wide_buffer(tokens, HEAD_DIM),
            wide_buffer(tokens, HEAD_DIM),
            buffer(3, tokens, width),
            buffer(2, TILE, TILE),
            buffer(tokens, depth),
            buffer(*w_qkv.shape),
            wide_buffer(RING, SLICE, depth),
            wide_buffer(32, depth),
            dma((2, tokens // BLOCK)),
            dma((2, 4)),
            dma((5,)),
            dma((2,)),
            dma((RING, 2)),
            dma((RING, 2)),
        ]
        + line_scratch((tokens, depth))
        + line_scratch((tokens, depth))
        + scatter_scratch,
        compiler_params=kernel_params(2, 63),
        cost_estimate=COST,
    )(
        prefix_len, projected, d_bin, b_out[None], gain1[None], gain2[None], mlp_partial, normed1,
        context, w_qkv, w_out, inputs, attn_sum, d_output, summed2,
    )
    mlp_sum, d_inputs, _, d_wqkv, d_wout, sum_wqkv, sum_wout, early, late = out
    if not spread:
        early, late = lax.psum((early, late), ("dp", "col"))
        sum_wqkv, sum_wout = scatter_low(d_wqkv, 1), scatter_low(d_wout, 1)
    return mlp_sum, d_inputs, sum_wqkv, sum_wout, early, late


def scatter_low(grad, dim):
    summed = lax.psum_scatter(grad, ("dp", "col"), scatter_dimension=dim, tiled=True)
    return summed.astype(jnp.float32)


def local(
    inputs,
    prefix_len,
    norm1_gain,
    norm1_shift,
    w_qkv,
    b_qv,
    w_out,
    b_out,
    norm2_gain,
    norm2_shift,
    w_in,
    b_in,
    w_down,
    b_down,
    d_output,
):
    low_mats = (
        w_qkv.astype(jnp.bfloat16),
        w_out.astype(jnp.bfloat16),
        w_in.astype(jnp.bfloat16),
        w_down.astype(jnp.bfloat16),
    )
    full_in, full_down = low_mats[2:]
    source = inputs.astype(jnp.float32)
    if (lax.axis_size("dp"), lax.axis_size("col")) == (2, 4):
        normed1_low, projected, context_low, full_qkv, full_out = head(
            prefix_len, inputs, norm1_gain, norm1_shift, b_qv, low_mats[0], low_mats[1]
        )
    else:
        full_qkv = lax.all_gather(low_mats[0], ("dp", "col"), axis=1, tiled=True)
        full_out = lax.all_gather(low_mats[1], ("dp", "col"), axis=1, tiled=True)
        full_in = lax.all_gather(full_in, ("dp", "col"), axis=0, tiled=True)
        full_down = lax.all_gather(full_down, ("dp", "col"), axis=1, tiled=True)
        normed1, _, _ = norm_forward(source, norm1_gain, norm1_shift)
        normed1_low = normed1.astype(jnp.bfloat16)
        projected = jnp.einsum(
            "td,cdn->ctn", normed1_low, full_qkv, preferred_element_type=jnp.float32
        )
        bias_rows = jnp.stack([b_qv[0], jnp.zeros_like(b_qv[0]), b_qv[1]])
        projected = (projected + bias_rows[:, None, :]).astype(jnp.bfloat16)
        context_low = attend(prefix_len, projected)
    attn_sum, summed2, mlp_partial, grad_wdown, grad_win, grad_bin = mlp_sums(
        context_low, full_out, b_out, norm2_gain, norm2_shift, b_in,
        inputs, full_in, full_down, d_output,
    )
    sent_win = scatter_low(grad_win, 0)
    sent_wdown = scatter_low(grad_wdown, 1)
    mlp_sum, d_inputs, sent_wqkv, sent_wout, early, late = backward(
        prefix_len, projected, grad_bin, b_out, norm1_gain, norm2_gain, mlp_partial, normed1_low,
        context_low, full_qkv, full_out, inputs, attn_sum, d_output, summed2,
    )
    hidden = source + attn_sum.astype(jnp.float32) + b_out
    output = (hidden + mlp_sum.astype(jnp.float32) + b_down).astype(jnp.bfloat16)
    width = b_qv.shape[1]
    return (
        output,
        d_inputs,
        late[0],
        late[1],
        sent_wqkv,
        early[5, : 2 * width].reshape(2, width),
        sent_wout,
        early[0],
        early[1],
        early[2],
        sent_win,
        early[4],
        sent_wdown,
        early[3],
    )


def solution(mesh):
    return jax.shard_map(
        local,
        mesh=mesh,
        in_specs=(
            P(("dp", "col"), None),
            P(("dp", "col")),
            P(),
            P(),
            P(None, ("dp", "col"), "row"),
            P(None, "row"),
            P("row", ("dp", "col")),
            P(),
            P(),
            P(),
            P(("dp", "col"), "row"),
            P("row"),
            P("row", ("dp", "col")),
            P(),
            P(("dp", "col"), None),
        ),
        out_specs=(
            P(("dp", "col"), None),
            P(("dp", "col"), None),
            P(),
            P(),
            P(None, ("dp", "col"), "row"),
            P(None, "row"),
            P("row", ("dp", "col")),
            P(),
            P(),
            P(),
            P(("dp", "col"), "row"),
            P("row"),
            P("row", ("dp", "col")),
            P(),
        ),
        check_vma=False,
    )
```

```python
from functools import partial

import jax
import jax.numpy as jnp
from jax import lax
from jax.experimental import pallas as pl
from jax.experimental.pallas import tpu as pltpu
from jax.sharding import PartitionSpec as P

HEAD_DIM = 128
MESH_IDS = pl.DeviceIdType.MESH
CHUNK = 32
LAG = 2


eps_norm = 1e-05


def norm_forward(values, norm_gain, norm_shift):
    average = jnp.mean(values, axis=-1, keepdims=True)
    centered = values - average
    variance = jnp.mean(centered * centered, axis=-1, keepdims=True)
    inverse = lax.rsqrt(variance + eps_norm)
    scaled = centered * inverse
    return (scaled * norm_gain + norm_shift, scaled, inverse)


def norm_backward(grad, scaled, inverse, norm_gain):
    grad_scaled = grad * norm_gain
    return inverse * (
        grad_scaled
        - jnp.mean(grad_scaled, axis=-1, keepdims=True)
        - scaled * jnp.mean(grad_scaled * scaled, axis=-1, keepdims=True)
    )


def dot(left, right, left_dim, right_dim):
    return lax.dot_general(
        left, right, (((left_dim,), (right_dim,)), ((), ())), preferred_element_type=jnp.float32
    )


def greet_row(n, others=()):
    r = lax.axis_index("row")
    last = n - 1
    bar = pltpu.get_barrier_semaphore()
    for cond, dev in ((r > 0, r - 1), (r < last, r + 1)):

        @pl.when(cond)
        def _():
            pl.semaphore_signal(bar, inc=1, device_id={"row": dev}, device_id_type=MESH_IDS)

    for other in others:
        pl.semaphore_signal(bar, inc=1, device_id=other, device_id_type=MESH_IDS)
    inside = (r > 0) & (r < last)

    @pl.when(inside)
    def _():
        pl.semaphore_wait(bar, 2 + len(others))

    @pl.when(jnp.logical_not(inside))
    def _():
        pl.semaphore_wait(bar, 1 + len(others))


def plane_partners():
    y, x = lax.axis_index("dp"), lax.axis_index("col")
    far_x, near = lax.rem(x + 2, 4), x + 1 - 2 * lax.rem(x, 2)
    far_near = lax.rem(near + 2, 4)
    ids = {"x": {"col": far_x}, "y": {"dp": 1 - y}, "near": {"col": near}}
    mine = {"own": y * 4 + x, "x": y * 4 + far_x, "y": (1 - y) * 4 + x, "xy": (1 - y) * 4 + far_x}
    theirs = {
        "own": y * 4 + near,
        "x": y * 4 + far_near,
        "y": (1 - y) * 4 + near,
        "xy": (1 - y) * 4 + far_near,
    }
    return ids, mine, theirs


KINDS = ("own", "x", "y", "xy")


def plane_gather(pieces, send_sem, recv_sem, near_send, near_recv, local_sem):
    ids, mine, theirs = plane_partners()
    count = len(pieces)

    def remote(kind, k, to, src, dst):
        row = KINDS.index(kind)
        near = to == "near"
        return pltpu.make_async_remote_copy(
            src_ref=src,
            dst_ref=dst,
            send_sem=(near_send if near else send_sem).at[row, k],
            recv_sem=(near_recv if near else recv_sem).at[row, k],
            device_id=ids[to],
            device_id_type=MESH_IDS,
        )

    def outgoing(k):
        own, place = pieces[k](mine["own"])
        return [remote("x", k, "x", own, place), remote("y", k, "y", own, place)]

    def local(k):
        own, place = pieces[k](mine["own"])
        return pltpu.make_async_copy(own, place, local_sem.at[k])

    def onward(k):
        kind, to = ("x", "y") if k % 2 == 0 else ("y", "x")
        place = pieces[k](mine[kind])[1]
        return remote("xy", k, to, place, place)

    def share(kind, k):
        own, place = pieces[k](mine[kind])
        return remote(kind, k, "near", own if kind == "own" else place, place)

    def start():
        for k in range(count):
            for copy in outgoing(k):
                copy.start()
        for k in range(count):
            share("own", k).start()
            local(k).start()

    def arrive(k):
        for copy in outgoing(k):
            copy.wait_recv()
        onward(k).start()
        share("x", k).start()
        share("y", k).start()

    def arrive_far(k):
        onward(k).wait_recv()
        share("xy", k).start()

    def finish():
        for k in range(count):
            local(k).wait()
            for copy in outgoing(k):
                copy.wait_send()
            onward(k).wait_send()
            for kind in KINDS:
                place = pieces[k](theirs[kind])[1]
                share(kind, k).wait_send()
                remote(kind, k, "near", place, place).wait_recv()

    return list(ids.values()), start, arrive, arrive_far, finish


def line_sum(n, p_ref, o_ref, held, rs_s, rs_r, ag_s, ag_r, loc):
    half = o_ref.shape[0] // 2
    chunks = held.shape[0] // 2 // CHUNK
    r = lax.axis_index("row")
    last = n - 1
    place = (r, last - r)
    after = (jnp.minimum(r + 1, last), jnp.maximum(r - 1, 0))
    before = (jnp.maximum(r - 1, 0), jnp.minimum(r + 1, last))

    def rows(d, c):
        return pl.ds(pl.multiple_of((half if d == 0 else 0) + c * CHUNK, CHUNK), CHUNK)

    def slot(d, c):
        return pl.ds(pl.multiple_of((1 - d) * chunks * CHUNK + c * CHUNK, CHUNK), CHUNK)


    def onward(d, c, src):
        return pltpu.make_async_remote_copy(
            src_ref=src.at[rows(d, c) if src is p_ref else slot(d, c)],
            dst_ref=held.at[slot(d, c)],
            send_sem=rs_s.at[d, c],
            recv_sem=rs_r.at[d, c],
            device_id={"row": after[d]},
            device_id_type=MESH_IDS,
        )

    def back(d, c, src):
        return pltpu.make_async_remote_copy(
            src_ref=src.at[slot(d, c) if src is held else rows(d, c)],
            dst_ref=o_ref.at[rows(d, c)],
            send_sem=ag_s.at[d, c],
            recv_sem=ag_r.at[d, c],
            device_id={"row": before[d]},
            device_id_type=MESH_IDS,
        )

    def keep(d, c):
        return pltpu.make_async_copy(held.at[slot(d, c)], o_ref.at[rows(d, c)], loc.at[c])

    def step(t):
        for d in (0, 1):

            @pl.when((place[d] == 0) & (t >= 0) & (t < chunks))
            def _():
                onward(d, t, p_ref).start()

            c = t - LAG * place[d]

            @pl.when((place[d] > 0) & (c >= 0) & (c < chunks))
            def _():
                onward(d, c, p_ref).wait_recv()
                here = slot(d, c)
                held[here] = (
                    held[here].astype(jnp.float32) + p_ref[rows(d, c)].astype(jnp.float32)
                ).astype(jnp.bfloat16)

                @pl.when(place[d] < last)
                def _():
                    onward(d, c, held).start()

                @pl.when(place[d] == last)
                def _():
                    back(d, c, held).start()
                    keep(d, c).start()

        for d in (0, 1):
            c = t - LAG * (2 * last - place[d])

            @pl.when((place[d] < last) & (c >= 0) & (c < chunks))
            def _():
                back(d, c, o_ref).wait_recv()

                @pl.when(place[d] > 0)
                def _():
                    back(d, c, o_ref).start()

    def settle(c):
        for d in (0, 1):

            @pl.when(place[d] < last)
            def _():
                onward(d, c, p_ref).wait_send()

            @pl.when(place[d] == last)
            def _():
                keep(d, c).wait()

    def finish(c):
        for d in (0, 1):

            @pl.when(place[d] > 0)
            def _():
                back(d, c, o_ref).wait_send()

    def drain():
        def both(c):
            settle(c)
            finish(c)

        loop(0, chunks, both)

    return step, drain, settle, lambda: loop(0, chunks, finish)


def line_steps(n, total_rows):
    return total_rows // 2 // CHUNK + LAG * 2 * (n - 1)


def line_scratch(shape):
    chunks = shape[0] // 2 // CHUNK
    dma = pltpu.SemaphoreType.DMA
    return [
        pltpu.VMEM(shape, jnp.bfloat16),
        dma((2, chunks)),
        dma((2, chunks)),
        dma((2, chunks)),
        dma((2, chunks)),
        dma((chunks,)),
    ]


def loop(start, stop, body):
    def one(t, carry):
        body(t)
        return carry

    lax.fori_loop(start, stop, one, 0)


COST = pl.CostEstimate(flops=1000, bytes_accessed=1000, transcendentals=0)
IN_VMEM = pl.BlockSpec(memory_space=pltpu.VMEM)
IN_HBM = pl.BlockSpec(memory_space=pl.ANY)


def low_shape(*shape):
    return jax.ShapeDtypeStruct(shape, jnp.bfloat16)


def kernel_params(collective_id, mib):
    return pltpu.CompilerParams(
        collective_id=collective_id, has_side_effects=True, vmem_limit_bytes=mib * 2**20
    )


TILE = 512
FEW = 16
BLOCK = 256


def mlp_sums_kernel(
    n, spread, ctx, w_out, b_out, gain, shift, b_in, src_hbm, w_in_hbm, w_down_hbm, g_hbm,
    branch, d_normed, mlp, d_wdown, d_win, d_bin,
    p, w_in, w_down, g, normed, act, d_pre, mlp_acc, d_acc, rows_a, rows_b, stage, w_stage,
    load_sem, block_sem, mlp_sem, store_sem, *more,
):
    tokens, depth = p.shape
    units = act.shape[1]
    half = tokens // 2
    part = BLOCK // 2
    blocks = tokens // BLOCK
    per_block = part // CHUNK
    quarters = units // TILE

    def sides(j):
        low_rows = pl.ds(pl.multiple_of(j * part, part), part)
        high_rows = pl.ds(pl.multiple_of(half + j * part, part), part)
        return low_rows, high_rows

    def own(j, side=None):
        if side is None:
            return pl.ds(pl.multiple_of(j * BLOCK, BLOCK), BLOCK)
        return pl.ds(pl.multiple_of(j * BLOCK + side * part, part), part)

    lines, gather_sems = more[:12], more[12:]
    loads = []
    others = []
    if spread:
        deep, wide = w_in_hbm.shape[0], w_down_hbm.shape[1]

        def in_piece(k, place):
            size = deep // 2
            there = pl.ds(pl.multiple_of(place * deep + k * size, size), size)
            return w_in_hbm.at[pl.ds(k * size, size)], w_in.at[there]

        def down_piece(k, place):
            some = pl.ds(k * (units // 2), units // 2)
            cols = pl.ds(pl.multiple_of(place * wide, wide), wide)
            return w_down_hbm.at[some], w_down.at[some, cols]

        pieces = [partial(f, k) for f in (in_piece, down_piece) for k in range(2)]
        others, start_gather, arrive, arrive_far, finish_gather = plane_gather(
            pieces, *gather_sems
        )
    else:
        loads = [
            pltpu.make_async_copy(w_in_hbm, w_in, load_sem.at[0]),
            pltpu.make_async_copy(w_down_hbm, w_down, load_sem.at[1]),
        ]
    for j in range(blocks):
        for side, here in enumerate((j * part, half + j * part)):
            loads.append(
                pltpu.make_async_copy(
                    g_hbm.at[pl.ds(here, part)],
                    g.at[pl.ds(j * BLOCK + side * part, part)],
                    load_sem.at[2 + 2 * j + side],
                )
            )
    for load in loads:
        load.start()
    d_bin[...] = jnp.zeros_like(d_bin)
    greet_row(n, others)
    if spread:
        start_gather()
    step1, _, settle1, finish1 = line_sum(n, p, branch, *lines[:6])
    step2, drain2, _, _ = line_sum(n, p, d_normed, *lines[6:])

    def project(j):
        low_rows, high_rows = sides(j)
        both = jnp.concatenate([ctx[low_rows], ctx[high_rows]], axis=0)
        for c in range(0, depth, TILE):
            cols = slice(c, c + TILE)
            term = dot(both, w_out[:, cols], 1, 0).astype(jnp.bfloat16)
            p[low_rows, cols] = term[:part]
            p[high_rows, cols] = term[part:]
        loop(j * per_block, (j + 1) * per_block, step1)

    for j in range(blocks):
        project(j)
        if spread and j == blocks - 2:
            for k in range(len(pieces)):
                arrive(k)
    if spread:
        for k in range(len(pieces)):
            arrive_far(k)
        finish_gather()
    for load in loads:
        load.wait()

    def norm_block(j):
        loop(j * per_block, (j + 1) * per_block, settle1)
        copies = []
        for i, (src, dst) in enumerate(((branch, rows_a), (src_hbm, rows_b))):
            for side, here in enumerate(sides(j)):
                copies.append(
                    pltpu.make_async_copy(
                        src.at[here], dst.at[pl.ds(side * part, part)], block_sem.at[i, side]
                    )
                )
        for copy in copies:
            copy.start()
        for copy in copies:
            copy.wait()

        def few(k):
            here = pl.ds(pl.multiple_of(k * 64, 64), 64)
            there = pl.ds(pl.multiple_of(j * BLOCK + k * 64, 64), 64)
            source = rows_b[here].astype(jnp.float32)
            hidden = source + rows_a[here].astype(jnp.float32) + b_out[...]
            normed[there] = norm_forward(hidden, gain[...], shift[...])[0].astype(jnp.bfloat16)

        loop(0, BLOCK // 64, few)

    def mlp_out(j):
        return [
            pltpu.make_async_copy(
                stage.at[pl.ds(side * part, part)], mlp.at[here], mlp_sem.at[side]
            )
            for side, here in enumerate(sides(j))
        ]

    first = tokens // 2 // CHUNK

    def block(j):
        for q in range(quarters):
            t = first + j * per_block + q
            step1(t)
            step2(t - first - per_block)
            if q == 0:
                norm_block(j)
            units_q = slice(q * TILE, (q + 1) * TILE)
            here = own(j)
            pre = dot(normed[here], w_in[:, units_q], 1, 0) + b_in[:, units_q]
            d_act = dot(g[here], w_down[units_q], 1, 1)
            lower = 0.5 * (1.0 + lax.erf(pre * 0.5**0.5))
            act[here, units_q] = (pre * lower).astype(jnp.bfloat16)
            slope = lower + pre * (jnp.exp(-0.5 * pre * pre) * (0.5 / jnp.pi) ** 0.5)
            low_pre = (d_act * slope).astype(jnp.bfloat16)
            d_pre[here, units_q] = low_pre
            d_bin[:, units_q] += jnp.sum(low_pre.astype(jnp.float32), axis=0, keepdims=True)
            for c in range(0, depth, TILE):
                cols = slice(c, c + TILE)
                m_term = dot(act[here, units_q], w_down[units_q, cols], 1, 0)
                d_term = dot(d_pre[here, units_q], w_in[cols, units_q], 1, 1)
                if q == 0:
                    mlp_acc[:, cols] = m_term
                    d_acc[:, cols] = d_term
                elif q < quarters - 1:
                    mlp_acc[:, cols] += m_term
                    d_acc[:, cols] += d_term
                else:
                    if c == 0:

                        @pl.when(j > 0)
                        def _():
                            for copy in mlp_out(j - 1):
                                copy.wait()

                    stage[:, cols] = (mlp_acc[:, cols] + m_term).astype(jnp.bfloat16)
                    d_low = (d_acc[:, cols] + d_term).astype(jnp.bfloat16)
                    for side, rows in enumerate(sides(j)):
                        p[rows, cols] = d_low[side * part : (side + 1) * part]
        for copy in mlp_out(j):
            copy.start()

    loop(0, blocks, block)
    begin = first
    steps = line_steps(n, tokens)
    tick = tokens // 2 // CHUNK - per_block
    jobs = ((act, g, d_wdown), (normed, d_pre, d_win))
    for k, (left, right, out) in enumerate(jobs):
        across = out.shape[1] // TILE
        tiles = (out.shape[0] // TILE) * across

        def store(tile, slot):
            m = pl.ds(pl.multiple_of((tile // across) * TILE, TILE), TILE)
            c = pl.ds(pl.multiple_of(lax.rem(tile, across) * TILE, TILE), TILE)
            copy = pltpu.make_async_copy(w_stage.at[slot], out.at[m, c], store_sem.at[slot])
            return m, c, copy

        def body(u):
            step2(tick + k * (tiles // 2) + u)
            for slot in range(2):
                m, c, copy = store(2 * u + slot, slot)
                if k == 0:

                    @pl.when(u > 0)
                    def _():
                        copy.wait()
                else:
                    copy.wait()
                w_stage[slot] = dot(left[:, m], right[:, c], 0, 0).astype(jnp.bfloat16)
                copy.start()

        loop(0, tiles // 2, body)
        tick_end = tick + (k + 1) * (tiles // 2)
    if tick_end < steps:
        loop(tick_end, steps, step2)
    for slot in range(2):
        store(slot, slot)[2].wait()
    for copy in mlp_out(blocks - 1):
        copy.wait()
    finish1()
    drain2()


def mlp_sums(context, w_out, b_out, gain, shift, b_in, inputs, w_in, w_down, d_output):
    tokens, depth = inputs.shape
    units = w_in.shape[1]
    spread = w_in.shape[0] < depth
    dma = pltpu.SemaphoreType.DMA
    low_buffer = lambda *shape: pltpu.VMEM(shape, jnp.bfloat16)
    return pl.pallas_call(
        partial(mlp_sums_kernel, lax.axis_size("row"), spread),
        out_shape=[
            low_shape(tokens, depth),
            low_shape(tokens, depth),
            low_shape(tokens, depth),
            low_shape(units, depth),
            low_shape(depth, units),
            jax.ShapeDtypeStruct((1, units), jnp.float32),
        ],
        in_specs=[IN_VMEM] * 6 + [IN_HBM] * 4,
        out_specs=[IN_HBM] * 5 + [IN_VMEM],
        scratch_shapes=[
            low_buffer(tokens, depth),
            low_buffer(depth, units),
            low_buffer(units, depth),
            low_buffer(tokens, depth),
            low_buffer(tokens, depth),
            low_buffer(tokens, units),
            low_buffer(tokens, units),
            pltpu.VMEM((BLOCK, depth), jnp.float32),
            pltpu.VMEM((BLOCK, depth), jnp.float32),
            low_buffer(BLOCK, depth),
            low_buffer(BLOCK, depth),
            low_buffer(BLOCK, depth),
            low_buffer(2, TILE, TILE),
            dma((2 + 2 * (tokens // BLOCK),)),
            dma((2, 2)),
            dma((2,)),
            dma((2,)),
        ]
        + line_scratch((tokens, depth))
        + line_scratch((tokens, depth))
        + ([dma((4, 4))] * 4 + [dma((4,))] if spread else []),
        compiler_params=kernel_params(1, 61),
        cost_estimate=COST,
    )(
        context, w_out, b_out[None], gain[None], shift[None], b_in[None],
        inputs, w_in, w_down, d_output,
    )


QUERY_ROWS = 256


def head_kernel(
    prefix_ref, src, gain, shift, b_q, b_v, w_qkv_hbm, w_out_hbm,
    normed_out, projected_out, context_out, full_qkv, full_out,
    weights, w_out, normed, projected, context, store_sem, *sems,
):
    tokens, depth = src.shape
    width = projected.shape[2]
    deep, wide = w_qkv_hbm.shape[1], w_out_hbm.shape[1]
    size, tall = deep // 2, width // 2

    def qkv_piece(c, k, place):
        there = pl.ds(pl.multiple_of(place * deep + k * size, size), size)
        return w_qkv_hbm.at[c, pl.ds(k * size, size)], weights.at[c, there]

    def out_piece(k, place):
        some = pl.ds(k * tall, tall)
        cols = pl.ds(pl.multiple_of(place * wide, wide), wide)
        return w_out_hbm.at[some], w_out.at[some, cols]

    parts = [[partial(qkv_piece, c, k) for k in range(2)] for c in range(3)]
    parts.append([partial(out_piece, k) for k in range(2)])
    others = list(plane_partners()[0].values())
    start, arrive, far, finish = zip(
        *[plane_gather(part, *sems[5 * i : 5 * i + 5])[1:] for i, part in enumerate(parts)]
    )
    bar = pltpu.get_barrier_semaphore()
    for other in others:
        pl.semaphore_signal(bar, inc=1, device_id=other, device_id_type=MESH_IDS)
    pl.semaphore_wait(bar, len(others))
    start[0]()
    start[1]()

    def few(r):
        here = pl.ds(pl.multiple_of(r * FEW, FEW), FEW)
        rows = norm_forward(src[here].astype(jnp.float32), gain[...], shift[...])[0]
        normed[here] = rows.astype(jnp.bfloat16)

    loop(0, tokens // FEW // 4, lambda r: [few(4 * r + i) for i in range(4)])
    stores = [
        pltpu.make_async_copy(src, dst, store_sem.at[i])
        for i, (src, dst) in enumerate(
            (
                (normed, normed_out),
                (weights, full_qkv),
                (projected, projected_out),
                (w_out, full_out),
                (context, context_out),
            )
        )
    ]
    stores[0].start()
    for i in range(2):
        for k in range(2):
            arrive[i](k)
    start[2]()
    for c in range(3):
        if c == 2:
            for k in range(2):
                arrive[2](k)
            start[3]()
        for k in range(2):
            far[c](k)
        finish[c]()

        def rows_of(i):
            here = pl.ds(pl.multiple_of(i * BLOCK, BLOCK), BLOCK)
            term = dot(normed[here], weights[c], 1, 0)
            if c != 1:
                term += (b_q if c == 0 else b_v)[...]
            projected[c, here] = term.astype(jnp.bfloat16)

        loop(0, tokens // BLOCK, rows_of)
    stores[1].start()
    stores[2].start()
    for k in range(2):
        arrive[3](k)
    attend_kernel(prefix_ref, projected, context)
    stores[4].start()
    for k in range(2):
        far[3](k)
    finish[3]()
    stores[3].start()
    for store in stores:
        store.wait()


def head(prefix_len, inputs, gain, shift, b_qv, w_qkv, w_out):
    tokens, depth = inputs.shape
    width = w_out.shape[0]
    dma = pltpu.SemaphoreType.DMA
    return pl.pallas_call(
        head_kernel,
        out_shape=[
            low_shape(tokens, depth),
            low_shape(3, tokens, width),
            low_shape(tokens, width),
            low_shape(3, depth, width),
            low_shape(width, depth),
        ],
        in_specs=[pl.BlockSpec(memory_space=pltpu.SMEM)] + [IN_VMEM] * 5 + [IN_HBM] * 2,
        out_specs=[IN_HBM] * 5,
        scratch_shapes=[
            pltpu.VMEM((3, depth, width), jnp.bfloat16),
            pltpu.VMEM((width, depth), jnp.bfloat16),
            pltpu.VMEM((tokens, depth), jnp.bfloat16),
            pltpu.VMEM((3, tokens, width), jnp.bfloat16),
            pltpu.VMEM((tokens, width), jnp.bfloat16),
            dma((5,)),
        ]
        + ([dma((4, 2))] * 4 + [dma((2,))]) * 4,
        compiler_params=kernel_params(3, 40),
        cost_estimate=COST,
    )(prefix_len, inputs, gain[None], shift[None], b_qv[:1], b_qv[1:], w_qkv, w_out)


def block_probs(i, prefix, cols, q, k):
    start = i * QUERY_ROWS
    width = max(start + QUERY_ROWS, q.shape[0] // 2)
    here = slice(start, start + QUERY_ROWS)
    scores = dot(k[:width, cols], q[here, cols], 1, 1) * HEAD_DIM ** (-0.5)
    key = lax.broadcasted_iota(jnp.int32, scores.shape, 0)
    query = lax.broadcasted_iota(jnp.int32, scores.shape, 1) + start
    scores = jnp.where((key <= query) | (key < prefix), scores, -1000000000.0)
    expo = jnp.exp(scores - jnp.max(scores, axis=0, keepdims=True))
    return here, width, expo * (1.0 / jnp.sum(expo, axis=0, keepdims=True))


def attend_kernel(prefix_ref, projected, context):
    q, k, v = (projected.at[c] for c in range(3))
    prefix = prefix_ref[0]

    def head(h):
        cols = pl.ds(pl.multiple_of(h * HEAD_DIM, HEAD_DIM), HEAD_DIM)
        v_t = v[:, cols].T
        for i in range(q.shape[0] // QUERY_ROWS):
            here, width, probs = block_probs(i, prefix, cols, q, k)
            out = dot(v_t[:, :width], probs.astype(jnp.bfloat16), 1, 0)
            context[here, cols] = out.T.astype(jnp.bfloat16)

    loop(0, q.shape[1] // HEAD_DIM, head)


def attend(prefix_len, projected):
    return pl.pallas_call(
        attend_kernel,
        out_shape=low_shape(*projected.shape[1:]),
        in_specs=[pl.BlockSpec(memory_space=pltpu.SMEM), IN_VMEM],
        out_specs=IN_VMEM,
        compiler_params=pltpu.CompilerParams(vmem_limit_bytes=32 * 2**20),
        cost_estimate=COST,
    )(prefix_len, projected)


def attend_piece(i, prefix, cols, q, k, v, k_t, d_context, d_proj, d_key, d_value, first):
    score_scale = HEAD_DIM ** (-0.5)
    here, width, probs = block_probs(i, prefix, cols, q, k)
    q_block, g_block = q[here, cols], d_context[here, cols]
    d_probs = dot(v[:width, cols], g_block, 1, 1)
    inner = jnp.sum(d_probs * probs, axis=0, keepdims=True)
    d_scores = (probs * (d_probs - inner)).astype(jnp.bfloat16)
    d_query = dot(k_t[:, :width], d_scores, 1, 0) * score_scale
    d_proj[0, here, cols] = d_query.T.astype(jnp.bfloat16)
    for total, term in (
        (d_key, dot(d_scores, q_block, 1, 0)),
        (d_value, dot(probs.astype(jnp.bfloat16), g_block, 1, 0)),
    ):
        if first:
            total[...] = term
        else:
            total[:width] += term


def plane_scatter(pieces, sems):
    ids, mine, theirs = plane_partners()
    near_send, near_recv, far_send, far_recv, last_send, last_recv, load_sem = sems
    count = len(pieces)

    def remote(src, dst, send, recv, to):
        return pltpu.make_async_remote_copy(
            src_ref=src,
            dst_ref=dst,
            send_sem=send,
            recv_sem=recv,
            device_id=ids[to],
            device_id_type=MESH_IDS,
        )

    def near(i, k):
        block, to, _, _, _ = pieces[k]
        place = theirs[KINDS[i]]
        return remote(block(place), to(i), near_send.at[i, k], near_recv.at[i, k], "near")

    def load(i, k):
        block, _, own, _, _ = pieces[k]
        return pltpu.make_async_copy(block(mine[KINDS[i]]), own(i), load_sem.at[i, k])

    def far(k):
        _, _, own, to, _ = pieces[k]
        return remote(own(3), to(), far_send.at[k], far_recv.at[k], "x" if k % 2 == 0 else "y")

    def last(i, k):
        _, _, own, _, to = pieces[k]
        return remote(
            own(i), to(i - 1), last_send.at[i - 1, k], last_recv.at[i - 1, k], KINDS[i]
        )

    def add(target, term):
        flat = target.shape[0]

        def some(r):
            here = pl.ds(pl.multiple_of(r * 128, 128), 128)
            target[here] = (
                target[here].astype(jnp.float32) + term[here].astype(jnp.float32)
            ).astype(jnp.bfloat16)

        loop(0, flat // 128, some)

    def start():
        for i in (3, 1, 2, 0):
            for k in range(count):
                near(i, k).start()
                load(i, k).start()

    def pair():
        for i in (3, 1, 2, 0):
            for k in range(count):
                near(i, k).wait_recv()
                load(i, k).wait()
                add(pieces[k][2](i), pieces[k][1](i))
                if i == 3:
                    far(k).start()
                elif i == 1 + k % 2:
                    last(i, k).start()

    def cross():
        for k in range(count):
            far(k).wait_recv()
            i = 2 - k % 2
            add(pieces[k][2](i), pieces[k][3]())
            last(i, k).start()

    def collect(k):
        for i in (1, 2):
            last(i, k).wait_recv()
        return pieces[k][2](0), pieces[k][4](0), pieces[k][4](1)

    def finish():
        for k in range(count):
            for i in range(4):
                near(i, k).wait_send()
            far(k).wait_send()
            for i in (1, 2):
                last(i, k).wait_send()

    return start, pair, cross, collect, finish


def sums_out(kind, vectors, slots, send_sem, recv_sem):
    ids = plane_partners()[0]

    def copy(i):
        return pltpu.make_async_remote_copy(
            src_ref=vectors,
            dst_ref=slots.at[i],
            send_sem=send_sem.at[kind, i],
            recv_sem=recv_sem.at[kind, i],
            device_id=ids[("near", "x", "y")[i]],
            device_id_type=MESH_IDS,
        )

    def begin(i):
        copy(i).start()

    def end(i):
        copy(i).wait()
        vectors[...] += slots[i]

    return begin, end


SLICE = 64
RING = 4


def backward_kernel(
    n, spread, prefix_ref, projected, d_bin, b_out, gain1, gain2,
    mlp_hbm, n1_hbm, ctx_hbm, w_qkv_hbm, w_out_hbm, src_hbm, attn_hbm, g_hbm, dn2_hbm,
    mlp_sum, d_inputs, d_hidden, d_wqkv, d_wout, sum_wqkv, sum_wout, early, late,
    p, d_context, n1, ctx, branch, d_key, d_value, d_proj, w_stage, total, weights, ring, partial_sums,
    p_sem, slice_sem, load_sem, store_sem, ring_in, ring_out, *more,
):
    lines, more = more[:12], more[12:]
    tokens, depth = p.shape
    width = projected.shape[2]
    half = tokens // 2
    chunks = half // CHUNK
    blocks = tokens // BLOCK
    part = BLOCK // 2
    per_block = part // CHUNK
    travel = LAG * 2 * (n - 1)
    prefix = prefix_ref[0]

    def sides(j, size):
        return (
            pl.ds(pl.multiple_of(j * size, size), size),
            pl.ds(pl.multiple_of(half + j * size, size), size),
        )

    p_loads = [
        [
            pltpu.make_async_copy(mlp_hbm.at[rows], p.at[rows], p_sem.at[side, j])
            for side, rows in enumerate((pl.ds(j * part, part), pl.ds(half + j * part, part)))
        ]
        for j in range(blocks)
    ]
    for loads in p_loads:
        for load in loads:
            load.start()
    w_out_load = pltpu.make_async_copy(w_out_hbm, total.at[pl.ds(0, width)], load_sem.at[0])
    w_out_load.start()
    loads = [
        pltpu.make_async_copy(src, dst, load_sem.at[1 + i])
        for i, (src, dst) in enumerate(
            ((n1_hbm, n1), (ctx_hbm, ctx), (w_qkv_hbm, weights), (src_hbm, n1))
        )
    ]
    early[...] = jnp.zeros_like(early)
    late[...] = jnp.zeros_like(late)
    early[4:5] = d_bin[...]
    partial_sums[...] = jnp.zeros_like(partial_sums)
    others = []
    if spread:
        slots_e, slots_l, small_s, small_r = more[:4]
        qkv_near, qkv_own, qkv_far, qkv_last, out_near, out_own, out_far, out_last = more[4:12]
        qkv_sum, out_sum, sum_sem = more[12:15]
        others = list(plane_partners()[0].values())
        early_begin, early_end = sums_out(0, early, slots_e, small_s, small_r)
        late_begin, late_end = sums_out(1, late, slots_l, small_s, small_r)
        places = 8
        deep, wide = depth // places, depth // places
        size = deep // 2
        tall = width // 2

        def qkv_piece(c, k):
            def block(place):
                there = pl.ds(pl.multiple_of(place * deep + k * size, size), size)
                return d_wqkv.at[c, there]

            some = pl.ds(k * size, size)
            return (
                block,
                lambda i: qkv_near.at[i, c, some],
                lambda i: qkv_own.at[i, c, some],
                lambda: qkv_far.at[c, some],
                lambda i: qkv_last.at[i, c, some],
            )

        def out_piece(k):
            some = pl.ds(k * tall, tall)

            def block(place):
                cols = pl.ds(pl.multiple_of(place * wide, wide), wide)
                return d_wout.at[some, cols]

            return (
                block,
                lambda i: out_near.at[i, some],
                lambda i: out_own.at[i, some],
                lambda: out_far.at[some],
                lambda i: out_last.at[i, some],
            )

        pieces = [qkv_piece(c, k) for c in range(3) for k in range(2)]
        pieces += [out_piece(k) for k in range(2)]
        start_scatter, pair, cross, collect, finish_scatter = plane_scatter(pieces, more[15:])
        stores = [
            pltpu.make_async_copy(qkv_sum, sum_wqkv, sum_sem.at[0]),
            pltpu.make_async_copy(out_sum, sum_wout, sum_sem.at[1]),
        ]

        def total_of(k):
            own, one, two = collect(k)
            if k < 6:
                target = qkv_sum.at[k // 2, pl.ds((k % 2) * size, size)]
            else:
                target = out_sum.at[pl.ds((k % 2) * tall, tall)]

            def some(r):
                here = pl.ds(pl.multiple_of(r * 128, 128), 128)
                target[here] = (
                    own[here].astype(jnp.float32)
                    + one[here].astype(jnp.float32)
                    + two[here].astype(jnp.float32)
                )

            loop(0, target.shape[0] // 128, some)

    greet_row(n, others)
    step1, _, settle1, finish1 = line_sum(n, p, mlp_sum, *lines[:6])
    step2, _, settle2, finish2 = line_sum(n, p, total, *lines[6:])

    def both_steps(t):
        step1(t)
        step2(t - chunks)

    slices = tokens // SLICE

    def slice_rows(k):
        return pl.ds(pl.multiple_of(k * SLICE, SLICE), SLICE)

    def slice_slot(k, i):
        return pl.ds(pl.multiple_of(half + (lax.rem(k, 2) * 4 + i) * SLICE, SLICE), SLICE)

    def slice_loads(k):
        return [
            pltpu.make_async_copy(
                src.at[slice_rows(k)], total.at[slice_slot(k, i)], slice_sem.at[lax.rem(k, 2), i]
            )
            for i, src in enumerate((dn2_hbm, attn_hbm, src_hbm, g_hbm))
        ]

    def hidden_store(k):
        return pltpu.make_async_copy(
            ring.at[lax.rem(k, RING)], d_hidden.at[slice_rows(k)], ring_out.at[lax.rem(k, RING), 0]
        )

    def norm_slice(k):
        @pl.when(k + 1 < slices)
        def _():
            for load in slice_loads(k + 1):
                load.start()

        for load in slice_loads(k):
            load.wait()

        @pl.when(k >= RING)
        def _():
            hidden_store(k - RING).wait()

        def few(r):
            rows = [
                pl.ds(pl.multiple_of(half + (lax.rem(k, 2) * 4 + i) * SLICE + r * FEW, FEW), FEW)
                for i in range(4)
            ]
            dn, attn, source, g = (total[some].astype(jnp.float32) for some in rows)
            _, scaled, inverse = norm_forward(source + attn + b_out[...], 1.0, 0.0)
            grad = g + norm_backward(dn, scaled, inverse, gain2[...])
            low = grad.astype(jnp.bfloat16)
            branch[pl.ds(pl.multiple_of(k * SLICE + r * FEW, FEW), FEW)] = low
            for i, term in enumerate((low.astype(jnp.float32), dn * scaled, dn, g)):
                partial_sums[8 * i : 8 * i + 8] += term[:8] + term[8:]
            ring[lax.rem(k, RING), pl.ds(pl.multiple_of(r * FEW, FEW), FEW)] = grad

        for r in range(SLICE // FEW):
            few(r)
        hidden_store(k).start()

    for load in slice_loads(0):
        load.start()
    norm_ticks = 4
    for load in p_loads[0]:
        load.wait()

    def norm_tick(t):
        step1(t)
        loop(t * (slices // norm_ticks), (t + 1) * (slices // norm_ticks), norm_slice)

    loop(0, norm_ticks, norm_tick)
    for i in range(4):
        early[i : i + 1] = jnp.sum(partial_sums[8 * i : 8 * i + 8], axis=0, keepdims=True)
    for k in range(slices - RING, slices):
        hidden_store(k).wait()
    for some in p_loads[1:]:
        for load in some:
            load.wait()
    for load in loads[:3]:
        load.start()
    w_out_load.wait()

    def context_rows(i):
        rows = pl.ds(pl.multiple_of(i * BLOCK, BLOCK), BLOCK)
        d_context[rows] = dot(branch[rows], total[:width], 1, 1).astype(jnp.bfloat16)

    loop(0, tokens // BLOCK, context_rows)
    partial_sums[...] = jnp.zeros_like(partial_sums)

    q, k, v = (projected.at[c] for c in range(3))
    q_blocks = tokens // QUERY_ROWS
    heads = width // HEAD_DIM
    head_ticks = q_blocks // 2

    def head(h):
        cols = pl.ds(pl.multiple_of(h * HEAD_DIM, HEAD_DIM), HEAD_DIM)
        k_t = k[:, cols].T
        for j in range(q_blocks):
            if j % 2 == 0:
                step1(norm_ticks + h * head_ticks + j // 2)
            attend_piece(
                q_blocks - 1 - j, prefix, cols, q, k, v, k_t, d_context, d_proj, d_key, d_value,
                j == 0,
            )
        d_proj[1, :, cols] = (d_key[...] * HEAD_DIM ** (-0.5)).astype(jnp.bfloat16)
        d_proj[2, :, cols] = d_value[...].astype(jnp.bfloat16)

    loop(0, heads, head)
    for b, c in ((0, 0), (1, 2)):
        early[5:6, b * width : (b + 1) * width] = jnp.sum(
            d_proj[c].astype(jnp.float32), axis=0, keepdims=True
        )
    for load in loads[:3]:
        load.wait()
    tick = norm_ticks + heads * head_ticks
    tiles = depth // TILE

    def tile_store(c, m):
        some = pl.ds(m * TILE, TILE)
        out = d_wqkv.at[c, some] if c < 3 else d_wout.at[:, some]
        return pltpu.make_async_copy(w_stage.at[m % 2], out, store_sem.at[m % 2])

    for c in range(4):
        step1(tick + c)
        for m in range(tiles):
            some = slice(m * TILE, (m + 1) * TILE)
            if c or m > 1:
                before = (c, m - 2) if m > 1 else (c - 1, tiles + m - 2)
                tile_store(*before).wait()
            if c < 3:
                term = dot(n1[:, some], d_proj[c], 0, 0)
            else:
                term = dot(ctx[...], branch[:, some], 0, 0)
            w_stage[m % 2] = term.astype(jnp.bfloat16)
            tile_store(c, m).start()
    for m in (tiles - 2, tiles - 1):
        tile_store(3, m).wait()
    loads[3].start()
    if tick + 4 < chunks:
        loop(tick + 4, chunks, step1)
    if spread:
        start_scatter()

    def gradient(j):
        loop(j * per_block, (j + 1) * per_block, settle1)
        low_rows, high_rows = sides(j, part)
        rows = [
            jnp.concatenate([d_proj[c, low_rows], d_proj[c, high_rows]], axis=0) for c in range(3)
        ]
        for i in range(0, depth, TILE):
            cols = slice(i, i + TILE)
            term = dot(rows[0], weights[0, cols], 1, 1)
            for c in (1, 2):
                term += dot(rows[c], weights[c, cols], 1, 1)
            term = term.astype(jnp.bfloat16)
            p[low_rows, cols] = term[:part]
            p[high_rows, cols] = term[part:]

    def hidden_loads(c):
        return [
            pltpu.make_async_copy(
                d_hidden.at[rows],
                ring.at[lax.rem(c, RING), pl.ds(side * CHUNK, CHUNK)],
                ring_in.at[lax.rem(c, RING), side],
            )
            for side, rows in enumerate(sides(c, CHUNK))
        ]

    def input_stores(c):
        return [
            pltpu.make_async_copy(
                ring.at[lax.rem(c, RING), pl.ds(side * CHUNK, CHUNK)],
                d_inputs.at[rows],
                ring_out.at[lax.rem(c, RING), side],
            )
            for side, rows in enumerate(sides(c, CHUNK))
        ]

    def norm_rows(c):
        settle2(c)
        for load in hidden_loads(c):
            load.wait()
        for side, rows in enumerate(sides(c, CHUNK)):
            for r in range(CHUNK // FEW):
                some = pl.ds(pl.multiple_of(rows.start + r * FEW, FEW), FEW)
                _, scaled, inverse = norm_forward(n1[some].astype(jnp.float32), 1.0, 0.0)
                grad = total[some].astype(jnp.float32)
                for i, term in enumerate((grad * scaled, grad)):
                    partial_sums[8 * i : 8 * i + 8] += term[:8] + term[8:]
                here = pl.ds(side * CHUNK + r * FEW, FEW)
                ring[lax.rem(c, RING), here] += norm_backward(grad, scaled, inverse, gain1[...])
        for store in input_stores(c):
            store.start()

        @pl.when(c >= 2)
        def _():
            for store in input_stores(c - 2):
                store.wait()

        @pl.when(c + 2 < chunks)
        def _():
            for load in hidden_loads(c + 2):
                load.start()

    arrival = chunks + travel

    def tick_of(t):
        both_steps(t)

        @pl.when(t >= arrival)
        def _():
            norm_rows(t - arrival)

    for j in range(blocks):
        gradient(j)
        if j == blocks - 1:
            for c in range(2):
                for load in hidden_loads(c):
                    load.start()
            loads[3].wait()
        begin = chunks + j * per_block
        loop(begin, begin + per_block, tick_of if j == blocks - 1 else both_steps)
        if spread:
            if j == 0:
                pair()
            else:
                early_end(j - 1)
            if j < blocks - 1:
                early_begin(j)
            else:
                cross()
    begin = chunks + blocks * per_block
    middle = begin + 2 * per_block
    loop(begin, middle, tick_of)
    if spread:
        for k in range(len(pieces)):
            total_of(k)
        for store in stores:
            store.start()
    loop(middle, arrival + chunks, tick_of)
    for i in range(2):
        late[i : i + 1] = jnp.sum(partial_sums[8 * i : 8 * i + 8], axis=0, keepdims=True)
    if spread:
        for i in range(3):
            late_begin(i)
            late_end(i)
    for c in (chunks - 2, chunks - 1):
        for store in input_stores(c):
            store.wait()
    if spread:
        finish_scatter()
        for store in stores:
            store.wait()
    finish1()
    finish2()


def backward(
    prefix_len, projected, d_bin, b_out, gain1, gain2, mlp_partial, normed1, context, w_qkv, w_out,
    inputs, attn_sum, d_output, summed2,
):
    tokens, depth = inputs.shape
    width = w_out.shape[0]
    spread = (lax.axis_size("dp"), lax.axis_size("col")) == (2, 4)
    dma = pltpu.SemaphoreType.DMA
    buffer = lambda *shape: pltpu.VMEM(shape, jnp.bfloat16)
    wide_buffer = lambda *shape: pltpu.VMEM(shape, jnp.float32)
    single = lambda *shape: jax.ShapeDtypeStruct(shape, jnp.float32)
    sums, scatter_scratch = [single(8, 128), single(8, 128)], []
    if spread:
        block, side = (3, depth // 8, width), (width, depth // 8)
        sums = [single(*block), single(*side)]
        scatter_scratch = [wide_buffer(3, 8, depth), wide_buffer(3, 8, depth)]
        scatter_scratch += [dma((2, 3)), dma((2, 3))]
        for shape in (block, side):
            scatter_scratch += [
                buffer(4, *shape), buffer(4, *shape), buffer(*shape), buffer(2, *shape)
            ]
        scatter_scratch += [wide_buffer(*block), wide_buffer(*side)]
        scatter_scratch += [dma((2,)), dma((4, 8)), dma((4, 8)), dma((8,)), dma((8,))]
        scatter_scratch += [dma((2, 8)), dma((2, 8)), dma((4, 8))]
    out = pl.pallas_call(
        partial(backward_kernel, lax.axis_size("row"), spread),
        out_shape=[
            low_shape(tokens, depth),
            single(tokens, depth),
            single(tokens, depth),
            low_shape(3, depth, width),
            low_shape(width, depth),
            *sums,
            single(8, depth),
            single(8, depth),
        ],
        in_specs=[pl.BlockSpec(memory_space=pltpu.SMEM)] + [IN_VMEM] * 5 + [IN_HBM] * 9,
        out_specs=[IN_HBM] * 7 + [IN_VMEM] * 2,
        scratch_shapes=[
            buffer(tokens, depth),
            buffer(tokens, width),
            buffer(tokens, depth),
            buffer(tokens, width),
            buffer(tokens, depth),
            wide_buffer(tokens, HEAD_DIM),
            wide_buffer(tokens, HEAD_DIM),
            buffer(3, tokens, width),
            buffer(2, TILE, TILE),
            buffer(tokens, depth),
            buffer(*w_qkv.shape),
            wide_buffer(RING, SLICE, depth),
            wide_buffer(32, depth),
            dma((2, tokens // BLOCK)),
            dma((2, 4)),
            dma((5,)),
            dma((2,)),
            dma((RING, 2)),
            dma((RING, 2)),
        ]
        + line_scratch((tokens, depth))
        + line_scratch((tokens, depth))
        + scatter_scratch,
        compiler_params=kernel_params(2, 63),
        cost_estimate=COST,
    )(
        prefix_len, projected, d_bin, b_out[None], gain1[None], gain2[None], mlp_partial, normed1,
        context, w_qkv, w_out, inputs, attn_sum, d_output, summed2,
    )
    mlp_sum, d_inputs, _, d_wqkv, d_wout, sum_wqkv, sum_wout, early, late = out
    if not spread:
        early, late = lax.psum((early, late), ("dp", "col"))
        sum_wqkv, sum_wout = scatter_low(d_wqkv, 1), scatter_low(d_wout, 1)
    return mlp_sum, d_inputs, sum_wqkv, sum_wout, early, late


def scatter_low(grad, dim):
    summed = lax.psum_scatter(grad, ("dp", "col"), scatter_dimension=dim, tiled=True)
    return summed.astype(jnp.float32)


def local(
    inputs,
    prefix_len,
    norm1_gain,
    norm1_shift,
    w_qkv,
    b_qv,
    w_out,
    b_out,
    norm2_gain,
    norm2_shift,
    w_in,
    b_in,
    w_down,
    b_down,
    d_output,
):
    low_mats = (
        w_qkv.astype(jnp.bfloat16),
        w_out.astype(jnp.bfloat16),
        w_in.astype(jnp.bfloat16),
        w_down.astype(jnp.bfloat16),
    )
    full_in, full_down = low_mats[2:]
    source = inputs.astype(jnp.float32)
    if (lax.axis_size("dp"), lax.axis_size("col")) == (2, 4):
        normed1_low, projected, context_low, full_qkv, full_out = head(
            prefix_len, inputs, norm1_gain, norm1_shift, b_qv, low_mats[0], low_mats[1]
        )
    else:
        full_qkv = lax.all_gather(low_mats[0], ("dp", "col"), axis=1, tiled=True)
        full_out = lax.all_gather(low_mats[1], ("dp", "col"), axis=1, tiled=True)
        full_in = lax.all_gather(full_in, ("dp", "col"), axis=0, tiled=True)
        full_down = lax.all_gather(full_down, ("dp", "col"), axis=1, tiled=True)
        normed1, _, _ = norm_forward(source, norm1_gain, norm1_shift)
        normed1_low = normed1.astype(jnp.bfloat16)
        projected = jnp.einsum(
            "td,cdn->ctn", normed1_low, full_qkv, preferred_element_type=jnp.float32
        )
        bias_rows = jnp.stack([b_qv[0], jnp.zeros_like(b_qv[0]), b_qv[1]])
        projected = (projected + bias_rows[:, None, :]).astype(jnp.bfloat16)
        context_low = attend(prefix_len, projected)
    attn_sum, summed2, mlp_partial, grad_wdown, grad_win, grad_bin = mlp_sums(
        context_low, full_out, b_out, norm2_gain, norm2_shift, b_in,
        inputs, full_in, full_down, d_output,
    )
    sent_win = scatter_low(grad_win, 0)
    sent_wdown = scatter_low(grad_wdown, 1)
    mlp_sum, d_inputs, sent_wqkv, sent_wout, early, late = backward(
        prefix_len, projected, grad_bin, b_out, norm1_gain, norm2_gain, mlp_partial, normed1_low,
        context_low, full_qkv, full_out, inputs, attn_sum, d_output, summed2,
    )
    hidden = source + attn_sum.astype(jnp.float32) + b_out
    output = (hidden + mlp_sum.astype(jnp.float32) + b_down).astype(jnp.bfloat16)
    width = b_qv.shape[1]
    return (
        output,
        d_inputs,
        late[0],
        late[1],
        sent_wqkv,
        early[5, : 2 * width].reshape(2, width),
        sent_wout,
        early[0],
        early[1],
        early[2],
        sent_win,
        early[4],
        sent_wdown,
        early[3],
    )


def solution(mesh):
    return jax.shard_map(
        local,
        mesh=mesh,
        in_specs=(
            P(("dp", "col"), None),
            P(("dp", "col")),
            P(),
            P(),
            P(None, ("dp", "col"), "row"),
            P(None, "row"),
            P("row", ("dp", "col")),
            P(),
            P(),
            P(),
            P(("dp", "col"), "row"),
            P("row"),
            P("row", ("dp", "col")),
            P(),
            P(("dp", "col"), None),
        ),
        out_specs=(
            P(("dp", "col"), None),
            P(("dp", "col"), None),
            P(),
            P(),
            P(None, ("dp", "col"), "row"),
            P(None, "row"),
            P("row", ("dp", "col")),
            P(),
            P(),
            P(),
            P(("dp", "col"), "row"),
            P("row"),
            P("row", ("dp", "col")),
            P(),
        ),
        check_vma=False,
    )
```

```python
from functools import partial

import jax
import jax.numpy as jnp
from jax import lax
from jax.experimental import pallas as pl
from jax.experimental.pallas import tpu as pltpu
from jax.sharding import PartitionSpec as P

HEAD_DIM = 128
MESH_IDS = pl.DeviceIdType.MESH
CHUNK = 32
LAG = 2


eps_norm = 1e-05


def norm_forward(values, norm_gain, norm_shift):
    average = jnp.mean(values, axis=-1, keepdims=True)
    centered = values - average
    variance = jnp.mean(centered * centered, axis=-1, keepdims=True)
    inverse = lax.rsqrt(variance + eps_norm)
    scaled = centered * inverse
    return (scaled * norm_gain + norm_shift, scaled, inverse)


def norm_backward(grad, scaled, inverse, norm_gain):
    grad_scaled = grad * norm_gain
    return inverse * (
        grad_scaled
        - jnp.mean(grad_scaled, axis=-1, keepdims=True)
        - scaled * jnp.mean(grad_scaled * scaled, axis=-1, keepdims=True)
    )


def dot(left, right, left_dim, right_dim):
    return lax.dot_general(
        left, right, (((left_dim,), (right_dim,)), ((), ())), preferred_element_type=jnp.float32
    )


def greet_row(n, others=()):
    r = lax.axis_index("row")
    last = n - 1
    bar = pltpu.get_barrier_semaphore()
    for cond, dev in ((r > 0, r - 1), (r < last, r + 1)):

        @pl.when(cond)
        def _():
            pl.semaphore_signal(bar, inc=1, device_id={"row": dev}, device_id_type=MESH_IDS)

    for other in others:
        pl.semaphore_signal(bar, inc=1, device_id=other, device_id_type=MESH_IDS)
    inside = (r > 0) & (r < last)

    @pl.when(inside)
    def _():
        pl.semaphore_wait(bar, 2 + len(others))

    @pl.when(jnp.logical_not(inside))
    def _():
        pl.semaphore_wait(bar, 1 + len(others))


def plane_partners():
    y, x = lax.axis_index("dp"), lax.axis_index("col")
    far_x, near = lax.rem(x + 2, 4), x + 1 - 2 * lax.rem(x, 2)
    far_near = lax.rem(near + 2, 4)
    ids = {"x": {"col": far_x}, "y": {"dp": 1 - y}, "near": {"col": near}}
    mine = {"own": y * 4 + x, "x": y * 4 + far_x, "y": (1 - y) * 4 + x, "xy": (1 - y) * 4 + far_x}
    theirs = {
        "own": y * 4 + near,
        "x": y * 4 + far_near,
        "y": (1 - y) * 4 + near,
        "xy": (1 - y) * 4 + far_near,
    }
    return ids, mine, theirs


KINDS = ("own", "x", "y", "xy")


def plane_gather(pieces, send_sem, recv_sem, near_send, near_recv, local_sem):
    ids, mine, theirs = plane_partners()
    count = len(pieces)

    def remote(kind, k, to, src, dst):
        row = KINDS.index(kind)
        near = to == "near"
        return pltpu.make_async_remote_copy(
            src_ref=src,
            dst_ref=dst,
            send_sem=(near_send if near else send_sem).at[row, k],
            recv_sem=(near_recv if near else recv_sem).at[row, k],
            device_id=ids[to],
            device_id_type=MESH_IDS,
        )

    def outgoing(k):
        own, place = pieces[k](mine["own"])
        return [remote("x", k, "x", own, place), remote("y", k, "y", own, place)]

    def local(k):
        own, place = pieces[k](mine["own"])
        return pltpu.make_async_copy(own, place, local_sem.at[k])

    def onward(k):
        kind, to = ("x", "y") if k % 2 == 0 else ("y", "x")
        place = pieces[k](mine[kind])[1]
        return remote("xy", k, to, place, place)

    def share(kind, k):
        own, place = pieces[k](mine[kind])
        return remote(kind, k, "near", own if kind == "own" else place, place)

    def start():
        for k in range(count):
            for copy in outgoing(k):
                copy.start()
        for k in range(count):
            share("own", k).start()
            local(k).start()

    def arrive(k):
        for copy in outgoing(k):
            copy.wait_recv()
        onward(k).start()
        share("x", k).start()
        share("y", k).start()

    def arrive_far(k):
        onward(k).wait_recv()
        share("xy", k).start()

    def finish():
        for k in range(count):
            local(k).wait()
            for copy in outgoing(k):
                copy.wait_send()
            onward(k).wait_send()
            for kind in KINDS:
                place = pieces[k](theirs[kind])[1]
                share(kind, k).wait_send()
                remote(kind, k, "near", place, place).wait_recv()

    return list(ids.values()), start, arrive, arrive_far, finish


def line_sum(n, p_ref, o_ref, held, rs_s, rs_r, ag_s, ag_r, loc):
    half = o_ref.shape[0] // 2
    chunks = held.shape[0] // 2 // CHUNK
    r = lax.axis_index("row")
    last = n - 1
    place = (r, last - r)
    after = (jnp.minimum(r + 1, last), jnp.maximum(r - 1, 0))
    before = (jnp.maximum(r - 1, 0), jnp.minimum(r + 1, last))

    def rows(d, c):
        return pl.ds(pl.multiple_of((half if d == 0 else 0) + c * CHUNK, CHUNK), CHUNK)

    def slot(d, c):
        return pl.ds(pl.multiple_of((1 - d) * chunks * CHUNK + c * CHUNK, CHUNK), CHUNK)


    def onward(d, c, src):
        return pltpu.make_async_remote_copy(
            src_ref=src.at[rows(d, c) if src is p_ref else slot(d, c)],
            dst_ref=held.at[slot(d, c)],
            send_sem=rs_s.at[d, c],
            recv_sem=rs_r.at[d, c],
            device_id={"row": after[d]},
            device_id_type=MESH_IDS,
        )

    def back(d, c, src):
        return pltpu.make_async_remote_copy(
            src_ref=src.at[slot(d, c) if src is held else rows(d, c)],
            dst_ref=o_ref.at[rows(d, c)],
            send_sem=ag_s.at[d, c],
            recv_sem=ag_r.at[d, c],
            device_id={"row": before[d]},
            device_id_type=MESH_IDS,
        )

    def keep(d, c):
        return pltpu.make_async_copy(held.at[slot(d, c)], o_ref.at[rows(d, c)], loc.at[c])

    def step(t):
        for d in (0, 1):

            @pl.when((place[d] == 0) & (t >= 0) & (t < chunks))
            def _():
                onward(d, t, p_ref).start()

            c = t - LAG * place[d]

            @pl.when((place[d] > 0) & (c >= 0) & (c < chunks))
            def _():
                onward(d, c, p_ref).wait_recv()
                here = slot(d, c)
                held[here] = (
                    held[here].astype(jnp.float32) + p_ref[rows(d, c)].astype(jnp.float32)
                ).astype(jnp.bfloat16)

                @pl.when(place[d] < last)
                def _():
                    onward(d, c, held).start()

                @pl.when(place[d] == last)
                def _():
                    back(d, c, held).start()
                    keep(d, c).start()

        for d in (0, 1):
            c = t - LAG * (2 * last - place[d])

            @pl.when((place[d] < last) & (c >= 0) & (c < chunks))
            def _():
                back(d, c, o_ref).wait_recv()

                @pl.when(place[d] > 0)
                def _():
                    back(d, c, o_ref).start()

    def settle(c):
        for d in (0, 1):

            @pl.when(place[d] < last)
            def _():
                onward(d, c, p_ref).wait_send()

            @pl.when(place[d] == last)
            def _():
                keep(d, c).wait()

    def finish(c):
        for d in (0, 1):

            @pl.when(place[d] > 0)
            def _():
                back(d, c, o_ref).wait_send()

    def drain():
        def both(c):
            settle(c)
            finish(c)

        loop(0, chunks, both)

    return step, drain, settle, lambda: loop(0, chunks, finish)


def line_steps(n, total_rows):
    return total_rows // 2 // CHUNK + LAG * 2 * (n - 1)


def line_scratch(shape):
    chunks = shape[0] // 2 // CHUNK
    dma = pltpu.SemaphoreType.DMA
    return [
        pltpu.VMEM(shape, jnp.bfloat16),
        dma((2, chunks)),
        dma((2, chunks)),
        dma((2, chunks)),
        dma((2, chunks)),
        dma((chunks,)),
    ]


def loop(start, stop, body):
    def one(t, carry):
        body(t)
        return carry

    lax.fori_loop(start, stop, one, 0)


COST = pl.CostEstimate(flops=1000, bytes_accessed=1000, transcendentals=0)
IN_VMEM = pl.BlockSpec(memory_space=pltpu.VMEM)
IN_HBM = pl.BlockSpec(memory_space=pl.ANY)


def low_shape(*shape):
    return jax.ShapeDtypeStruct(shape, jnp.bfloat16)


def kernel_params(collective_id, mib):
    return pltpu.CompilerParams(
        collective_id=collective_id, has_side_effects=True, vmem_limit_bytes=mib * 2**20
    )


TILE = 512
FEW = 16
BLOCK = 256


def mlp_sums_kernel(
    n, spread, ctx, w_out, b_out, gain, shift, b_in, src_hbm, w_in_hbm, w_down_hbm, g_hbm,
    branch, d_normed, mlp, d_wdown, d_win, d_bin,
    p, w_in, w_down, g, normed, act, d_pre, mlp_acc, d_acc, rows_a, rows_b, stage, w_stage,
    load_sem, block_sem, mlp_sem, store_sem, *more,
):
    tokens, depth = p.shape
    units = act.shape[1]
    half = tokens // 2
    part = BLOCK // 2
    blocks = tokens // BLOCK
    per_block = part // CHUNK
    quarters = units // TILE

    def sides(j):
        low_rows = pl.ds(pl.multiple_of(j * part, part), part)
        high_rows = pl.ds(pl.multiple_of(half + j * part, part), part)
        return low_rows, high_rows

    def own(j, side=None):
        if side is None:
            return pl.ds(pl.multiple_of(j * BLOCK, BLOCK), BLOCK)
        return pl.ds(pl.multiple_of(j * BLOCK + side * part, part), part)

    lines, gather_sems = more[:12], more[12:]
    loads = []
    others = []
    if spread:
        deep, wide = w_in_hbm.shape[0], w_down_hbm.shape[1]

        def in_piece(k, place):
            size = deep // 2
            there = pl.ds(pl.multiple_of(place * deep + k * size, size), size)
            return w_in_hbm.at[pl.ds(k * size, size)], w_in.at[there]

        def down_piece(k, place):
            some = pl.ds(k * (units // 2), units // 2)
            cols = pl.ds(pl.multiple_of(place * wide, wide), wide)
            return w_down_hbm.at[some], w_down.at[some, cols]

        pieces = [partial(f, k) for f in (in_piece, down_piece) for k in range(2)]
        others, start_gather, arrive, arrive_far, finish_gather = plane_gather(
            pieces, *gather_sems
        )
    else:
        loads = [
            pltpu.make_async_copy(w_in_hbm, w_in, load_sem.at[0]),
            pltpu.make_async_copy(w_down_hbm, w_down, load_sem.at[1]),
        ]
    for j in range(blocks):
        for side, here in enumerate((j * part, half + j * part)):
            loads.append(
                pltpu.make_async_copy(
                    g_hbm.at[pl.ds(here, part)],
                    g.at[pl.ds(j * BLOCK + side * part, part)],
                    load_sem.at[2 + 2 * j + side],
                )
            )
    for load in loads:
        load.start()
    d_bin[...] = jnp.zeros_like(d_bin)
    greet_row(n, others)
    if spread:
        start_gather()
    step1, _, settle1, finish1 = line_sum(n, p, branch, *lines[:6])
    step2, drain2, _, _ = line_sum(n, p, d_normed, *lines[6:])

    def project(j):
        low_rows, high_rows = sides(j)
        both = jnp.concatenate([ctx[low_rows], ctx[high_rows]], axis=0)
        for c in range(0, depth, TILE):
            cols = slice(c, c + TILE)
            term = dot(both, w_out[:, cols], 1, 0).astype(jnp.bfloat16)
            p[low_rows, cols] = term[:part]
            p[high_rows, cols] = term[part:]
        loop(j * per_block, (j + 1) * per_block, step1)

    for j in range(blocks):
        project(j)
        if spread and j == blocks - 2:
            for k in range(len(pieces)):
                arrive(k)
    if spread:
        for k in range(len(pieces)):
            arrive_far(k)
        finish_gather()
    for load in loads:
        load.wait()

    def norm_block(j):
        loop(j * per_block, (j + 1) * per_block, settle1)
        copies = []
        for i, (src, dst) in enumerate(((branch, rows_a), (src_hbm, rows_b))):
            for side, here in enumerate(sides(j)):
                copies.append(
                    pltpu.make_async_copy(
                        src.at[here], dst.at[pl.ds(side * part, part)], block_sem.at[i, side]
                    )
                )
        for copy in copies:
            copy.start()
        for copy in copies:
            copy.wait()

        def few(k):
            here = pl.ds(pl.multiple_of(k * 64, 64), 64)
            there = pl.ds(pl.multiple_of(j * BLOCK + k * 64, 64), 64)
            source = rows_b[here].astype(jnp.float32)
            hidden = source + rows_a[here].astype(jnp.float32) + b_out[...]
            normed[there] = norm_forward(hidden, gain[...], shift[...])[0].astype(jnp.bfloat16)

        loop(0, BLOCK // 64, few)

    def mlp_out(j):
        return [
            pltpu.make_async_copy(
                stage.at[pl.ds(side * part, part)], mlp.at[here], mlp_sem.at[side]
            )
            for side, here in enumerate(sides(j))
        ]

    first = tokens // 2 // CHUNK

    def block(j):
        for q in range(quarters):
            t = first + j * per_block + q
            step1(t)
            step2(t - first - per_block)
            if q == 0:
                norm_block(j)
            units_q = slice(q * TILE, (q + 1) * TILE)
            here = own(j)
            pre = dot(normed[here], w_in[:, units_q], 1, 0) + b_in[:, units_q]
            d_act = dot(g[here], w_down[units_q], 1, 1)
            lower = 0.5 * (1.0 + lax.erf(pre * 0.5**0.5))
            act[here, units_q] = (pre * lower).astype(jnp.bfloat16)
            slope = lower + pre * (jnp.exp(-0.5 * pre * pre) * (0.5 / jnp.pi) ** 0.5)
            low_pre = (d_act * slope).astype(jnp.bfloat16)
            d_pre[here, units_q] = low_pre
            d_bin[:, units_q] += jnp.sum(low_pre.astype(jnp.float32), axis=0, keepdims=True)
            for c in range(0, depth, TILE):
                cols = slice(c, c + TILE)
                m_term = dot(act[here, units_q], w_down[units_q, cols], 1, 0)
                d_term = dot(d_pre[here, units_q], w_in[cols, units_q], 1, 1)
                if q == 0:
                    mlp_acc[:, cols] = m_term
                    d_acc[:, cols] = d_term
                elif q < quarters - 1:
                    mlp_acc[:, cols] += m_term
                    d_acc[:, cols] += d_term
                else:
                    if c == 0:

                        @pl.when(j > 0)
                        def _():
                            for copy in mlp_out(j - 1):
                                copy.wait()

                    stage[:, cols] = (mlp_acc[:, cols] + m_term).astype(jnp.bfloat16)
                    d_low = (d_acc[:, cols] + d_term).astype(jnp.bfloat16)
                    for side, rows in enumerate(sides(j)):
                        p[rows, cols] = d_low[side * part : (side + 1) * part]
        for copy in mlp_out(j):
            copy.start()

    loop(0, blocks, block)
    begin = first
    steps = line_steps(n, tokens)
    tick = tokens // 2 // CHUNK - per_block
    jobs = ((act, g, d_wdown), (normed, d_pre, d_win))
    for k, (left, right, out) in enumerate(jobs):
        across = out.shape[1] // TILE
        tiles = (out.shape[0] // TILE) * across

        def store(tile, slot):
            m = pl.ds(pl.multiple_of((tile // across) * TILE, TILE), TILE)
            c = pl.ds(pl.multiple_of(lax.rem(tile, across) * TILE, TILE), TILE)
            copy = pltpu.make_async_copy(w_stage.at[slot], out.at[m, c], store_sem.at[slot])
            return m, c, copy

        def body(u):
            step2(tick + k * (tiles // 2) + u)
            for slot in range(2):
                m, c, copy = store(2 * u + slot, slot)
                if k == 0:

                    @pl.when(u > 0)
                    def _():
                        copy.wait()
                else:
                    copy.wait()
                w_stage[slot] = dot(left[:, m], right[:, c], 0, 0).astype(jnp.bfloat16)
                copy.start()

        loop(0, tiles // 2, body)
        tick_end = tick + (k + 1) * (tiles // 2)
    if tick_end < steps:
        loop(tick_end, steps, step2)
    for slot in range(2):
        store(slot, slot)[2].wait()
    for copy in mlp_out(blocks - 1):
        copy.wait()
    finish1()
    drain2()


def mlp_sums(context, w_out, b_out, gain, shift, b_in, inputs, w_in, w_down, d_output):
    tokens, depth = inputs.shape
    units = w_in.shape[1]
    spread = w_in.shape[0] < depth
    dma = pltpu.SemaphoreType.DMA
    low_buffer = lambda *shape: pltpu.VMEM(shape, jnp.bfloat16)
    return pl.pallas_call(
        partial(mlp_sums_kernel, lax.axis_size("row"), spread),
        out_shape=[
            low_shape(tokens, depth),
            low_shape(tokens, depth),
            low_shape(tokens, depth),
            low_shape(units, depth),
            low_shape(depth, units),
            jax.ShapeDtypeStruct((1, units), jnp.float32),
        ],
        in_specs=[IN_VMEM] * 6 + [IN_HBM] * 4,
        out_specs=[IN_HBM] * 5 + [IN_VMEM],
        scratch_shapes=[
            low_buffer(tokens, depth),
            low_buffer(depth, units),
            low_buffer(units, depth),
            low_buffer(tokens, depth),
            low_buffer(tokens, depth),
            low_buffer(tokens, units),
            low_buffer(tokens, units),
            pltpu.VMEM((BLOCK, depth), jnp.float32),
            pltpu.VMEM((BLOCK, depth), jnp.float32),
            low_buffer(BLOCK, depth),
            low_buffer(BLOCK, depth),
            low_buffer(BLOCK, depth),
            low_buffer(2, TILE, TILE),
            dma((2 + 2 * (tokens // BLOCK),)),
            dma((2, 2)),
            dma((2,)),
            dma((2,)),
        ]
        + line_scratch((tokens, depth))
        + line_scratch((tokens, depth))
        + ([dma((4, 4))] * 4 + [dma((4,))] if spread else []),
        compiler_params=kernel_params(1, 61),
        cost_estimate=COST,
    )(
        context, w_out, b_out[None], gain[None], shift[None], b_in[None],
        inputs, w_in, w_down, d_output,
    )


QUERY_ROWS = 256


def head_kernel(
    prefix_ref, src, gain, shift, b_q, b_v, w_qkv_hbm, w_out_hbm,
    normed_out, projected_out, context_out, full_qkv, full_out,
    weights, w_out, normed, projected, context, store_sem, *sems,
):
    tokens, depth = src.shape
    width = projected.shape[2]
    deep, wide = w_qkv_hbm.shape[1], w_out_hbm.shape[1]
    size, tall = deep // 2, width // 2

    def qkv_piece(c, k, place):
        there = pl.ds(pl.multiple_of(place * deep + k * size, size), size)
        return w_qkv_hbm.at[c, pl.ds(k * size, size)], weights.at[c, there]

    def out_piece(k, place):
        some = pl.ds(k * tall, tall)
        cols = pl.ds(pl.multiple_of(place * wide, wide), wide)
        return w_out_hbm.at[some], w_out.at[some, cols]

    parts = [[partial(qkv_piece, c, k) for k in range(2)] for c in range(3)]
    parts.append([partial(out_piece, k) for k in range(2)])
    others = list(plane_partners()[0].values())
    start, arrive, far, finish = zip(
        *[plane_gather(part, *sems[5 * i : 5 * i + 5])[1:] for i, part in enumerate(parts)]
    )
    bar = pltpu.get_barrier_semaphore()
    for other in others:
        pl.semaphore_signal(bar, inc=1, device_id=other, device_id_type=MESH_IDS)
    pl.semaphore_wait(bar, len(others))
    start[0]()
    start[1]()

    def few(r):
        here = pl.ds(pl.multiple_of(r * FEW, FEW), FEW)
        rows = norm_forward(src[here].astype(jnp.float32), gain[...], shift[...])[0]
        normed[here] = rows.astype(jnp.bfloat16)

    loop(0, tokens // FEW // 4, lambda r: [few(4 * r + i) for i in range(4)])
    stores = [
        pltpu.make_async_copy(src, dst, store_sem.at[i])
        for i, (src, dst) in enumerate(
            (
                (normed, normed_out),
                (weights, full_qkv),
                (projected, projected_out),
                (w_out, full_out),
                (context, context_out),
            )
        )
    ]
    stores[0].start()
    for i in range(2):
        for k in range(2):
            arrive[i](k)
    start[2]()
    for c in range(3):
        if c == 2:
            for k in range(2):
                arrive[2](k)
            start[3]()
        for k in range(2):
            far[c](k)
        finish[c]()

        def rows_of(i):
            here = pl.ds(pl.multiple_of(i * BLOCK, BLOCK), BLOCK)
            term = dot(normed[here], weights[c], 1, 0)
            if c != 1:
                term += (b_q if c == 0 else b_v)[...]
            projected[c, here] = term.astype(jnp.bfloat16)

        loop(0, tokens // BLOCK, rows_of)
    stores[1].start()
    stores[2].start()
    for k in range(2):
        arrive[3](k)
    attend_kernel(prefix_ref, projected, context)
    stores[4].start()
    for k in range(2):
        far[3](k)
    finish[3]()
    stores[3].start()
    for store in stores:
        store.wait()


def head(prefix_len, inputs, gain, shift, b_qv, w_qkv, w_out):
    tokens, depth = inputs.shape
    width = w_out.shape[0]
    dma = pltpu.SemaphoreType.DMA
    return pl.pallas_call(
        head_kernel,
        out_shape=[
            low_shape(tokens, depth),
            low_shape(3, tokens, width),
            low_shape(tokens, width),
            low_shape(3, depth, width),
            low_shape(width, depth),
        ],
        in_specs=[pl.BlockSpec(memory_space=pltpu.SMEM)] + [IN_VMEM] * 5 + [IN_HBM] * 2,
        out_specs=[IN_HBM] * 5,
        scratch_shapes=[
            pltpu.VMEM((3, depth, width), jnp.bfloat16),
            pltpu.VMEM((width, depth), jnp.bfloat16),
            pltpu.VMEM((tokens, depth), jnp.bfloat16),
            pltpu.VMEM((3, tokens, width), jnp.bfloat16),
            pltpu.VMEM((tokens, width), jnp.bfloat16),
            dma((5,)),
        ]
        + ([dma((4, 2))] * 4 + [dma((2,))]) * 4,
        compiler_params=kernel_params(3, 62),
        cost_estimate=COST,
    )(prefix_len, inputs, gain[None], shift[None], b_qv[:1], b_qv[1:], w_qkv, w_out)


def block_probs(i, prefix, cols, q, k):
    start = i * QUERY_ROWS
    width = max(start + QUERY_ROWS, q.shape[0] // 2)
    here = slice(start, start + QUERY_ROWS)
    scores = dot(k[:width, cols], q[here, cols], 1, 1) * HEAD_DIM ** (-0.5)
    key = lax.broadcasted_iota(jnp.int32, scores.shape, 0)
    query = lax.broadcasted_iota(jnp.int32, scores.shape, 1) + start
    scores = jnp.where((key <= query) | (key < prefix), scores, -1000000000.0)
    expo = jnp.exp(scores - jnp.max(scores, axis=0, keepdims=True))
    return here, width, expo * (1.0 / jnp.sum(expo, axis=0, keepdims=True))


def attend_kernel(prefix_ref, projected, context):
    q, k, v = (projected.at[c] for c in range(3))
    prefix = prefix_ref[0]

    def head(h):
        cols = pl.ds(pl.multiple_of(h * HEAD_DIM, HEAD_DIM), HEAD_DIM)
        v_t = v[:, cols].T
        for i in range(q.shape[0] // QUERY_ROWS):
            here, width, probs = block_probs(i, prefix, cols, q, k)
            out = dot(v_t[:, :width], probs.astype(jnp.bfloat16), 1, 0)
            context[here, cols] = out.T.astype(jnp.bfloat16)

    loop(0, q.shape[1] // HEAD_DIM, head)


def attend(prefix_len, projected):
    return pl.pallas_call(
        attend_kernel,
        out_shape=low_shape(*projected.shape[1:]),
        in_specs=[pl.BlockSpec(memory_space=pltpu.SMEM), IN_VMEM],
        out_specs=IN_VMEM,
        compiler_params=pltpu.CompilerParams(vmem_limit_bytes=32 * 2**20),
        cost_estimate=COST,
    )(prefix_len, projected)


def attend_piece(i, prefix, cols, q, k, v, k_t, d_context, d_proj, d_key, d_value, first):
    score_scale = HEAD_DIM ** (-0.5)
    here, width, probs = block_probs(i, prefix, cols, q, k)
    q_block, g_block = q[here, cols], d_context[here, cols]
    d_probs = dot(v[:width, cols], g_block, 1, 1)
    inner = jnp.sum(d_probs * probs, axis=0, keepdims=True)
    d_scores = (probs * (d_probs - inner)).astype(jnp.bfloat16)
    d_query = dot(k_t[:, :width], d_scores, 1, 0) * score_scale
    d_proj[0, here, cols] = d_query.T.astype(jnp.bfloat16)
    for total, term in (
        (d_key, dot(d_scores, q_block, 1, 0)),
        (d_value, dot(probs.astype(jnp.bfloat16), g_block, 1, 0)),
    ):
        if first:
            total[...] = term
        else:
            total[:width] += term


def plane_scatter(pieces, sems):
    ids, mine, theirs = plane_partners()
    near_send, near_recv, far_send, far_recv, last_send, last_recv, load_sem = sems
    count = len(pieces)

    def remote(src, dst, send, recv, to):
        return pltpu.make_async_remote_copy(
            src_ref=src,
            dst_ref=dst,
            send_sem=send,
            recv_sem=recv,
            device_id=ids[to],
            device_id_type=MESH_IDS,
        )

    def near(i, k):
        block, to, _, _, _ = pieces[k]
        place = theirs[KINDS[i]]
        return remote(block(place), to(i), near_send.at[i, k], near_recv.at[i, k], "near")

    def load(i, k):
        block, _, own, _, _ = pieces[k]
        return pltpu.make_async_copy(block(mine[KINDS[i]]), own(i), load_sem.at[i, k])

    def far(k):
        _, _, own, to, _ = pieces[k]
        return remote(own(3), to(), far_send.at[k], far_recv.at[k], "x" if k % 2 == 0 else "y")

    def last(i, k):
        _, _, own, _, to = pieces[k]
        return remote(
            own(i), to(i - 1), last_send.at[i - 1, k], last_recv.at[i - 1, k], KINDS[i]
        )

    def add(target, term):
        flat = target.shape[0]

        def some(r):
            here = pl.ds(pl.multiple_of(r * 128, 128), 128)
            target[here] = (
                target[here].astype(jnp.float32) + term[here].astype(jnp.float32)
            ).astype(jnp.bfloat16)

        loop(0, flat // 128, some)

    def start():
        for i in (3, 1, 2, 0):
            for k in range(count):
                near(i, k).start()
                load(i, k).start()

    def pair():
        for i in (3, 1, 2, 0):
            for k in range(count):
                near(i, k).wait_recv()
                load(i, k).wait()
                add(pieces[k][2](i), pieces[k][1](i))
                if i == 3:
                    far(k).start()
                elif i == 1 + k % 2:
                    last(i, k).start()

    def cross():
        for k in range(count):
            far(k).wait_recv()
            i = 2 - k % 2
            add(pieces[k][2](i), pieces[k][3]())
            last(i, k).start()

    def collect(k):
        for i in (1, 2):
            last(i, k).wait_recv()
        return pieces[k][2](0), pieces[k][4](0), pieces[k][4](1)

    def finish():
        for k in range(count):
            for i in range(4):
                near(i, k).wait_send()
            far(k).wait_send()
            for i in (1, 2):
                last(i, k).wait_send()

    return start, pair, cross, collect, finish


def sums_out(kind, vectors, slots, send_sem, recv_sem):
    ids = plane_partners()[0]

    def copy(i):
        return pltpu.make_async_remote_copy(
            src_ref=vectors,
            dst_ref=slots.at[i],
            send_sem=send_sem.at[kind, i],
            recv_sem=recv_sem.at[kind, i],
            device_id=ids[("near", "x", "y")[i]],
            device_id_type=MESH_IDS,
        )

    def begin(i):
        copy(i).start()

    def end(i):
        copy(i).wait()
        vectors[...] += slots[i]

    return begin, end


SLICE = 64
RING = 4


def backward_kernel(
    n, spread, prefix_ref, projected, d_bin, b_out, b_down, gain1, gain2,
    mlp_hbm, n1_hbm, ctx_hbm, w_qkv_hbm, w_out_hbm, src_hbm, attn_hbm, g_hbm, dn2_hbm,
    mlp_sum, output, d_inputs, d_hidden, d_wqkv, d_wout, sum_wqkv, sum_wout, early, late,
    p, d_context, n1, ctx, branch, d_key, d_value, d_proj, w_stage, total, weights, ring, partial_sums,
    p_sem, slice_sem, load_sem, store_sem, ring_in, ring_out, out_in, out_store, *more,
):
    lines, more = more[:12], more[12:]
    tokens, depth = p.shape
    width = projected.shape[2]
    half = tokens // 2
    chunks = half // CHUNK
    blocks = tokens // BLOCK
    part = BLOCK // 2
    per_block = part // CHUNK
    travel = LAG * 2 * (n - 1)
    prefix = prefix_ref[0]

    def sides(j, size):
        return (
            pl.ds(pl.multiple_of(j * size, size), size),
            pl.ds(pl.multiple_of(half + j * size, size), size),
        )

    p_loads = [
        [
            pltpu.make_async_copy(mlp_hbm.at[rows], p.at[rows], p_sem.at[side, j])
            for side, rows in enumerate((pl.ds(j * part, part), pl.ds(half + j * part, part)))
        ]
        for j in range(blocks)
    ]
    for loads in p_loads:
        for load in loads:
            load.start()
    w_out_load = pltpu.make_async_copy(w_out_hbm, total.at[pl.ds(0, width)], load_sem.at[0])
    w_out_load.start()
    loads = [
        pltpu.make_async_copy(src, dst, load_sem.at[1 + i])
        for i, (src, dst) in enumerate(
            ((n1_hbm, n1), (ctx_hbm, ctx), (w_qkv_hbm, weights), (src_hbm, n1))
        )
    ]
    early[...] = jnp.zeros_like(early)
    late[...] = jnp.zeros_like(late)
    early[4:5] = d_bin[...]
    partial_sums[...] = jnp.zeros_like(partial_sums)
    others = []
    if spread:
        slots_e, slots_l, small_s, small_r = more[:4]
        qkv_near, qkv_own, qkv_far, qkv_last, out_near, out_own, out_far, out_last = more[4:12]
        qkv_sum, out_sum, sum_sem = more[12:15]
        others = list(plane_partners()[0].values())
        early_begin, early_end = sums_out(0, early, slots_e, small_s, small_r)
        late_begin, late_end = sums_out(1, late, slots_l, small_s, small_r)
        places = 8
        deep, wide = depth // places, depth // places
        size = deep // 2
        tall = width // 2

        def qkv_piece(c, k):
            def block(place):
                there = pl.ds(pl.multiple_of(place * deep + k * size, size), size)
                return d_wqkv.at[c, there]

            some = pl.ds(k * size, size)
            return (
                block,
                lambda i: qkv_near.at[i, c, some],
                lambda i: qkv_own.at[i, c, some],
                lambda: qkv_far.at[c, some],
                lambda i: qkv_last.at[i, c, some],
            )

        def out_piece(k):
            some = pl.ds(k * tall, tall)

            def block(place):
                cols = pl.ds(pl.multiple_of(place * wide, wide), wide)
                return d_wout.at[some, cols]

            return (
                block,
                lambda i: out_near.at[i, some],
                lambda i: out_own.at[i, some],
                lambda: out_far.at[some],
                lambda i: out_last.at[i, some],
            )

        pieces = [qkv_piece(c, k) for c in range(3) for k in range(2)]
        pieces += [out_piece(k) for k in range(2)]
        start_scatter, pair, cross, collect, finish_scatter = plane_scatter(pieces, more[15:])
        stores = [
            pltpu.make_async_copy(qkv_sum, sum_wqkv, sum_sem.at[0]),
            pltpu.make_async_copy(out_sum, sum_wout, sum_sem.at[1]),
        ]

        def total_of(k):
            own, one, two = collect(k)
            if k < 6:
                target = qkv_sum.at[k // 2, pl.ds((k % 2) * size, size)]
            else:
                target = out_sum.at[pl.ds((k % 2) * tall, tall)]

            def some(r):
                here = pl.ds(pl.multiple_of(r * 128, 128), 128)
                target[here] = (
                    own[here].astype(jnp.float32)
                    + one[here].astype(jnp.float32)
                    + two[here].astype(jnp.float32)
                )

            loop(0, target.shape[0] // 128, some)

    greet_row(n, others)
    step1, _, settle1, finish1 = line_sum(n, p, mlp_sum, *lines[:6])
    step2, _, settle2, finish2 = line_sum(n, p, total, *lines[6:])

    def both_steps(t):
        step1(t)
        step2(t - chunks)

    slices = tokens // SLICE

    def slice_rows(k):
        return pl.ds(pl.multiple_of(k * SLICE, SLICE), SLICE)

    def slice_slot(k, i):
        return pl.ds(pl.multiple_of(half + (lax.rem(k, 2) * 4 + i) * SLICE, SLICE), SLICE)

    def slice_loads(k):
        return [
            pltpu.make_async_copy(
                src.at[slice_rows(k)], total.at[slice_slot(k, i)], slice_sem.at[lax.rem(k, 2), i]
            )
            for i, src in enumerate((dn2_hbm, attn_hbm, src_hbm, g_hbm))
        ]

    def hidden_store(k):
        return pltpu.make_async_copy(
            ring.at[lax.rem(k, RING)], d_hidden.at[slice_rows(k)], ring_out.at[lax.rem(k, RING), 0]
        )

    def norm_slice(k):
        @pl.when(k + 1 < slices)
        def _():
            for load in slice_loads(k + 1):
                load.start()

        for load in slice_loads(k):
            load.wait()

        @pl.when(k >= RING)
        def _():
            hidden_store(k - RING).wait()

        def few(r):
            rows = [
                pl.ds(pl.multiple_of(half + (lax.rem(k, 2) * 4 + i) * SLICE + r * FEW, FEW), FEW)
                for i in range(4)
            ]
            dn, attn, source, g = (total[some].astype(jnp.float32) for some in rows)
            _, scaled, inverse = norm_forward(source + attn + b_out[...], 1.0, 0.0)
            grad = g + norm_backward(dn, scaled, inverse, gain2[...])
            low = grad.astype(jnp.bfloat16)
            branch[pl.ds(pl.multiple_of(k * SLICE + r * FEW, FEW), FEW)] = low
            for i, term in enumerate((low.astype(jnp.float32), dn * scaled, dn, g)):
                partial_sums[8 * i : 8 * i + 8] += term[:8] + term[8:]
            ring[lax.rem(k, RING), pl.ds(pl.multiple_of(r * FEW, FEW), FEW)] = grad

        for r in range(SLICE // FEW):
            few(r)
        hidden_store(k).start()

    for load in slice_loads(0):
        load.start()
    norm_ticks = 4
    for load in p_loads[0]:
        load.wait()

    def norm_tick(t):
        step1(t)
        loop(t * (slices // norm_ticks), (t + 1) * (slices // norm_ticks), norm_slice)

    loop(0, norm_ticks, norm_tick)
    for i in range(4):
        early[i : i + 1] = jnp.sum(partial_sums[8 * i : 8 * i + 8], axis=0, keepdims=True)
    for k in range(slices - RING, slices):
        hidden_store(k).wait()
    for some in p_loads[1:]:
        for load in some:
            load.wait()
    for load in loads[:3]:
        load.start()
    w_out_load.wait()

    def context_rows(i):
        rows = pl.ds(pl.multiple_of(i * BLOCK, BLOCK), BLOCK)
        d_context[rows] = dot(branch[rows], total[:width], 1, 1).astype(jnp.bfloat16)

    loop(0, tokens // BLOCK, context_rows)
    partial_sums[...] = jnp.zeros_like(partial_sums)

    q, k, v = (projected.at[c] for c in range(3))
    q_blocks = tokens // QUERY_ROWS
    heads = width // HEAD_DIM
    head_ticks = q_blocks // 2

    def head(h):
        cols = pl.ds(pl.multiple_of(h * HEAD_DIM, HEAD_DIM), HEAD_DIM)
        k_t = k[:, cols].T
        for j in range(q_blocks):
            if j % 2 == 0:
                step1(norm_ticks + h * head_ticks + j // 2)
            attend_piece(
                q_blocks - 1 - j, prefix, cols, q, k, v, k_t, d_context, d_proj, d_key, d_value,
                j == 0,
            )
        d_proj[1, :, cols] = (d_key[...] * HEAD_DIM ** (-0.5)).astype(jnp.bfloat16)
        d_proj[2, :, cols] = d_value[...].astype(jnp.bfloat16)

    loop(0, heads, head)
    for b, c in ((0, 0), (1, 2)):
        early[5:6, b * width : (b + 1) * width] = jnp.sum(
            d_proj[c].astype(jnp.float32), axis=0, keepdims=True
        )
    for load in loads[:3]:
        load.wait()
    tick = norm_ticks + heads * head_ticks
    tiles = depth // TILE

    def tile_store(c, m):
        some = pl.ds(m * TILE, TILE)
        out = d_wqkv.at[c, some] if c < 3 else d_wout.at[:, some]
        return pltpu.make_async_copy(w_stage.at[m % 2], out, store_sem.at[m % 2])

    for c in range(4):
        step1(tick + c)
        for m in range(tiles):
            some = slice(m * TILE, (m + 1) * TILE)
            if c or m > 1:
                before = (c, m - 2) if m > 1 else (c - 1, tiles + m - 2)
                tile_store(*before).wait()
            if c < 3:
                term = dot(n1[:, some], d_proj[c], 0, 0)
            else:
                term = dot(ctx[...], branch[:, some], 0, 0)
            w_stage[m % 2] = term.astype(jnp.bfloat16)
            tile_store(c, m).start()
    for m in (tiles - 2, tiles - 1):
        tile_store(3, m).wait()
    loads[3].start()
    if tick + 4 < chunks:
        loop(tick + 4, chunks, step1)
    if spread:
        start_scatter()

    def gradient(j):
        loop(j * per_block, (j + 1) * per_block, settle1)
        low_rows, high_rows = sides(j, part)
        rows = [
            jnp.concatenate([d_proj[c, low_rows], d_proj[c, high_rows]], axis=0) for c in range(3)
        ]
        for i in range(0, depth, TILE):
            cols = slice(i, i + TILE)
            term = dot(rows[0], weights[0, cols], 1, 1)
            for c in (1, 2):
                term += dot(rows[c], weights[c, cols], 1, 1)
            term = term.astype(jnp.bfloat16)
            p[low_rows, cols] = term[:part]
            p[high_rows, cols] = term[part:]

    def hidden_loads(c):
        return [
            pltpu.make_async_copy(
                d_hidden.at[rows],
                ring.at[lax.rem(c, RING), pl.ds(side * CHUNK, CHUNK)],
                ring_in.at[lax.rem(c, RING), side],
            )
            for side, rows in enumerate(sides(c, CHUNK))
        ]

    def input_stores(c):
        return [
            pltpu.make_async_copy(
                ring.at[lax.rem(c, RING), pl.ds(side * CHUNK, CHUNK)],
                d_inputs.at[rows],
                ring_out.at[lax.rem(c, RING), side],
            )
            for side, rows in enumerate(sides(c, CHUNK))
        ]

    def norm_rows(c):
        settle2(c)
        for load in hidden_loads(c):
            load.wait()
        for side, rows in enumerate(sides(c, CHUNK)):
            for r in range(CHUNK // FEW):
                some = pl.ds(pl.multiple_of(rows.start + r * FEW, FEW), FEW)
                _, scaled, inverse = norm_forward(n1[some].astype(jnp.float32), 1.0, 0.0)
                grad = total[some].astype(jnp.float32)
                for i, term in enumerate((grad * scaled, grad)):
                    partial_sums[8 * i : 8 * i + 8] += term[:8] + term[8:]
                here = pl.ds(side * CHUNK + r * FEW, FEW)
                ring[lax.rem(c, RING), here] += norm_backward(grad, scaled, inverse, gain1[...])
        for store in input_stores(c):
            store.start()

        @pl.when(c >= 2)
        def _():
            for store in input_stores(c - 2):
                store.wait()

        @pl.when(c + 2 < chunks)
        def _():
            for load in hidden_loads(c + 2):
                load.start()

    def out_slot(c, i, side):
        begin = (lax.rem(c, 2) * 4 + i) * 2 * CHUNK + side * CHUNK
        return pl.ds(pl.multiple_of(begin, CHUNK), CHUNK)

    def out_loads(c):
        return [
            pltpu.make_async_copy(
                src.at[rows], branch.at[out_slot(c, i, side)], out_in.at[i, side]
            )
            for i, src in enumerate((src_hbm, attn_hbm, mlp_sum))
            for side, rows in enumerate(sides(c, CHUNK))
        ]

    def out_stores(c):
        return [
            pltpu.make_async_copy(
                branch.at[out_slot(c, 3, side)], output.at[rows], out_store.at[lax.rem(c, 2), side]
            )
            for side, rows in enumerate(sides(c, CHUNK))
        ]

    def output_rows(c):
        for load in out_loads(c):
            load.wait()

        @pl.when(c >= 2)
        def _():
            for store in out_stores(c - 2):
                store.wait()

        for side in range(2):
            source, attn, mlp = (
                branch[out_slot(c, i, side)].astype(jnp.float32) for i in range(3)
            )
            whole = source + attn + b_out[...] + mlp + b_down[...]
            branch[out_slot(c, 3, side)] = whole.astype(jnp.bfloat16)
        for store in out_stores(c):
            store.start()

    arrival = chunks + travel

    def tick_of(t):
        both_steps(t)

        @pl.when(t >= arrival)
        def _():
            norm_rows(t - arrival)

    for j in range(blocks):
        gradient(j)
        if j == blocks - 1:
            for c in range(2):
                for load in hidden_loads(c):
                    load.start()
            loads[3].wait()
        begin = chunks + j * per_block

        def with_output(t):
            for load in out_loads(t - chunks):
                load.start()
            (tick_of if j == blocks - 1 else both_steps)(t)
            output_rows(t - chunks)

        loop(begin, begin + per_block, with_output)
        if spread:
            if j == 0:
                pair()
            else:
                early_end(j - 1)
            if j < blocks - 1:
                early_begin(j)
    begin = chunks + blocks * per_block
    middle = begin + 2 * per_block + 2
    loop(begin, begin + per_block, tick_of)
    if spread:
        cross()
    loop(begin + per_block, middle, tick_of)
    if spread:
        for k in range(len(pieces)):
            total_of(k)
        for store in stores:
            store.start()
    loop(middle, arrival + chunks, tick_of)
    for i in range(2):
        late[i : i + 1] = jnp.sum(partial_sums[8 * i : 8 * i + 8], axis=0, keepdims=True)
    if spread:
        for i in range(3):
            late_begin(i)
            late_end(i)
    for c in (chunks - 2, chunks - 1):
        for store in input_stores(c) + out_stores(c):
            store.wait()
    if spread:
        finish_scatter()
        for store in stores:
            store.wait()
    finish1()
    finish2()


def backward(
    prefix_len, projected, d_bin, b_out, b_down, gain1, gain2, mlp_partial, normed1, context, w_qkv, w_out,
    inputs, attn_sum, d_output, summed2,
):
    tokens, depth = inputs.shape
    width = w_out.shape[0]
    spread = (lax.axis_size("dp"), lax.axis_size("col")) == (2, 4)
    dma = pltpu.SemaphoreType.DMA
    buffer = lambda *shape: pltpu.VMEM(shape, jnp.bfloat16)
    wide_buffer = lambda *shape: pltpu.VMEM(shape, jnp.float32)
    single = lambda *shape: jax.ShapeDtypeStruct(shape, jnp.float32)
    sums, scatter_scratch = [single(8, 128), single(8, 128)], []
    if spread:
        block, side = (3, depth // 8, width), (width, depth // 8)
        sums = [single(*block), single(*side)]
        scatter_scratch = [wide_buffer(3, 8, depth), wide_buffer(3, 8, depth)]
        scatter_scratch += [dma((2, 3)), dma((2, 3))]
        for shape in (block, side):
            scatter_scratch += [
                buffer(4, *shape), buffer(4, *shape), buffer(*shape), buffer(2, *shape)
            ]
        scatter_scratch += [wide_buffer(*block), wide_buffer(*side)]
        scatter_scratch += [dma((2,)), dma((4, 8)), dma((4, 8)), dma((8,)), dma((8,))]
        scatter_scratch += [dma((2, 8)), dma((2, 8)), dma((4, 8))]
    out = pl.pallas_call(
        partial(backward_kernel, lax.axis_size("row"), spread),
        out_shape=[
            low_shape(tokens, depth),
            low_shape(tokens, depth),
            single(tokens, depth),
            single(tokens, depth),
            low_shape(3, depth, width),
            low_shape(width, depth),
            *sums,
            single(8, depth),
            single(8, depth),
        ],
        in_specs=[pl.BlockSpec(memory_space=pltpu.SMEM)] + [IN_VMEM] * 6 + [IN_HBM] * 9,
        out_specs=[IN_HBM] * 8 + [IN_VMEM] * 2,
        scratch_shapes=[
            buffer(tokens, depth),
            buffer(tokens, width),
            buffer(tokens, depth),
            buffer(tokens, width),
            buffer(tokens, depth),
            wide_buffer(tokens, HEAD_DIM),
            wide_buffer(tokens, HEAD_DIM),
            buffer(3, tokens, width),
            buffer(2, TILE, TILE),
            buffer(tokens, depth),
            buffer(*w_qkv.shape),
            wide_buffer(RING, SLICE, depth),
            wide_buffer(32, depth),
            dma((2, tokens // BLOCK)),
            dma((2, 4)),
            dma((5,)),
            dma((2,)),
            dma((RING, 2)),
            dma((RING, 2)),
            dma((3, 2)),
            dma((2, 2)),
        ]
        + line_scratch((tokens, depth))
        + line_scratch((tokens, depth))
        + scatter_scratch,
        compiler_params=kernel_params(2, 63),
        cost_estimate=COST,
    )(
        prefix_len, projected, d_bin, b_out[None], b_down[None], gain1[None], gain2[None], mlp_partial, normed1,
        context, w_qkv, w_out, inputs, attn_sum, d_output, summed2,
    )
    _, output, d_inputs, _, d_wqkv, d_wout, sum_wqkv, sum_wout, early, late = out
    if not spread:
        early, late = lax.psum((early, late), ("dp", "col"))
        sum_wqkv, sum_wout = scatter_low(d_wqkv, 1), scatter_low(d_wout, 1)
    return output, d_inputs, sum_wqkv, sum_wout, early, late


def scatter_low(grad, dim):
    summed = lax.psum_scatter(grad, ("dp", "col"), scatter_dimension=dim, tiled=True)
    return summed.astype(jnp.float32)


def local(
    inputs,
    prefix_len,
    norm1_gain,
    norm1_shift,
    w_qkv,
    b_qv,
    w_out,
    b_out,
    norm2_gain,
    norm2_shift,
    w_in,
    b_in,
    w_down,
    b_down,
    d_output,
):
    low_mats = (
        w_qkv.astype(jnp.bfloat16),
        w_out.astype(jnp.bfloat16),
        w_in.astype(jnp.bfloat16),
        w_down.astype(jnp.bfloat16),
    )
    full_in, full_down = low_mats[2:]
    source = inputs.astype(jnp.float32)
    if (lax.axis_size("dp"), lax.axis_size("col")) == (2, 4):
        normed1_low, projected, context_low, full_qkv, full_out = head(
            prefix_len, inputs, norm1_gain, norm1_shift, b_qv, low_mats[0], low_mats[1]
        )
    else:
        full_qkv = lax.all_gather(low_mats[0], ("dp", "col"), axis=1, tiled=True)
        full_out = lax.all_gather(low_mats[1], ("dp", "col"), axis=1, tiled=True)
        full_in = lax.all_gather(full_in, ("dp", "col"), axis=0, tiled=True)
        full_down = lax.all_gather(full_down, ("dp", "col"), axis=1, tiled=True)
        normed1, _, _ = norm_forward(source, norm1_gain, norm1_shift)
        normed1_low = normed1.astype(jnp.bfloat16)
        projected = jnp.einsum(
            "td,cdn->ctn", normed1_low, full_qkv, preferred_element_type=jnp.float32
        )
        bias_rows = jnp.stack([b_qv[0], jnp.zeros_like(b_qv[0]), b_qv[1]])
        projected = (projected + bias_rows[:, None, :]).astype(jnp.bfloat16)
        context_low = attend(prefix_len, projected)
    attn_sum, summed2, mlp_partial, grad_wdown, grad_win, grad_bin = mlp_sums(
        context_low, full_out, b_out, norm2_gain, norm2_shift, b_in,
        inputs, full_in, full_down, d_output,
    )
    sent_win = scatter_low(grad_win, 0)
    sent_wdown = scatter_low(grad_wdown, 1)
    output, d_inputs, sent_wqkv, sent_wout, early, late = backward(
        prefix_len, projected, grad_bin, b_out, b_down, norm1_gain, norm2_gain, mlp_partial, normed1_low,
        context_low, full_qkv, full_out, inputs, attn_sum, d_output, summed2,
    )
    width = b_qv.shape[1]
    return (
        output,
        d_inputs,
        late[0],
        late[1],
        sent_wqkv,
        early[5, : 2 * width].reshape(2, width),
        sent_wout,
        early[0],
        early[1],
        early[2],
        sent_win,
        early[4],
        sent_wdown,
        early[3],
    )


def solution(mesh):
    return jax.shard_map(
        local,
        mesh=mesh,
        in_specs=(
            P(("dp", "col"), None),
            P(("dp", "col")),
            P(),
            P(),
            P(None, ("dp", "col"), "row"),
            P(None, "row"),
            P("row", ("dp", "col")),
            P(),
            P(),
            P(),
            P(("dp", "col"), "row"),
            P("row"),
            P("row", ("dp", "col")),
            P(),
            P(("dp", "col"), None),
        ),
        out_specs=(
            P(("dp", "col"), None),
            P(("dp", "col"), None),
            P(),
            P(),
            P(None, ("dp", "col"), "row"),
            P(None, "row"),
            P("row", ("dp", "col")),
            P(),
            P(),
            P(),
            P(("dp", "col"), "row"),
            P("row"),
            P("row", ("dp", "col")),
            P(),
        ),
        check_vma=False,
    )
```

```python
from functools import partial

import jax
import jax.numpy as jnp
from jax import lax
from jax.experimental import pallas as pl
from jax.experimental.pallas import tpu as pltpu
from jax.sharding import PartitionSpec as P

HEAD_DIM = 128
MESH_IDS = pl.DeviceIdType.MESH
CHUNK = 32
LAG = 2


eps_norm = 1e-05


def norm_forward(values, norm_gain, norm_shift):
    average = jnp.mean(values, axis=-1, keepdims=True)
    centered = values - average
    variance = jnp.mean(centered * centered, axis=-1, keepdims=True)
    inverse = lax.rsqrt(variance + eps_norm)
    scaled = centered * inverse
    return (scaled * norm_gain + norm_shift, scaled, inverse)


def norm_backward(grad, scaled, inverse, norm_gain):
    grad_scaled = grad * norm_gain
    return inverse * (
        grad_scaled
        - jnp.mean(grad_scaled, axis=-1, keepdims=True)
        - scaled * jnp.mean(grad_scaled * scaled, axis=-1, keepdims=True)
    )


def dot(left, right, left_dim, right_dim):
    return lax.dot_general(
        left, right, (((left_dim,), (right_dim,)), ((), ())), preferred_element_type=jnp.float32
    )


def greet_row(n, others=()):
    r = lax.axis_index("row")
    last = n - 1
    bar = pltpu.get_barrier_semaphore()
    for cond, dev in ((r > 0, r - 1), (r < last, r + 1)):

        @pl.when(cond)
        def _():
            pl.semaphore_signal(bar, inc=1, device_id={"row": dev}, device_id_type=MESH_IDS)

    for other in others:
        pl.semaphore_signal(bar, inc=1, device_id=other, device_id_type=MESH_IDS)
    inside = (r > 0) & (r < last)

    @pl.when(inside)
    def _():
        pl.semaphore_wait(bar, 2 + len(others))

    @pl.when(jnp.logical_not(inside))
    def _():
        pl.semaphore_wait(bar, 1 + len(others))


def plane_partners():
    y, x = lax.axis_index("dp"), lax.axis_index("col")
    far_x, near = lax.rem(x + 2, 4), x + 1 - 2 * lax.rem(x, 2)
    far_near = lax.rem(near + 2, 4)
    ids = {"x": {"col": far_x}, "y": {"dp": 1 - y}, "near": {"col": near}}
    mine = {"own": y * 4 + x, "x": y * 4 + far_x, "y": (1 - y) * 4 + x, "xy": (1 - y) * 4 + far_x}
    theirs = {
        "own": y * 4 + near,
        "x": y * 4 + far_near,
        "y": (1 - y) * 4 + near,
        "xy": (1 - y) * 4 + far_near,
    }
    return ids, mine, theirs


KINDS = ("own", "x", "y", "xy")


def plane_gather(pieces, send_sem, recv_sem, near_send, near_recv, local_sem):
    ids, mine, theirs = plane_partners()
    count = len(pieces)

    def remote(kind, k, to, src, dst):
        row = KINDS.index(kind)
        near = to == "near"
        return pltpu.make_async_remote_copy(
            src_ref=src,
            dst_ref=dst,
            send_sem=(near_send if near else send_sem).at[row, k],
            recv_sem=(near_recv if near else recv_sem).at[row, k],
            device_id=ids[to],
            device_id_type=MESH_IDS,
        )

    def outgoing(k):
        own, place = pieces[k](mine["own"])
        return [remote("x", k, "x", own, place), remote("y", k, "y", own, place)]

    def local(k):
        own, place = pieces[k](mine["own"])
        return pltpu.make_async_copy(own, place, local_sem.at[k])

    def onward(k):
        kind, to = ("x", "y") if k % 2 == 0 else ("y", "x")
        place = pieces[k](mine[kind])[1]
        return remote("xy", k, to, place, place)

    def share(kind, k):
        own, place = pieces[k](mine[kind])
        return remote(kind, k, "near", own if kind == "own" else place, place)

    def start():
        for k in range(count):
            for copy in outgoing(k):
                copy.start()
        for k in range(count):
            share("own", k).start()
            local(k).start()

    def arrive(k):
        for copy in outgoing(k):
            copy.wait_recv()
        onward(k).start()
        share("x", k).start()
        share("y", k).start()

    def arrive_far(k):
        onward(k).wait_recv()
        share("xy", k).start()

    def finish():
        for k in range(count):
            local(k).wait()
            for copy in outgoing(k):
                copy.wait_send()
            onward(k).wait_send()
            for kind in KINDS:
                place = pieces[k](theirs[kind])[1]
                share(kind, k).wait_send()
                remote(kind, k, "near", place, place).wait_recv()

    return list(ids.values()), start, arrive, arrive_far, finish


def line_sum(n, p_ref, o_ref, held, rs_s, rs_r, ag_s, ag_r, loc):
    half = o_ref.shape[0] // 2
    chunks = held.shape[0] // 2 // CHUNK
    r = lax.axis_index("row")
    last = n - 1
    place = (r, last - r)
    after = (jnp.minimum(r + 1, last), jnp.maximum(r - 1, 0))
    before = (jnp.maximum(r - 1, 0), jnp.minimum(r + 1, last))

    def rows(d, c):
        return pl.ds(pl.multiple_of((half if d == 0 else 0) + c * CHUNK, CHUNK), CHUNK)

    def slot(d, c):
        return pl.ds(pl.multiple_of((1 - d) * chunks * CHUNK + c * CHUNK, CHUNK), CHUNK)


    def onward(d, c, src):
        return pltpu.make_async_remote_copy(
            src_ref=src.at[rows(d, c) if src is p_ref else slot(d, c)],
            dst_ref=held.at[slot(d, c)],
            send_sem=rs_s.at[d, c],
            recv_sem=rs_r.at[d, c],
            device_id={"row": after[d]},
            device_id_type=MESH_IDS,
        )

    def back(d, c, src):
        return pltpu.make_async_remote_copy(
            src_ref=src.at[slot(d, c) if src is held else rows(d, c)],
            dst_ref=o_ref.at[rows(d, c)],
            send_sem=ag_s.at[d, c],
            recv_sem=ag_r.at[d, c],
            device_id={"row": before[d]},
            device_id_type=MESH_IDS,
        )

    def keep(d, c):
        return pltpu.make_async_copy(held.at[slot(d, c)], o_ref.at[rows(d, c)], loc.at[c])

    def step(t):
        for d in (0, 1):

            @pl.when((place[d] == 0) & (t >= 0) & (t < chunks))
            def _():
                onward(d, t, p_ref).start()

            c = t - LAG * place[d]

            @pl.when((place[d] > 0) & (c >= 0) & (c < chunks))
            def _():
                onward(d, c, p_ref).wait_recv()
                here = slot(d, c)
                held[here] = (
                    held[here].astype(jnp.float32) + p_ref[rows(d, c)].astype(jnp.float32)
                ).astype(jnp.bfloat16)

                @pl.when(place[d] < last)
                def _():
                    onward(d, c, held).start()

                @pl.when(place[d] == last)
                def _():
                    back(d, c, held).start()
                    keep(d, c).start()

        for d in (0, 1):
            c = t - LAG * (2 * last - place[d])

            @pl.when((place[d] < last) & (c >= 0) & (c < chunks))
            def _():
                back(d, c, o_ref).wait_recv()

                @pl.when(place[d] > 0)
                def _():
                    back(d, c, o_ref).start()

    def settle(c):
        for d in (0, 1):

            @pl.when(place[d] < last)
            def _():
                onward(d, c, p_ref).wait_send()

            @pl.when(place[d] == last)
            def _():
                keep(d, c).wait()

    def finish(c):
        for d in (0, 1):

            @pl.when(place[d] > 0)
            def _():
                back(d, c, o_ref).wait_send()

    def drain():
        def both(c):
            settle(c)
            finish(c)

        loop(0, chunks, both)

    return step, drain, settle, lambda: loop(0, chunks, finish)


def line_steps(n, total_rows):
    return total_rows // 2 // CHUNK + LAG * 2 * (n - 1)


def line_scratch(shape):
    chunks = shape[0] // 2 // CHUNK
    dma = pltpu.SemaphoreType.DMA
    return [
        pltpu.VMEM(shape, jnp.bfloat16),
        dma((2, chunks)),
        dma((2, chunks)),
        dma((2, chunks)),
        dma((2, chunks)),
        dma((chunks,)),
    ]


def loop(start, stop, body):
    def one(t, carry):
        body(t)
        return carry

    lax.fori_loop(start, stop, one, 0)


COST = pl.CostEstimate(flops=1000, bytes_accessed=1000, transcendentals=0)
IN_VMEM = pl.BlockSpec(memory_space=pltpu.VMEM)
IN_HBM = pl.BlockSpec(memory_space=pl.ANY)


def low_shape(*shape):
    return jax.ShapeDtypeStruct(shape, jnp.bfloat16)


def kernel_params(collective_id, mib):
    return pltpu.CompilerParams(
        collective_id=collective_id, has_side_effects=True, vmem_limit_bytes=mib * 2**20
    )


TILE = 512
FEW = 16
BLOCK = 256


def mlp_sums_kernel(
    n, spread, ctx, w_out, b_out, gain, shift, b_in, src_hbm, w_in_hbm, w_down_hbm, g_hbm,
    branch, d_normed, mlp, d_wdown, d_win, d_bin,
    p, w_in, w_down, g, normed, act, d_pre, mlp_acc, d_acc, rows_a, rows_b, stage, w_stage,
    load_sem, block_sem, mlp_sem, store_sem, *more,
):
    tokens, depth = p.shape
    units = act.shape[1]
    half = tokens // 2
    part = BLOCK // 2
    blocks = tokens // BLOCK
    per_block = part // CHUNK
    quarters = units // TILE

    def sides(j):
        low_rows = pl.ds(pl.multiple_of(j * part, part), part)
        high_rows = pl.ds(pl.multiple_of(half + j * part, part), part)
        return low_rows, high_rows

    def own(j, side=None):
        if side is None:
            return pl.ds(pl.multiple_of(j * BLOCK, BLOCK), BLOCK)
        return pl.ds(pl.multiple_of(j * BLOCK + side * part, part), part)

    lines, gather_sems = more[:12], more[12:]
    loads = []
    others = []
    if spread:
        deep, wide = w_in_hbm.shape[0], w_down_hbm.shape[1]

        def in_piece(k, place):
            size = deep // 2
            there = pl.ds(pl.multiple_of(place * deep + k * size, size), size)
            return w_in_hbm.at[pl.ds(k * size, size)], w_in.at[there]

        def down_piece(k, place):
            some = pl.ds(k * (units // 2), units // 2)
            cols = pl.ds(pl.multiple_of(place * wide, wide), wide)
            return w_down_hbm.at[some], w_down.at[some, cols]

        pieces = [partial(f, k) for f in (in_piece, down_piece) for k in range(2)]
        others, start_gather, arrive, arrive_far, finish_gather = plane_gather(
            pieces, *gather_sems
        )
    else:
        loads = [
            pltpu.make_async_copy(w_in_hbm, w_in, load_sem.at[0]),
            pltpu.make_async_copy(w_down_hbm, w_down, load_sem.at[1]),
        ]
    for j in range(blocks):
        for side, here in enumerate((j * part, half + j * part)):
            loads.append(
                pltpu.make_async_copy(
                    g_hbm.at[pl.ds(here, part)],
                    g.at[pl.ds(j * BLOCK + side * part, part)],
                    load_sem.at[2 + 2 * j + side],
                )
            )
    for load in loads:
        load.start()
    d_bin[...] = jnp.zeros_like(d_bin)
    greet_row(n, others)
    if spread:
        start_gather()
    step1, _, settle1, finish1 = line_sum(n, p, branch, *lines[:6])
    step2, drain2, _, _ = line_sum(n, p, d_normed, *lines[6:])

    def project(j):
        low_rows, high_rows = sides(j)
        both = jnp.concatenate([ctx[low_rows], ctx[high_rows]], axis=0)
        for c in range(0, depth, TILE):
            cols = slice(c, c + TILE)
            term = dot(both, w_out[:, cols], 1, 0).astype(jnp.bfloat16)
            p[low_rows, cols] = term[:part]
            p[high_rows, cols] = term[part:]
        loop(j * per_block, (j + 1) * per_block, step1)

    for j in range(blocks):
        project(j)
        if spread and j == blocks - 2:
            for k in range(len(pieces)):
                arrive(k)
    if spread:
        for k in range(len(pieces)):
            arrive_far(k)
        finish_gather()
    for load in loads:
        load.wait()

    def norm_block(j):
        loop(j * per_block, (j + 1) * per_block, settle1)
        copies = []
        for i, (src, dst) in enumerate(((branch, rows_a), (src_hbm, rows_b))):
            for side, here in enumerate(sides(j)):
                copies.append(
                    pltpu.make_async_copy(
                        src.at[here], dst.at[pl.ds(side * part, part)], block_sem.at[i, side]
                    )
                )
        for copy in copies:
            copy.start()
        for copy in copies:
            copy.wait()

        def few(k):
            here = pl.ds(pl.multiple_of(k * 64, 64), 64)
            there = pl.ds(pl.multiple_of(j * BLOCK + k * 64, 64), 64)
            source = rows_b[here].astype(jnp.float32)
            hidden = source + rows_a[here].astype(jnp.float32) + b_out[...]
            normed[there] = norm_forward(hidden, gain[...], shift[...])[0].astype(jnp.bfloat16)

        loop(0, BLOCK // 64, few)

    def mlp_out(j):
        return [
            pltpu.make_async_copy(
                stage.at[pl.ds(side * part, part)], mlp.at[here], mlp_sem.at[side]
            )
            for side, here in enumerate(sides(j))
        ]

    first = tokens // 2 // CHUNK

    def block(j):
        for q in range(quarters):
            t = first + j * per_block + q
            step1(t)
            step2(t - first - per_block)
            if q == 0:
                norm_block(j)
            units_q = slice(q * TILE, (q + 1) * TILE)
            here = own(j)
            pre = dot(normed[here], w_in[:, units_q], 1, 0) + b_in[:, units_q]
            d_act = dot(g[here], w_down[units_q], 1, 1)
            lower = 0.5 * (1.0 + lax.erf(pre * 0.5**0.5))
            act[here, units_q] = (pre * lower).astype(jnp.bfloat16)
            slope = lower + pre * (jnp.exp(-0.5 * pre * pre) * (0.5 / jnp.pi) ** 0.5)
            low_pre = (d_act * slope).astype(jnp.bfloat16)
            d_pre[here, units_q] = low_pre
            d_bin[:, units_q] += jnp.sum(low_pre.astype(jnp.float32), axis=0, keepdims=True)
            for c in range(0, depth, TILE):
                cols = slice(c, c + TILE)
                m_term = dot(act[here, units_q], w_down[units_q, cols], 1, 0)
                d_term = dot(d_pre[here, units_q], w_in[cols, units_q], 1, 1)
                if q == 0:
                    mlp_acc[:, cols] = m_term
                    d_acc[:, cols] = d_term
                elif q < quarters - 1:
                    mlp_acc[:, cols] += m_term
                    d_acc[:, cols] += d_term
                else:
                    if c == 0:

                        @pl.when(j > 0)
                        def _():
                            for copy in mlp_out(j - 1):
                                copy.wait()

                    stage[:, cols] = (mlp_acc[:, cols] + m_term).astype(jnp.bfloat16)
                    d_low = (d_acc[:, cols] + d_term).astype(jnp.bfloat16)
                    for side, rows in enumerate(sides(j)):
                        p[rows, cols] = d_low[side * part : (side + 1) * part]
        for copy in mlp_out(j):
            copy.start()

    loop(0, blocks, block)
    begin = first
    steps = line_steps(n, tokens)
    tick = tokens // 2 // CHUNK - per_block
    jobs = ((act, g, d_wdown), (normed, d_pre, d_win))
    for k, (left, right, out) in enumerate(jobs):
        across = out.shape[1] // TILE
        tiles = (out.shape[0] // TILE) * across

        def store(tile, slot):
            m = pl.ds(pl.multiple_of((tile // across) * TILE, TILE), TILE)
            c = pl.ds(pl.multiple_of(lax.rem(tile, across) * TILE, TILE), TILE)
            copy = pltpu.make_async_copy(w_stage.at[slot], out.at[m, c], store_sem.at[slot])
            return m, c, copy

        def body(u):
            step2(tick + k * (tiles // 2) + u)
            for slot in range(2):
                m, c, copy = store(2 * u + slot, slot)
                if k == 0:

                    @pl.when(u > 0)
                    def _():
                        copy.wait()
                else:
                    copy.wait()
                w_stage[slot] = dot(left[:, m], right[:, c], 0, 0).astype(jnp.bfloat16)
                copy.start()

        loop(0, tiles // 2, body)
        tick_end = tick + (k + 1) * (tiles // 2)
    if tick_end < steps:
        loop(tick_end, steps, step2)
    for slot in range(2):
        store(slot, slot)[2].wait()
    for copy in mlp_out(blocks - 1):
        copy.wait()
    finish1()
    drain2()


def mlp_sums(context, w_out, b_out, gain, shift, b_in, inputs, w_in, w_down, d_output):
    tokens, depth = inputs.shape
    units = w_in.shape[1]
    spread = w_in.shape[0] < depth
    dma = pltpu.SemaphoreType.DMA
    low_buffer = lambda *shape: pltpu.VMEM(shape, jnp.bfloat16)
    return pl.pallas_call(
        partial(mlp_sums_kernel, lax.axis_size("row"), spread),
        out_shape=[
            low_shape(tokens, depth),
            low_shape(tokens, depth),
            low_shape(tokens, depth),
            low_shape(units, depth),
            low_shape(depth, units),
            jax.ShapeDtypeStruct((1, units), jnp.float32),
        ],
        in_specs=[IN_VMEM] * 6 + [IN_HBM] * 4,
        out_specs=[IN_HBM] * 5 + [IN_VMEM],
        scratch_shapes=[
            low_buffer(tokens, depth),
            low_buffer(depth, units),
            low_buffer(units, depth),
            low_buffer(tokens, depth),
            low_buffer(tokens, depth),
            low_buffer(tokens, units),
            low_buffer(tokens, units),
            pltpu.VMEM((BLOCK, depth), jnp.float32),
            pltpu.VMEM((BLOCK, depth), jnp.float32),
            low_buffer(BLOCK, depth),
            low_buffer(BLOCK, depth),
            low_buffer(BLOCK, depth),
            low_buffer(2, TILE, TILE),
            dma((2 + 2 * (tokens // BLOCK),)),
            dma((2, 2)),
            dma((2,)),
            dma((2,)),
        ]
        + line_scratch((tokens, depth))
        + line_scratch((tokens, depth))
        + ([dma((4, 4))] * 4 + [dma((4,))] if spread else []),
        compiler_params=kernel_params(1, 61),
        cost_estimate=COST,
    )(
        context, w_out, b_out[None], gain[None], shift[None], b_in[None],
        inputs, w_in, w_down, d_output,
    )


QUERY_ROWS = 256


def head_kernel(
    prefix_ref, src, gain, shift, b_q, b_v, w_qkv_hbm, w_out_hbm,
    normed_out, projected_out, context_out, full_qkv, full_out,
    weights, w_out, normed, projected, context, store_sem, *sems,
):
    tokens, depth = src.shape
    width = projected.shape[2]
    deep, wide = w_qkv_hbm.shape[1], w_out_hbm.shape[1]
    size, tall = deep // 2, width // 2

    def qkv_piece(c, k, place):
        there = pl.ds(pl.multiple_of(place * deep + k * size, size), size)
        return w_qkv_hbm.at[c, pl.ds(k * size, size)], weights.at[c, there]

    def out_piece(k, place):
        some = pl.ds(k * tall, tall)
        cols = pl.ds(pl.multiple_of(place * wide, wide), wide)
        return w_out_hbm.at[some], w_out.at[some, cols]

    parts = [[partial(qkv_piece, c, k) for k in range(2)] for c in range(3)]
    parts.append([partial(out_piece, k) for k in range(2)])
    others = list(plane_partners()[0].values())
    start, arrive, far, finish = zip(
        *[plane_gather(part, *sems[5 * i : 5 * i + 5])[1:] for i, part in enumerate(parts)]
    )
    bar = pltpu.get_barrier_semaphore()
    for other in others:
        pl.semaphore_signal(bar, inc=1, device_id=other, device_id_type=MESH_IDS)
    pl.semaphore_wait(bar, len(others))
    start[0]()
    start[1]()

    def few(r):
        here = pl.ds(pl.multiple_of(r * FEW, FEW), FEW)
        rows = norm_forward(src[here].astype(jnp.float32), gain[...], shift[...])[0]
        normed[here] = rows.astype(jnp.bfloat16)

    loop(0, tokens // FEW // 4, lambda r: [few(4 * r + i) for i in range(4)])
    stores = [
        pltpu.make_async_copy(src, dst, store_sem.at[i])
        for i, (src, dst) in enumerate(
            (
                (normed, normed_out),
                (weights, full_qkv),
                (projected, projected_out),
                (w_out, full_out),
                (context, context_out),
            )
        )
    ]
    stores[0].start()
    for i in range(2):
        for k in range(2):
            arrive[i](k)
    start[2]()
    for c in range(3):
        if c == 2:
            for k in range(2):
                arrive[2](k)
            start[3]()
        for k in range(2):
            far[c](k)
        finish[c]()

        def rows_of(i):
            here = pl.ds(pl.multiple_of(i * BLOCK, BLOCK), BLOCK)
            term = dot(normed[here], weights[c], 1, 0)
            if c != 1:
                term += (b_q if c == 0 else b_v)[...]
            projected[c, here] = term.astype(jnp.bfloat16)

        loop(0, tokens // BLOCK, rows_of)
    stores[1].start()
    stores[2].start()
    for k in range(2):
        arrive[3](k)
    attend_kernel(prefix_ref, projected, context)
    stores[4].start()
    for k in range(2):
        far[3](k)
    finish[3]()
    stores[3].start()
    for store in stores:
        store.wait()


def head(prefix_len, inputs, gain, shift, b_qv, w_qkv, w_out):
    tokens, depth = inputs.shape
    width = w_out.shape[0]
    dma = pltpu.SemaphoreType.DMA
    return pl.pallas_call(
        head_kernel,
        out_shape=[
            low_shape(tokens, depth),
            low_shape(3, tokens, width),
            low_shape(tokens, width),
            low_shape(3, depth, width),
            low_shape(width, depth),
        ],
        in_specs=[pl.BlockSpec(memory_space=pltpu.SMEM)] + [IN_VMEM] * 5 + [IN_HBM] * 2,
        out_specs=[IN_HBM] * 5,
        scratch_shapes=[
            pltpu.VMEM((3, depth, width), jnp.bfloat16),
            pltpu.VMEM((width, depth), jnp.bfloat16),
            pltpu.VMEM((tokens, depth), jnp.bfloat16),
            pltpu.VMEM((3, tokens, width), jnp.bfloat16),
            pltpu.VMEM((tokens, width), jnp.bfloat16),
            dma((5,)),
        ]
        + ([dma((4, 2))] * 4 + [dma((2,))]) * 4,
        compiler_params=kernel_params(3, 62),
        cost_estimate=COST,
    )(prefix_len, inputs, gain[None], shift[None], b_qv[:1], b_qv[1:], w_qkv, w_out)


def block_probs(i, prefix, cols, q, k):
    start = i * QUERY_ROWS
    width = max(start + QUERY_ROWS, q.shape[0] // 2)
    here = slice(start, start + QUERY_ROWS)
    scores = dot(k[:width, cols], q[here, cols], 1, 1) * HEAD_DIM ** (-0.5)
    key = lax.broadcasted_iota(jnp.int32, scores.shape, 0)
    query = lax.broadcasted_iota(jnp.int32, scores.shape, 1) + start
    scores = jnp.where((key <= query) | (key < prefix), scores, -1000000000.0)
    expo = jnp.exp(scores - jnp.max(scores, axis=0, keepdims=True))
    return here, width, expo * (1.0 / jnp.sum(expo, axis=0, keepdims=True))


def attend_kernel(prefix_ref, projected, context):
    q, k, v = (projected.at[c] for c in range(3))
    prefix = prefix_ref[0]

    def head(h):
        cols = pl.ds(pl.multiple_of(h * HEAD_DIM, HEAD_DIM), HEAD_DIM)
        v_t = v[:, cols].T
        for i in range(q.shape[0] // QUERY_ROWS):
            here, width, probs = block_probs(i, prefix, cols, q, k)
            out = dot(v_t[:, :width], probs.astype(jnp.bfloat16), 1, 0)
            context[here, cols] = out.T.astype(jnp.bfloat16)

    loop(0, q.shape[1] // HEAD_DIM, head)


def attend(prefix_len, projected):
    return pl.pallas_call(
        attend_kernel,
        out_shape=low_shape(*projected.shape[1:]),
        in_specs=[pl.BlockSpec(memory_space=pltpu.SMEM), IN_VMEM],
        out_specs=IN_VMEM,
        compiler_params=pltpu.CompilerParams(vmem_limit_bytes=32 * 2**20),
        cost_estimate=COST,
    )(prefix_len, projected)


def attend_piece(i, prefix, cols, q, k, v, k_t, d_context, d_proj, d_key, d_value, first):
    score_scale = HEAD_DIM ** (-0.5)
    here, width, probs = block_probs(i, prefix, cols, q, k)
    q_block, g_block = q[here, cols], d_context[here, cols]
    d_probs = dot(v[:width, cols], g_block, 1, 1)
    inner = jnp.sum(d_probs * probs, axis=0, keepdims=True)
    d_scores = (probs * (d_probs - inner)).astype(jnp.bfloat16)
    d_query = dot(k_t[:, :width], d_scores, 1, 0) * score_scale
    d_proj[0, here, cols] = d_query.T.astype(jnp.bfloat16)
    for total, term in (
        (d_key, dot(d_scores, q_block, 1, 0)),
        (d_value, dot(probs.astype(jnp.bfloat16), g_block, 1, 0)),
    ):
        if first:
            total[...] = term
        else:
            total[:width] += term


def plane_scatter(pieces, sems):
    ids, mine, theirs = plane_partners()
    near_send, near_recv, far_send, far_recv, last_send, last_recv, load_sem = sems
    count = len(pieces)

    def remote(src, dst, send, recv, to):
        return pltpu.make_async_remote_copy(
            src_ref=src,
            dst_ref=dst,
            send_sem=send,
            recv_sem=recv,
            device_id=ids[to],
            device_id_type=MESH_IDS,
        )

    def near(i, k):
        block, to, _, _, _ = pieces[k]
        place = theirs[KINDS[i]]
        return remote(block(place), to(i), near_send.at[i, k], near_recv.at[i, k], "near")

    def load(i, k):
        block, _, own, _, _ = pieces[k]
        return pltpu.make_async_copy(block(mine[KINDS[i]]), own(i), load_sem.at[i, k])

    def far(k):
        _, _, own, to, _ = pieces[k]
        return remote(own(3), to(), far_send.at[k], far_recv.at[k], "x" if k % 2 == 0 else "y")

    def last(i, k):
        _, _, own, _, to = pieces[k]
        return remote(
            own(i), to(i - 1), last_send.at[i - 1, k], last_recv.at[i - 1, k], KINDS[i]
        )

    def add(target, term):
        flat = target.shape[0]

        def some(r):
            here = pl.ds(pl.multiple_of(r * 128, 128), 128)
            target[here] = (
                target[here].astype(jnp.float32) + term[here].astype(jnp.float32)
            ).astype(jnp.bfloat16)

        loop(0, flat // 128, some)

    def start():
        for i in (3, 1, 2, 0):
            for k in range(count):
                near(i, k).start()
                load(i, k).start()

    def pair():
        for i in (3, 1, 2, 0):
            for k in range(count):
                near(i, k).wait_recv()
                load(i, k).wait()
                add(pieces[k][2](i), pieces[k][1](i))
                if i == 3:
                    far(k).start()
                elif i == 1 + k % 2:
                    last(i, k).start()

    def cross():
        for k in range(count):
            far(k).wait_recv()
            i = 2 - k % 2
            add(pieces[k][2](i), pieces[k][3]())
            last(i, k).start()

    def collect(k):
        for i in (1, 2):
            last(i, k).wait_recv()
        return pieces[k][2](0), pieces[k][4](0), pieces[k][4](1)

    def finish():
        for k in range(count):
            for i in range(4):
                near(i, k).wait_send()
            far(k).wait_send()
            for i in (1, 2):
                last(i, k).wait_send()

    return start, pair, cross, collect, finish


def sums_out(kind, vectors, slots, send_sem, recv_sem):
    ids = plane_partners()[0]

    def copy(i):
        return pltpu.make_async_remote_copy(
            src_ref=vectors,
            dst_ref=slots.at[i],
            send_sem=send_sem.at[kind, i],
            recv_sem=recv_sem.at[kind, i],
            device_id=ids[("near", "x", "y")[i]],
            device_id_type=MESH_IDS,
        )

    def begin(i):
        copy(i).start()

    def end(i):
        copy(i).wait()
        vectors[...] += slots[i]

    return begin, end


SLICE = 64
RING = 4


def backward_kernel(
    n, spread, prefix_ref, projected, d_bin, b_out, b_down, gain1, gain2,
    mlp_hbm, n1_hbm, ctx_hbm, w_qkv_hbm, w_out_hbm, src_hbm, attn_hbm, g_hbm, dn2_hbm,
    mlp_sum, output, d_inputs, d_hidden, d_wqkv, d_wout, sum_wqkv, sum_wout, early, late,
    p, d_context, n1, ctx, branch, d_key, d_value, d_proj, w_stage, total, weights, ring, partial_sums,
    p_sem, slice_sem, load_sem, store_sem, ring_in, ring_out, out_in, out_store, *more,
):
    lines, more = more[:12], more[12:]
    tokens, depth = p.shape
    width = projected.shape[2]
    half = tokens // 2
    chunks = half // CHUNK
    blocks = tokens // BLOCK
    part = BLOCK // 2
    per_block = part // CHUNK
    travel = LAG * 2 * (n - 1)
    prefix = prefix_ref[0]

    def sides(j, size):
        return (
            pl.ds(pl.multiple_of(j * size, size), size),
            pl.ds(pl.multiple_of(half + j * size, size), size),
        )

    p_loads = [
        [
            pltpu.make_async_copy(mlp_hbm.at[rows], p.at[rows], p_sem.at[side, j])
            for side, rows in enumerate((pl.ds(j * part, part), pl.ds(half + j * part, part)))
        ]
        for j in range(blocks)
    ]
    for loads in p_loads:
        for load in loads:
            load.start()
    w_out_load = pltpu.make_async_copy(w_out_hbm, total.at[pl.ds(0, width)], load_sem.at[0])
    w_out_load.start()
    loads = [
        pltpu.make_async_copy(src, dst, load_sem.at[1 + i])
        for i, (src, dst) in enumerate(
            ((n1_hbm, n1), (ctx_hbm, ctx), (w_qkv_hbm, weights), (src_hbm, n1))
        )
    ]
    early[...] = jnp.zeros_like(early)
    late[...] = jnp.zeros_like(late)
    early[4:5] = d_bin[...]
    partial_sums[...] = jnp.zeros_like(partial_sums)
    others = []
    if spread:
        slots_e, slots_l, small_s, small_r = more[:4]
        qkv_near, qkv_own, qkv_far, qkv_last, out_near, out_own, out_far, out_last = more[4:12]
        qkv_sum, out_sum, sum_sem = more[12:15]
        others = list(plane_partners()[0].values())
        early_begin, early_end = sums_out(0, early, slots_e, small_s, small_r)
        late_begin, late_end = sums_out(1, late, slots_l, small_s, small_r)
        places = 8
        deep, wide = depth // places, depth // places
        size = deep // 2
        tall = width // 2

        def qkv_piece(c, k):
            def block(place):
                there = pl.ds(pl.multiple_of(place * deep + k * size, size), size)
                return d_wqkv.at[c, there]

            some = pl.ds(k * size, size)
            return (
                block,
                lambda i: qkv_near.at[i, c, some],
                lambda i: qkv_own.at[i, c, some],
                lambda: qkv_far.at[c, some],
                lambda i: qkv_last.at[i, c, some],
            )

        def out_piece(k):
            some = pl.ds(k * tall, tall)

            def block(place):
                cols = pl.ds(pl.multiple_of(place * wide, wide), wide)
                return d_wout.at[some, cols]

            return (
                block,
                lambda i: out_near.at[i, some],
                lambda i: out_own.at[i, some],
                lambda: out_far.at[some],
                lambda i: out_last.at[i, some],
            )

        pieces = [qkv_piece(c, k) for c in range(3) for k in range(2)]
        pieces += [out_piece(k) for k in range(2)]
        start_scatter, pair, cross, collect, finish_scatter = plane_scatter(pieces, more[15:])
        stores = [
            pltpu.make_async_copy(qkv_sum, sum_wqkv, sum_sem.at[0]),
            pltpu.make_async_copy(out_sum, sum_wout, sum_sem.at[1]),
        ]

        def total_of(k):
            own, one, two = collect(k)
            if k < 6:
                target = qkv_sum.at[k // 2, pl.ds((k % 2) * size, size)]
            else:
                target = out_sum.at[pl.ds((k % 2) * tall, tall)]

            def some(r):
                here = pl.ds(pl.multiple_of(r * 128, 128), 128)
                target[here] = (
                    own[here].astype(jnp.float32)
                    + one[here].astype(jnp.float32)
                    + two[here].astype(jnp.float32)
                )

            loop(0, target.shape[0] // 128, some)

    greet_row(n, others)
    step1, _, settle1, finish1 = line_sum(n, p, mlp_sum, *lines[:6])
    step2, _, settle2, finish2 = line_sum(n, p, total, *lines[6:])

    def both_steps(t):
        step1(t)
        step2(t - chunks)

    slices = tokens // SLICE

    def slice_rows(k):
        return pl.ds(pl.multiple_of(k * SLICE, SLICE), SLICE)

    def slice_slot(k, i):
        return pl.ds(pl.multiple_of(half + (lax.rem(k, 2) * 4 + i) * SLICE, SLICE), SLICE)

    def slice_loads(k):
        return [
            pltpu.make_async_copy(
                src.at[slice_rows(k)], total.at[slice_slot(k, i)], slice_sem.at[lax.rem(k, 2), i]
            )
            for i, src in enumerate((dn2_hbm, attn_hbm, src_hbm, g_hbm))
        ]

    def hidden_store(k):
        return pltpu.make_async_copy(
            ring.at[lax.rem(k, RING)], d_hidden.at[slice_rows(k)], ring_out.at[lax.rem(k, RING), 0]
        )

    def norm_slice(k):
        @pl.when(k + 1 < slices)
        def _():
            for load in slice_loads(k + 1):
                load.start()

        for load in slice_loads(k):
            load.wait()

        @pl.when(k >= RING)
        def _():
            hidden_store(k - RING).wait()

        def few(r):
            rows = [
                pl.ds(pl.multiple_of(half + (lax.rem(k, 2) * 4 + i) * SLICE + r * FEW, FEW), FEW)
                for i in range(4)
            ]
            dn, attn, source, g = (total[some].astype(jnp.float32) for some in rows)
            _, scaled, inverse = norm_forward(source + attn + b_out[...], 1.0, 0.0)
            grad = g + norm_backward(dn, scaled, inverse, gain2[...])
            low = grad.astype(jnp.bfloat16)
            branch[pl.ds(pl.multiple_of(k * SLICE + r * FEW, FEW), FEW)] = low
            for i, term in enumerate((low.astype(jnp.float32), dn * scaled, dn, g)):
                partial_sums[8 * i : 8 * i + 8] += term[:8] + term[8:]
            ring[lax.rem(k, RING), pl.ds(pl.multiple_of(r * FEW, FEW), FEW)] = grad

        for r in range(SLICE // FEW):
            few(r)
        hidden_store(k).start()

    for load in slice_loads(0):
        load.start()
    norm_ticks = 4
    for load in p_loads[0]:
        load.wait()

    def norm_tick(t):
        step1(t)
        loop(t * (slices // norm_ticks), (t + 1) * (slices // norm_ticks), norm_slice)

    loop(0, norm_ticks, norm_tick)
    for i in range(4):
        early[i : i + 1] = jnp.sum(partial_sums[8 * i : 8 * i + 8], axis=0, keepdims=True)
    for k in range(slices - RING, slices):
        hidden_store(k).wait()
    for some in p_loads[1:]:
        for load in some:
            load.wait()
    for load in loads[:3]:
        load.start()
    w_out_load.wait()

    def context_rows(i):
        rows = pl.ds(pl.multiple_of(i * BLOCK, BLOCK), BLOCK)
        d_context[rows] = dot(branch[rows], total[:width], 1, 1).astype(jnp.bfloat16)

    loop(0, tokens // BLOCK, context_rows)
    partial_sums[...] = jnp.zeros_like(partial_sums)

    q, k, v = (projected.at[c] for c in range(3))
    q_blocks = tokens // QUERY_ROWS
    heads = width // HEAD_DIM
    head_ticks = q_blocks // 2

    def head(h):
        cols = pl.ds(pl.multiple_of(h * HEAD_DIM, HEAD_DIM), HEAD_DIM)
        k_t = k[:, cols].T
        for j in range(q_blocks):
            if j % 2 == 0:
                step1(norm_ticks + h * head_ticks + j // 2)
            attend_piece(
                q_blocks - 1 - j, prefix, cols, q, k, v, k_t, d_context, d_proj, d_key, d_value,
                j == 0,
            )
        d_proj[1, :, cols] = (d_key[...] * HEAD_DIM ** (-0.5)).astype(jnp.bfloat16)
        d_proj[2, :, cols] = d_value[...].astype(jnp.bfloat16)

    loop(0, heads, head)
    for b, c in ((0, 0), (1, 2)):
        early[5:6, b * width : (b + 1) * width] = jnp.sum(
            d_proj[c].astype(jnp.float32), axis=0, keepdims=True
        )
    for load in loads[:3]:
        load.wait()
    tick = norm_ticks + heads * head_ticks
    tiles = depth // TILE

    def tile_store(c, m):
        some = pl.ds(m * TILE, TILE)
        out = d_wqkv.at[c, some] if c < 3 else d_wout.at[:, some]
        return pltpu.make_async_copy(w_stage.at[m % 2], out, store_sem.at[m % 2])

    for c in range(4):
        step1(tick + c)
        for m in range(tiles):
            some = slice(m * TILE, (m + 1) * TILE)
            if c or m > 1:
                before = (c, m - 2) if m > 1 else (c - 1, tiles + m - 2)
                tile_store(*before).wait()
            if c < 3:
                term = dot(n1[:, some], d_proj[c], 0, 0)
            else:
                term = dot(ctx[...], branch[:, some], 0, 0)
            w_stage[m % 2] = term.astype(jnp.bfloat16)
            tile_store(c, m).start()
    for m in (tiles - 2, tiles - 1):
        tile_store(3, m).wait()
    loads[3].start()
    if tick + 4 < chunks:
        loop(tick + 4, chunks, step1)
    if spread:
        start_scatter()

    def gradient(j):
        loop(j * per_block, (j + 1) * per_block, settle1)
        low_rows, high_rows = sides(j, part)
        rows = [
            jnp.concatenate([d_proj[c, low_rows], d_proj[c, high_rows]], axis=0) for c in range(3)
        ]
        for i in range(0, depth, TILE):
            cols = slice(i, i + TILE)
            term = dot(rows[0], weights[0, cols], 1, 1)
            for c in (1, 2):
                term += dot(rows[c], weights[c, cols], 1, 1)
            term = term.astype(jnp.bfloat16)
            p[low_rows, cols] = term[:part]
            p[high_rows, cols] = term[part:]

    def hidden_loads(c):
        return [
            pltpu.make_async_copy(
                d_hidden.at[rows],
                ring.at[lax.rem(c, RING), pl.ds(side * CHUNK, CHUNK)],
                ring_in.at[lax.rem(c, RING), side],
            )
            for side, rows in enumerate(sides(c, CHUNK))
        ]

    def input_stores(c):
        return [
            pltpu.make_async_copy(
                ring.at[lax.rem(c, RING), pl.ds(side * CHUNK, CHUNK)],
                d_inputs.at[rows],
                ring_out.at[lax.rem(c, RING), side],
            )
            for side, rows in enumerate(sides(c, CHUNK))
        ]

    def norm_rows(c):
        settle2(c)
        for load in hidden_loads(c):
            load.wait()
        for side, rows in enumerate(sides(c, CHUNK)):
            for r in range(CHUNK // FEW):
                some = pl.ds(pl.multiple_of(rows.start + r * FEW, FEW), FEW)
                _, scaled, inverse = norm_forward(n1[some].astype(jnp.float32), 1.0, 0.0)
                grad = total[some].astype(jnp.float32)
                for i, term in enumerate((grad * scaled, grad)):
                    partial_sums[8 * i : 8 * i + 8] += term[:8] + term[8:]
                here = pl.ds(side * CHUNK + r * FEW, FEW)
                ring[lax.rem(c, RING), here] += norm_backward(grad, scaled, inverse, gain1[...])
        for store in input_stores(c):
            store.start()

        @pl.when(c >= 2)
        def _():
            for store in input_stores(c - 2):
                store.wait()

        @pl.when(c + 2 < chunks)
        def _():
            for load in hidden_loads(c + 2):
                load.start()

    def out_slot(c, i, side):
        begin = (lax.rem(c, 2) * 4 + i) * 2 * CHUNK + side * CHUNK
        return pl.ds(pl.multiple_of(begin, CHUNK), CHUNK)

    def out_loads(c):
        return [
            pltpu.make_async_copy(
                src.at[rows], branch.at[out_slot(c, i, side)], out_in.at[i, side]
            )
            for i, src in enumerate((src_hbm, attn_hbm, mlp_sum))
            for side, rows in enumerate(sides(c, CHUNK))
        ]

    def out_stores(c):
        return [
            pltpu.make_async_copy(
                branch.at[out_slot(c, 3, side)], output.at[rows], out_store.at[lax.rem(c, 2), side]
            )
            for side, rows in enumerate(sides(c, CHUNK))
        ]

    def output_rows(c):
        for load in out_loads(c):
            load.wait()

        @pl.when(c >= 2)
        def _():
            for store in out_stores(c - 2):
                store.wait()

        for side in range(2):
            source, attn, mlp = (
                branch[out_slot(c, i, side)].astype(jnp.float32) for i in range(3)
            )
            whole = source + attn + b_out[...] + mlp + b_down[...]
            branch[out_slot(c, 3, side)] = whole.astype(jnp.bfloat16)
        for store in out_stores(c):
            store.start()

    arrival = chunks + travel

    def tick_of(t):
        both_steps(t)

        @pl.when(t >= arrival)
        def _():
            norm_rows(t - arrival)

    for j in range(blocks):
        gradient(j)
        if j == blocks - 1:
            for c in range(2):
                for load in hidden_loads(c):
                    load.start()
            loads[3].wait()
        begin = chunks + j * per_block

        def with_output(t):
            for load in out_loads(t - chunks):
                load.start()
            (tick_of if j == blocks - 1 else both_steps)(t)
            output_rows(t - chunks)

        if spread and j == 0:
            loop(begin, begin + 2, with_output)
            pair()
            begin = begin + 2
        loop(begin, chunks + (j + 1) * per_block, with_output)
        if spread:
            if j > 0:
                early_end(j - 1)
            if j < blocks - 1:
                early_begin(j)
    begin = chunks + blocks * per_block
    middle = begin + 2 * per_block + 2
    loop(begin, begin + per_block, tick_of)
    if spread:
        cross()
    loop(begin + per_block, middle, tick_of)
    if spread:
        for k in range(len(pieces)):
            total_of(k)
        for store in stores:
            store.start()
    loop(middle, arrival + chunks, tick_of)
    for i in range(2):
        late[i : i + 1] = jnp.sum(partial_sums[8 * i : 8 * i + 8], axis=0, keepdims=True)
    if spread:
        for i in range(3):
            late_begin(i)
            late_end(i)
    for c in (chunks - 2, chunks - 1):
        for store in input_stores(c) + out_stores(c):
            store.wait()
    if spread:
        finish_scatter()
        for store in stores:
            store.wait()
    finish1()
    finish2()


def backward(
    prefix_len, projected, d_bin, b_out, b_down, gain1, gain2, mlp_partial, normed1, context, w_qkv, w_out,
    inputs, attn_sum, d_output, summed2,
):
    tokens, depth = inputs.shape
    width = w_out.shape[0]
    spread = (lax.axis_size("dp"), lax.axis_size("col")) == (2, 4)
    dma = pltpu.SemaphoreType.DMA
    buffer = lambda *shape: pltpu.VMEM(shape, jnp.bfloat16)
    wide_buffer = lambda *shape: pltpu.VMEM(shape, jnp.float32)
    single = lambda *shape: jax.ShapeDtypeStruct(shape, jnp.float32)
    sums, scatter_scratch = [single(8, 128), single(8, 128)], []
    if spread:
        block, side = (3, depth // 8, width), (width, depth // 8)
        sums = [single(*block), single(*side)]
        scatter_scratch = [wide_buffer(3, 8, depth), wide_buffer(3, 8, depth)]
        scatter_scratch += [dma((2, 3)), dma((2, 3))]
        for shape in (block, side):
            scatter_scratch += [
                buffer(4, *shape), buffer(4, *shape), buffer(*shape), buffer(2, *shape)
            ]
        scatter_scratch += [wide_buffer(*block), wide_buffer(*side)]
        scatter_scratch += [dma((2,)), dma((4, 8)), dma((4, 8)), dma((8,)), dma((8,))]
        scatter_scratch += [dma((2, 8)), dma((2, 8)), dma((4, 8))]
    out = pl.pallas_call(
        partial(backward_kernel, lax.axis_size("row"), spread),
        out_shape=[
            low_shape(tokens, depth),
            low_shape(tokens, depth),
            single(tokens, depth),
            single(tokens, depth),
            low_shape(3, depth, width),
            low_shape(width, depth),
            *sums,
            single(8, depth),
            single(8, depth),
        ],
        in_specs=[pl.BlockSpec(memory_space=pltpu.SMEM)] + [IN_VMEM] * 6 + [IN_HBM] * 9,
        out_specs=[IN_HBM] * 8 + [IN_VMEM] * 2,
        scratch_shapes=[
            buffer(tokens, depth),
            buffer(tokens, width),
            buffer(tokens, depth),
            buffer(tokens, width),
            buffer(tokens, depth),
            wide_buffer(tokens, HEAD_DIM),
            wide_buffer(tokens, HEAD_DIM),
            buffer(3, tokens, width),
            buffer(2, TILE, TILE),
            buffer(tokens, depth),
            buffer(*w_qkv.shape),
            wide_buffer(RING, SLICE, depth),
            wide_buffer(32, depth),
            dma((2, tokens // BLOCK)),
            dma((2, 4)),
            dma((5,)),
            dma((2,)),
            dma((RING, 2)),
            dma((RING, 2)),
            dma((3, 2)),
            dma((2, 2)),
        ]
        + line_scratch((tokens, depth))
        + line_scratch((tokens, depth))
        + scatter_scratch,
        compiler_params=kernel_params(2, 63),
        cost_estimate=COST,
    )(
        prefix_len, projected, d_bin, b_out[None], b_down[None], gain1[None], gain2[None], mlp_partial, normed1,
        context, w_qkv, w_out, inputs, attn_sum, d_output, summed2,
    )
    _, output, d_inputs, _, d_wqkv, d_wout, sum_wqkv, sum_wout, early, late = out
    if not spread:
        early, late = lax.psum((early, late), ("dp", "col"))
        sum_wqkv, sum_wout = scatter_low(d_wqkv, 1), scatter_low(d_wout, 1)
    return output, d_inputs, sum_wqkv, sum_wout, early, late


def scatter_low(grad, dim):
    summed = lax.psum_scatter(grad, ("dp", "col"), scatter_dimension=dim, tiled=True)
    return summed.astype(jnp.float32)


def local(
    inputs,
    prefix_len,
    norm1_gain,
    norm1_shift,
    w_qkv,
    b_qv,
    w_out,
    b_out,
    norm2_gain,
    norm2_shift,
    w_in,
    b_in,
    w_down,
    b_down,
    d_output,
):
    low_mats = (
        w_qkv.astype(jnp.bfloat16),
        w_out.astype(jnp.bfloat16),
        w_in.astype(jnp.bfloat16),
        w_down.astype(jnp.bfloat16),
    )
    full_in, full_down = low_mats[2:]
    source = inputs.astype(jnp.float32)
    if (lax.axis_size("dp"), lax.axis_size("col")) == (2, 4):
        normed1_low, projected, context_low, full_qkv, full_out = head(
            prefix_len, inputs, norm1_gain, norm1_shift, b_qv, low_mats[0], low_mats[1]
        )
    else:
        full_qkv = lax.all_gather(low_mats[0], ("dp", "col"), axis=1, tiled=True)
        full_out = lax.all_gather(low_mats[1], ("dp", "col"), axis=1, tiled=True)
        full_in = lax.all_gather(full_in, ("dp", "col"), axis=0, tiled=True)
        full_down = lax.all_gather(full_down, ("dp", "col"), axis=1, tiled=True)
        normed1, _, _ = norm_forward(source, norm1_gain, norm1_shift)
        normed1_low = normed1.astype(jnp.bfloat16)
        projected = jnp.einsum(
            "td,cdn->ctn", normed1_low, full_qkv, preferred_element_type=jnp.float32
        )
        bias_rows = jnp.stack([b_qv[0], jnp.zeros_like(b_qv[0]), b_qv[1]])
        projected = (projected + bias_rows[:, None, :]).astype(jnp.bfloat16)
        context_low = attend(prefix_len, projected)
    attn_sum, summed2, mlp_partial, grad_wdown, grad_win, grad_bin = mlp_sums(
        context_low, full_out, b_out, norm2_gain, norm2_shift, b_in,
        inputs, full_in, full_down, d_output,
    )
    sent_win = scatter_low(grad_win, 0)
    sent_wdown = scatter_low(grad_wdown, 1)
    output, d_inputs, sent_wqkv, sent_wout, early, late = backward(
        prefix_len, projected, grad_bin, b_out, b_down, norm1_gain, norm2_gain, mlp_partial, normed1_low,
        context_low, full_qkv, full_out, inputs, attn_sum, d_output, summed2,
    )
    width = b_qv.shape[1]
    return (
        output,
        d_inputs,
        late[0],
        late[1],
        sent_wqkv,
        early[5, : 2 * width].reshape(2, width),
        sent_wout,
        early[0],
        early[1],
        early[2],
        sent_win,
        early[4],
        sent_wdown,
        early[3],
    )


def solution(mesh):
    return jax.shard_map(
        local,
        mesh=mesh,
        in_specs=(
            P(("dp", "col"), None),
            P(("dp", "col")),
            P(),
            P(),
            P(None, ("dp", "col"), "row"),
            P(None, "row"),
            P("row", ("dp", "col")),
            P(),
            P(),
            P(),
            P(("dp", "col"), "row"),
            P("row"),
            P("row", ("dp", "col")),
            P(),
            P(("dp", "col"), None),
        ),
        out_specs=(
            P(("dp", "col"), None),
            P(("dp", "col"), None),
            P(),
            P(),
            P(None, ("dp", "col"), "row"),
            P(None, "row"),
            P("row", ("dp", "col")),
            P(),
            P(),
            P(),
            P(("dp", "col"), "row"),
            P("row"),
            P("row", ("dp", "col")),
            P(),
        ),
        check_vma=False,
    )
```
